32 devices in a mesh: fsdp: 8 (over z, x), rep: 4 (over y, core).
Axes of the slice: x: 2, y: 2, z: 4, core: 2. Of those that a mesh axis runs over, the one named last changes fastest.
Arguments:
- tokens: bfloat16 [16384, 768], P(('fsdp', 'rep')), may hold values from -6 to 6
- bucket_item_counts: int32 [32, 4], P(('fsdp', 'rep')), may hold values from 0 to 8, as said below
- slot_item_lengths: int32 [32, 8], P(('fsdp', 'rep')), may hold values from 1 to 512, as said below
- frozen: bfloat16 [7099392], P(('fsdp', 'rep')), as said below
- query_lowrank_matrix: float32 [8, 768], replicated, may hold values from -1.2 to 1.2
- value_lowrank_matrix: float32 [8, 768], replicated, may hold values from -1.2 to 1.2
- output_gradient: bfloat16 [16384, 768], P(('fsdp', 'rep')), may hold values from -12 to 12
- evaluation_tokens: bfloat16 [65536, 768], P(('fsdp', 'rep')), may hold values from -6 to 6
- evaluation_lengths: int32 [128], P(('fsdp', 'rep')), may hold values from 128 to 512
Outputs:
- layer_training_output: bfloat16 [16384, 768], P(('fsdp', 'rep'))
- token_gradient: float32 [16384, 768], P(('fsdp', 'rep'))
- query_lowrank_gradient: float32 [8, 768], replicated
- value_lowrank_gradient: float32 [8, 768], replicated
- evaluation_output: bfloat16 [65536, 768], P(('fsdp', 'rep'))
The draws below stay inside these ranges and needn't reach their ends.
Inputs may be any that keep to these rules, and one draw needn't show every extreme that they name: `bucket_item_counts`: each device's counts fill its 512 tokens exactly; items never cross a boundary of 512 rows. `slot_item_lengths`: slot j of a device belongs to its j-th item, whose length lies between half its bucket plus one and its bucket; slots past a device's items hold 1. `frozen`: laid out as the first step says.
All inputs are finite; a program needn't handle non-finite values.
Results may differ from the reference program's by a relative error of at most 0.015.
The reference program's roundings to bfloat16 on the way count: a program that leaves them out, or rounds other values in their place, can miss the bound.
Values may be sent and summed in bfloat16 or wider, within the bound.
No kernel may reach another device: no remote copies, remote signals or barrier semaphores. Data moves between devices by JAX's collectives and lax.ppermute only.
A program may use at most 192 MiB of HBM per device.

```python
from functools import partial
import jax
import jax.numpy as jnp
import numpy as np
from jax import lax

MODEL_WIDTH = 768
HEADS = 12
HEAD_DIM = 64
HIDDEN_UNITS = 3072
ADAPTER_RANK = 8
BUCKET = 512
TOK_DEV = 512
EVAL_DEV = 2048
TOKENS = 16384
EVAL_TOKENS = 65536
PARAMS_DEV = 221856


def bucket_plan(key):
    device_count = TOKENS // TOK_DEV
    block_count = TOK_DEV // BUCKET
    pattern_table = jnp.array(np.array([[1, 0, 0, 0], [0, 2, 0, 0], [0, 1, 2, 0], [0, 1, 1, 2], [0, 0, 4, 0], [0, 0, 2, 4], [0, 0, 0, 8], [0, 1, 0, 4]], dtype=np.int32))
    pick_ids = jax.random.randint(jax.random.fold_in(key, 101), (device_count, block_count), 0, 8)
    pick_ids = pick_ids.at[0, 0].set(0)
    pick_ids = pick_ids.at[device_count - 1].set(6)
    counts = jnp.sum(pattern_table[pick_ids], axis=1).astype(jnp.int32)
    item_total = TOK_DEV * 8 // BUCKET
    raw_draws = jax.random.randint(jax.random.fold_in(key, 102), (device_count, item_total), 0, 1 << 20)
    bounds = jnp.cumsum(counts, axis=1)
    slot_ids = jnp.arange(item_total, dtype=jnp.int32)[None, :]
    bucket_level = jnp.sum((slot_ids[:, :, None] >= bounds[:, None, :3]).astype(jnp.int32), axis=2)
    sizes_table = jnp.array([BUCKET, BUCKET // 2, BUCKET // 4, BUCKET // 8], jnp.int32)
    extent = sizes_table[bucket_level]
    half_size = extent // 2
    lengths = half_size + 1 + raw_draws % (extent - half_size)
    lengths = jnp.where(slot_ids < bounds[:, 3:4], lengths, 1)
    lengths = lengths.at[0, 0].set(BUCKET)
    return (counts, lengths.astype(jnp.int32))


def draw_bucket_item_counts(key, part):
    plan_pair = bucket_plan(key)
    return plan_pair[0]


def draw_slot_item_lengths(key, part):
    plan_pair = bucket_plan(key)
    return plan_pair[1]


def draw_frozen(key, part):
    key = jax.random.fold_in(key, 7)
    device_count = TOKENS // TOK_DEV
    padded = PARAMS_DEV * device_count
    parameter_pieces = [(MODEL_WIDTH * MODEL_WIDTH, MODEL_WIDTH ** (-0.5), 0.0), (MODEL_WIDTH * MODEL_WIDTH, MODEL_WIDTH ** (-0.5), 0.0), (MODEL_WIDTH * MODEL_WIDTH, MODEL_WIDTH ** (-0.5), 0.0), (MODEL_WIDTH * MODEL_WIDTH, 8.0 * MODEL_WIDTH ** (-0.5), 0.0), (MODEL_WIDTH * HIDDEN_UNITS, MODEL_WIDTH ** (-0.5), 0.0), (HIDDEN_UNITS * MODEL_WIDTH, HIDDEN_UNITS ** (-0.5), 0.0), (MODEL_WIDTH, 0.3, 0.0), (MODEL_WIDTH, 0.3, 0.0), (MODEL_WIDTH, 0.3, 0.0), (HIDDEN_UNITS, 0.3, 0.0), (MODEL_WIDTH, 0.3, 0.0), (MODEL_WIDTH, 0.1, 1.0), (MODEL_WIDTH, 0.1, 0.0), (MODEL_WIDTH, 0.1, 1.0), (MODEL_WIDTH, 0.1, 0.0), (MODEL_WIDTH * ADAPTER_RANK, MODEL_WIDTH ** (-0.5), 0.0), (MODEL_WIDTH * ADAPTER_RANK, MODEL_WIDTH ** (-0.5), 0.0)]
    used_count = 0
    scale_parts = []
    shift_parts = []
    for entry_count, piece_scale, piece_shift in parameter_pieces:
        scale_parts.append(np.full((entry_count,), piece_scale, np.float32))
        shift_parts.append(np.full((entry_count,), piece_shift, np.float32))
        used_count = used_count + entry_count
    scale_parts.append(np.ones((padded - used_count,), np.float32))
    shift_parts.append(np.zeros((padded - used_count,), np.float32))
    scale_vec = jnp.array(np.concatenate(scale_parts))
    shift_vec = jnp.array(np.concatenate(shift_parts))
    base_draw = jax.random.truncated_normal(key, -4.0, 4.0, (padded,), jnp.float32)
    return (base_draw * scale_vec + shift_vec).astype(jnp.bfloat16)


def draw_output_gradient(key, part):
    key = jax.random.fold_in(key, 9)
    ramp = jnp.exp(jnp.log(3.0) * jnp.arange(TOKENS, dtype=jnp.float32) / (TOKENS - 1))[:, None]
    base_draw = jax.random.truncated_normal(key, -4.0, 4.0, (TOKENS, MODEL_WIDTH), jnp.float32)
    return (base_draw * ramp).astype(jnp.bfloat16)


def draw_evaluation_lengths(key, part):
    key = jax.random.fold_in(key, 11)
    lengths = jax.random.randint(key, (EVAL_TOKENS // BUCKET,), BUCKET // 4, BUCKET + 1)
    lengths = lengths.at[0].set(BUCKET)
    lengths = lengths.at[EVAL_TOKENS // BUCKET - 1].set(BUCKET // 4)
    return lengths.astype(jnp.int32)


def steps_of(rng, dims, shards, smallest, largest):
    factor_of = 1.0
    for dim, parts in shards:
        heights = jax.random.uniform(jax.random.fold_in(jax.random.fold_in(rng, 6), dim), (parts,), jnp.float32, smallest / len(shards), largest / len(shards))
        factor_of = factor_of * jnp.repeat(jnp.exp(heights), dims[dim] // parts).reshape((-1,) + (1,) * (len(dims) - 1 - dim))
    return factor_of


def scatter_about(stream_key, shape, scale, limit, split=(), kind=jnp.bfloat16):
    loudness = steps_of(stream_key, shape, split, -0.22, 0.18) if split else 1.0
    drawn = jax.random.normal(stream_key, shape, jnp.float32) * scale * loudness
    return jnp.minimum(jnp.maximum(drawn, -limit), limit).astype(kind)


def setup_inputs(seed: int = 0) -> dict:
    streams_of = jax.random.split(jax.random.key(seed), 10)
    return {
        "tokens": scatter_about(streams_of[0], (TOKENS, MODEL_WIDTH), 1.0, 6.0, ((0, 32),)),
        "bucket_item_counts": draw_bucket_item_counts(jax.random.fold_in(streams_of[9], 71), 0),
        "slot_item_lengths": draw_slot_item_lengths(jax.random.fold_in(streams_of[9], 71), 0),
        "frozen": draw_frozen(jax.random.fold_in(streams_of[9], 71), 0),
        "query_lowrank_matrix": scatter_about(streams_of[4], (ADAPTER_RANK, MODEL_WIDTH), 0.2, 1.2, (), jnp.float32),
        "value_lowrank_matrix": scatter_about(streams_of[5], (ADAPTER_RANK, MODEL_WIDTH), 0.2, 1.2, (), jnp.float32),
        "output_gradient": draw_output_gradient(jax.random.fold_in(streams_of[9], 71), 0),
        "evaluation_tokens": scatter_about(streams_of[7], (EVAL_TOKENS, MODEL_WIDTH), 1.0, 6.0, ((0, 32),)),
        "evaluation_lengths": draw_evaluation_lengths(jax.random.fold_in(streams_of[9], 71), 0),
    }


adapter_scale = 2.0

@jax.custom_vjp
def reduced_precision(v):
    return lax.optimization_barrier(v.astype(jnp.bfloat16)).astype(jnp.float32)

@jax.custom_vjp
def low_back(v):
    return v

def low_keep(v):
    return (reduced_precision(v), None)

def low_pass(kept, grad):
    return (grad,)

def back_keep(v):
    return (v, None)

def back_low(kept, grad):
    return (reduced_precision(grad),)
reduced_precision.defvjp(low_keep, low_pass)
low_back.defvjp(back_keep, back_low)

def round_both(value):
    return reduced_precision(low_back(value))

def product_highest_precision(left, right):
    return jnp.dot(left, right, precision=lax.Precision.HIGHEST)

def unpack_parameters(flattened_parameters, hidden_model_width, feedforward_width, adapter_rank_size):
    parameter_pieces = [('w_query', (hidden_model_width, hidden_model_width)), ('w_key', (hidden_model_width, hidden_model_width)), ('w_value', (hidden_model_width, hidden_model_width)), ('w_out', (hidden_model_width, hidden_model_width)), ('w_up', (hidden_model_width, feedforward_width)), ('w_down', (feedforward_width, hidden_model_width)), ('b_query', (hidden_model_width,)), ('b_value', (hidden_model_width,)), ('b_out', (hidden_model_width,)), ('b_up', (feedforward_width,)), ('b_down', (hidden_model_width,)), ('gain_one', (hidden_model_width,)), ('shift_one', (hidden_model_width,)), ('gain_two', (hidden_model_width,)), ('shift_two', (hidden_model_width,)), ('a_query', (hidden_model_width, adapter_rank_size)), ('a_value', (hidden_model_width, adapter_rank_size))]
    parameter_set = {}
    offset_at = 0
    for piece_name, piece_shape in parameter_pieces:
        entry_count = 1
        for extent in piece_shape:
            entry_count = entry_count * extent
        parameter_set[piece_name] = flattened_parameters[offset_at:offset_at + entry_count].reshape(piece_shape)
        offset_at = offset_at + entry_count
    return parameter_set

def token_layout(counts, lengths, row_total, block_rows):
    position = jnp.arange(row_total, dtype=jnp.int32)
    item_indices = jnp.zeros((row_total,), jnp.int32)
    offset = jnp.zeros((row_total,), jnp.int32)
    region_start = jnp.zeros((), jnp.int32)
    before = jnp.zeros((), jnp.int32)
    for bucket_level in range(4):
        extent = block_rows // 2 ** bucket_level
        finish = region_start + counts[bucket_level].astype(jnp.int32) * extent
        inside = (position >= region_start) & (position < finish)
        relative = position - region_start
        item_indices = jnp.where(inside, before + relative // extent, item_indices)
        offset = jnp.where(inside, relative % extent, offset)
        region_start = finish
        before = before + counts[bucket_level].astype(jnp.int32)
    slot_ids = jnp.arange(lengths.shape[0], dtype=jnp.int32)
    length = lax.optimization_barrier(jnp.sum(jnp.where(item_indices[:, None] == slot_ids[None, :], lengths[None, :].astype(jnp.int32), 0), axis=1))
    return (item_indices, offset < length)

def layer_norm(resid, norm_gain, norm_shift):
    centred = resid - lax.optimization_barrier(jnp.mean(resid, axis=-1, keepdims=True))
    spread = lax.optimization_barrier(jnp.mean(centred * centred, axis=-1, keepdims=True))
    return centred * lax.rsqrt(spread + 1e-05) * norm_gain + norm_shift

def attend_block(block_parts):
    query_rows, key_rows, value_rows, item_indices, valid_key_mask = block_parts
    row_count = query_rows.shape[0]
    head_query = query_rows.reshape(row_count, HEADS, HEAD_DIM)
    head_key = key_rows.reshape(row_count, HEADS, HEAD_DIM)
    head_value = value_rows.reshape(row_count, HEADS, HEAD_DIM)
    scores = jnp.einsum('qhd,khd->hqk', head_query, head_key, precision=lax.Precision.HIGHEST) * HEAD_DIM ** (-0.5)
    scores = low_back(scores)
    allowed = (item_indices[:, None] == item_indices[None, :]) & valid_key_mask[None, :]
    scores = jnp.where(allowed[None], scores, -1e+30)
    top_score = lax.optimization_barrier(jnp.max(scores, axis=-1, keepdims=True))
    expo_scores = jnp.exp(scores - top_score)
    soft_probs = reduced_precision(expo_scores / lax.optimization_barrier(jnp.sum(expo_scores, axis=-1, keepdims=True)))
    context = jnp.einsum('hqk,khd->qhd', soft_probs, head_value, precision=lax.Precision.HIGHEST)
    return context.reshape(row_count, HEADS * HEAD_DIM)

def encoder_layer_forward(input_arrays, parameter_set, adapter_pair, item_indices, valid_key_mask):
    query_complete = product_highest_precision(input_arrays, parameter_set['w_query']) + parameter_set['b_query']
    value_complete = product_highest_precision(input_arrays, parameter_set['w_value']) + parameter_set['b_value']
    if adapter_pair is not None:
        query_adapter_out = round_both(product_highest_precision(input_arrays, parameter_set['a_query']))
        value_adapter_out = round_both(product_highest_precision(input_arrays, parameter_set['a_value']))
        query_complete = query_complete + adapter_scale * product_highest_precision(query_adapter_out, adapter_pair[0])
        value_complete = value_complete + adapter_scale * product_highest_precision(value_adapter_out, adapter_pair[1])
    query_complete = round_both(query_complete)
    key_full = round_both(product_highest_precision(input_arrays, parameter_set['w_key']))
    value_complete = round_both(value_complete)
    block_count = input_arrays.shape[0] // BUCKET

    def split_blocks(array_in):
        return array_in.reshape((block_count, BUCKET) + array_in.shape[1:])
    context = lax.map(jax.checkpoint(attend_block), (split_blocks(query_complete), split_blocks(key_full), split_blocks(value_complete), split_blocks(item_indices), split_blocks(valid_key_mask)))
    context = round_both(context.reshape(input_arrays.shape[0], HEADS * HEAD_DIM))
    attn_out = low_back(product_highest_precision(context, parameter_set['w_out']) + parameter_set['b_out'])
    hidden_one = round_both(layer_norm(input_arrays + attn_out, parameter_set['gain_one'], parameter_set['shift_one']))
    up_rows = low_back(product_highest_precision(hidden_one, parameter_set['w_up']) + parameter_set['b_up'])
    gelu_rows = reduced_precision(jax.nn.gelu(up_rows, approximate=False))
    down_rows = low_back(product_highest_precision(gelu_rows, parameter_set['w_down']) + parameter_set['b_down'])
    return layer_norm(hidden_one + down_rows, parameter_set['gain_two'], parameter_set['shift_two'])

def reference(tokens, bucket_item_counts, slot_item_lengths, frozen, query_lowrank_matrix, value_lowrank_matrix, output_gradient, evaluation_tokens, evaluation_lengths):
    parameter_set = unpack_parameters(frozen.astype(jnp.float32), MODEL_WIDTH, HIDDEN_UNITS, ADAPTER_RANK)
    item_indices, valid_key_mask = jax.vmap(partial(token_layout, row_total=TOK_DEV, block_rows=BUCKET))(bucket_item_counts, slot_item_lengths)
    item_indices = item_indices.reshape(-1)
    valid_key_mask = valid_key_mask.reshape(-1)
    input_arrays = tokens.astype(jnp.float32)

    def training_step(layer_input, query_lowrank_term, value_lowrank_term):
        return encoder_layer_forward(layer_input, parameter_set, (reduced_precision(query_lowrank_term), reduced_precision(value_lowrank_term)), item_indices, valid_key_mask)
    layer_training_output, backward_closure = jax.vjp(training_step, input_arrays, query_lowrank_matrix.astype(jnp.float32), value_lowrank_matrix.astype(jnp.float32))
    token_gradient, query_lowrank_gradient, value_lowrank_gradient = backward_closure(output_gradient.astype(jnp.float32))
    merged_weights = dict(parameter_set)
    merged_weights['w_query'] = reduced_precision(parameter_set['w_query'] + adapter_scale * product_highest_precision(parameter_set['a_query'], reduced_precision(query_lowrank_matrix.astype(jnp.float32))))
    merged_weights['w_value'] = reduced_precision(parameter_set['w_value'] + adapter_scale * product_highest_precision(parameter_set['a_value'], reduced_precision(value_lowrank_matrix.astype(jnp.float32))))
    group_count = evaluation_tokens.shape[0] // EVAL_DEV
    positions = jnp.arange(EVAL_DEV, dtype=jnp.int32)
    eval_items = positions // BUCKET

    def evaluate(group_parts):
        rows_in, lengths_in = group_parts
        valid_rows = positions % BUCKET < jnp.repeat(lengths_in.astype(jnp.int32), BUCKET)
        return encoder_layer_forward(rows_in, merged_weights, None, eval_items, valid_rows)
    evaluation_output = lax.map(evaluate, (evaluation_tokens.astype(jnp.float32).reshape(group_count, EVAL_DEV, MODEL_WIDTH), evaluation_lengths.reshape(group_count, EVAL_DEV // BUCKET)))
    evaluation_output = evaluation_output.reshape(evaluation_tokens.shape[0], MODEL_WIDTH)
    return (layer_training_output.astype(jnp.bfloat16), token_gradient.astype(jnp.float32), query_lowrank_gradient.astype(jnp.float32), value_lowrank_gradient.astype(jnp.float32), evaluation_output.astype(jnp.bfloat16))
```

```python
import functools

import jax
import jax.numpy as jnp
from jax import lax
from jax.experimental import pallas as pl
from jax.experimental.pallas import tpu as pltpu
from jax.sharding import PartitionSpec as P

WIDTH = 768
HEADS = 12
HEAD_DIM = 64
SLABS = 4
BUCKET = 512
CHUNK = 256
PAIR = 2 * HEAD_DIM
PAIRS = HEADS // 2
WEIGHT_ROWS = WIDTH * (4 + 2 * SLABS)
QKV_ROWS = 3 * WIDTH
VECTOR_ROWS = 12
RANK = 8
FORBIDDEN = -1e30
EPS = 1e-5
VMEM = 60 * 2**20

f32 = jnp.float32
bf16 = jnp.bfloat16

BQ, BV, BO, B1, B2, G1, C1, G2, C2 = 0, 1, 2, 3, 7, 8, 9, 10, 11


def dot(left, right):
    return jnp.dot(left, right, preferred_element_type=f32)


def dot_last(left, right):
    return lax.dot_general(left, right, (((1,), (1,)), ((), ())), preferred_element_type=f32)


def dot_first(left, right):
    return lax.dot_general(left, right, (((0,), (0,)), ((), ())), preferred_element_type=f32)


def row(tail_ref, at):
    return tail_ref[...].astype(f32)[at : at + 1]


def normalise(resid):
    centred = resid - jnp.mean(resid, axis=-1, keepdims=True)
    scale = lax.rsqrt(jnp.mean(centred * centred, axis=-1, keepdims=True) + EPS)
    return centred * scale, scale


def normalise_back(grad, normed, scale):
    return scale * (
        grad
        - jnp.mean(grad, axis=-1, keepdims=True)
        - normed * jnp.mean(grad * normed, axis=-1, keepdims=True)
    )


def half_error_function(value):
    return 0.5 + 0.5 * lax.erf(value * 0.7071067811865476)


def gelu(value):
    return value * half_error_function(value)


def gelu_slope(value):
    density = jnp.exp(value * value * -0.5) * 0.3989422804014327
    return half_error_function(value) + value * density


def low_lanes(rows):
    return lax.broadcasted_iota(jnp.int32, (rows, PAIR), 1) < HEAD_DIM


def head_stack(pair):
    low = low_lanes(pair.shape[0])
    zero = jnp.zeros_like(pair)
    return jnp.concatenate([jnp.where(low, pair, zero), jnp.where(low, zero, pair)], axis=0)


def item_masks(counts_ref, lengths_ref):
    position = lax.broadcasted_iota(jnp.int32, (BUCKET, 128), 0)
    column = lax.broadcasted_iota(jnp.int32, (BUCKET, 128), 1)
    start = jnp.zeros((BUCKET, 128), jnp.int32)
    finish = jnp.zeros((BUCKET, 128), jnp.int32)
    valid = jnp.zeros((BUCKET, 128), jnp.int32)
    base = jnp.int32(0)
    first = jnp.int32(0)
    for level in range(counts_ref.shape[1]):
        extent = BUCKET >> level
        count = counts_ref[0, level]
        inside = (column >= first) & (column < first + count)
        here = base + (column - first) * extent
        start = jnp.where(inside, here, start)
        finish = jnp.where(inside, here + extent, finish)
        base = base + count * extent
        first = first + count
    for slot in range(lengths_ref.shape[1]):
        valid = jnp.where(column == slot, lengths_ref[0, slot], valid)
    member = (position >= start) & (position < finish)
    allowed = member & (position < start + valid)
    return (
        jnp.where(member, 1.0, 0.0).astype(bf16),
        jnp.where(allowed, 0.0, FORBIDDEN).astype(bf16),
    )


def attend(q_s, k_s, v_s, query_mask, key_mask, put):
    rows = q_s.shape[0]
    ones = jnp.ones((rows, 128), bf16)
    masks = jnp.concatenate([query_mask, query_mask], axis=0)
    low = low_lanes(rows)

    def scores_of(pair):
        at = slice(PAIR * pair, PAIR * (pair + 1))
        left = jnp.concatenate([head_stack(q_s[:, at]), masks], axis=1)
        return dot_last(left, jnp.concatenate([k_s[:, at], key_mask], axis=1))

    scores = scores_of(0)
    for pair in range(PAIRS):
        later = scores_of(pair + 1) if pair + 1 < PAIRS else None
        at = slice(PAIR * pair, PAIR * (pair + 1))
        top = jnp.max(scores, axis=-1, keepdims=True)
        weights = jnp.exp(scores - top).astype(bf16)
        mixed = dot(weights, jnp.concatenate([v_s[:, at], ones], axis=1))
        mixed = mixed[:, :PAIR] / mixed[:, PAIR:]
        put(at, jnp.where(low, mixed[:rows], mixed[rows:]).astype(bf16))
        scores = later


def train_attention_kernel(
    counts_ref, lengths_ref, x_ref, tail_ref, a_ref, bq_ref, bv_ref, w_any,
    ctx_ref, q_ref, k_ref, v_ref, w, sems,
):
    copies = [
        pltpu.make_async_copy(w_any.at[pl.ds(WIDTH * i, WIDTH)], w.at[i], sems.at[i]) for i in range(3)
    ]
    for copy in copies:
        copy.start()
    query_mask, key_mask = item_masks(counts_ref, lengths_ref)
    x = x_ref[...]
    aq = dot(x, a_ref[0]).astype(bf16)
    av = dot(x, a_ref[1]).astype(bf16)
    copies[0].wait()
    q = dot(x, w[0]) + row(tail_ref, BQ) + 2.0 * dot(aq, bq_ref[...])
    q_ref[...] = (q.astype(bf16).astype(f32) * HEAD_DIM**-0.5).astype(bf16)
    copies[1].wait()
    k_ref[...] = dot(x, w[1]).astype(bf16)
    copies[2].wait()
    v_ref[...] = (dot(x, w[2]) + row(tail_ref, BV) + 2.0 * dot(av, bv_ref[...])).astype(bf16)

    def put(at, value):
        ctx_ref[:, at] = value

    attend(q_ref, k_ref, v_ref, query_mask, key_mask, put)


def eval_attention_kernel(
    lengths_ref, x_ref, tail_ref, a_ref, bq_ref, bv_ref, w_any,
    ctx_ref, w, q_s, k_s, v_s, sems,
):
    step = pl.program_id(0)

    @pl.when(step == 0)
    def _():
        copies = [
            pltpu.make_async_copy(w_any.at[pl.ds(WIDTH * i, WIDTH)], w.at[i], sems.at[i])
            for i in range(3)
        ]
        for copy in copies:
            copy.start()
        for i, b_ref in ((0, bq_ref), (2, bv_ref)):
            copies[i].wait()
            merged = w[i].astype(f32) + 2.0 * dot(a_ref[i // 2], b_ref[...])
            w[i] = merged.astype(bf16)
        copies[1].wait()

    x = x_ref[...]
    q = dot(x, w[0]) + row(tail_ref, BQ)
    q_s[...] = (q.astype(bf16).astype(f32) * HEAD_DIM**-0.5).astype(bf16)
    k_s[...] = dot(x, w[1]).astype(bf16)
    v_s[...] = (dot(x, w[2]) + row(tail_ref, BV)).astype(bf16)
    position = lax.broadcasted_iota(jnp.int32, (BUCKET, 128), 0)
    column = lax.broadcasted_iota(jnp.int32, (BUCKET, 128), 1)
    length = lengths_ref[step]
    key_mask = jnp.where((column > 0) | (position < length), 0.0, FORBIDDEN).astype(bf16)
    query_mask = jnp.where(column == 0, 1.0, 0.0).astype(bf16)

    def put(at, value):
        ctx_ref[:, at] = value

    attend(q_s, k_s, v_s, query_mask, key_mask, put)


def feed_forward(h1, tail_ref, w1, w2, ready, keep):
    per_slab = WIDTH // CHUNK
    chunks = [(slab, CHUNK * part) for slab in range(SLABS) for part in range(per_slab)]

    def up(chunk):
        slab, at = chunk
        if at == 0:
            ready(slab)
        u = dot(h1, w1[slab, :, at : at + CHUNK]) + row(tail_ref, B1 + slab)[:, at : at + CHUNK]
        keep(slab, at, u)
        return u

    total = None
    u = up(chunks[0])
    for i, (slab, at) in enumerate(chunks):
        later = up(chunks[i + 1]) if i + 1 < len(chunks) else None
        part = dot(gelu(u).astype(bf16), w2[slab, at : at + CHUNK, :])
        total = part if total is None else total + part
        u = later
    return total


def eval_tail_kernel(
    x_ref, ctx_ref, tail_ref, wo_any, w1_any, w2_any, out_ref, wo, w1, w2, sems
):
    first = pl.program_id(0) == 0
    copies = [pltpu.make_async_copy(wo_any, wo, sems.at[0])]
    for slab in range(SLABS):
        copies.append(pltpu.make_async_copy(w1_any.at[slab], w1.at[slab], sems.at[1 + 2 * slab]))
        copies.append(pltpu.make_async_copy(w2_any.at[slab], w2.at[slab], sems.at[2 + 2 * slab]))

    @pl.when(first)
    def _():
        for copy in copies:
            copy.start()
        for copy in copies:
            copy.wait()

    resid = x_ref[...].astype(f32) + (dot(ctx_ref[...], wo[...]) + row(tail_ref, BO))
    normed, _ = normalise(resid)
    h1 = (normed * row(tail_ref, G1) + row(tail_ref, C1)).astype(bf16)
    down = feed_forward(h1, tail_ref, w1, w2, lambda slab: None, lambda slab, at, u: None)
    normed, _ = normalise(h1.astype(f32) + (down + row(tail_ref, B2)))
    out_ref[...] = (normed * row(tail_ref, G2) + row(tail_ref, C2)).astype(bf16)


def attention_back(q_ref, k_ref, v_ref, dctx, masks, dq_s, dk_s, dv_s):
    query_mask, key_mask = masks
    rows = q_ref.shape[0]
    masks = jnp.concatenate([query_mask, query_mask], axis=0)
    for pair in range(PAIRS):
        at = slice(PAIR * pair, PAIR * (pair + 1))
        q2, k, v, d2 = head_stack(q_ref[:, at]), k_ref[:, at], v_ref[:, at], head_stack(dctx[:, at])
        scores = dot_last(
            jnp.concatenate([k, key_mask], axis=1), jnp.concatenate([q2, masks], axis=1)
        )
        top = jnp.max(scores, axis=0, keepdims=True)
        probs = jnp.exp(scores - top)
        probs = probs * (1.0 / jnp.sum(probs, axis=0, keepdims=True))
        grad_probs = dot_last(v, d2)
        dv_s[:, at] = dot(probs.astype(bf16), d2).astype(bf16)
        weighted = probs * grad_probs
        inner = jnp.sum(weighted, axis=0, keepdims=True)
        grad_scores = (probs * (grad_probs - inner)).astype(bf16)
        dk_s[:, at] = dot(grad_scores, q2).astype(bf16)
        crossed = dot_first(k, grad_scores)
        dq = jnp.concatenate([crossed[:HEAD_DIM, :rows], crossed[HEAD_DIM:, rows:]], axis=0)
        dq_s[:, at] = (dq.T * HEAD_DIM**-0.5).astype(bf16)


def train_kernel(
    counts_ref, lengths_ref, x_ref, q_ref, k_ref, v_ref, ctx_ref, grad_ref, tail_ref, a_ref, bq_ref, bv_ref,
    w_any, wo_any, w1_any, w2_any,
    out_ref, token_ref, gq_ref, gv_ref,
    w, wo, w1, w2, u_s, dq_s, dk_s, dv_s, sems,
):
    copies = [pltpu.make_async_copy(wo_any, wo, sems.at[0])]
    for slab in range(SLABS):
        copies.append(pltpu.make_async_copy(w1_any.at[slab], w1.at[slab], sems.at[1 + 2 * slab]))
        copies.append(pltpu.make_async_copy(w2_any.at[slab], w2.at[slab], sems.at[2 + 2 * slab]))
    qkv = pltpu.make_async_copy(w_any.at[pl.ds(0, QKV_ROWS)], w, sems.at[1 + 2 * SLABS])
    for copy in [*copies, qkv]:
        copy.start()

    x = x_ref[...]
    copies[0].wait()
    resid = x.astype(f32) + (dot(ctx_ref[...], wo[...]) + row(tail_ref, BO))
    normed_one, scale_one = normalise(resid)
    h1 = (normed_one * row(tail_ref, G1) + row(tail_ref, C1)).astype(bf16)

    def ready(slab):
        copies[1 + 2 * slab].wait()
        copies[2 + 2 * slab].wait()

    def keep(slab, at, u):
        u_s[slab, :, at : at + CHUNK] = u

    down = feed_forward(h1, tail_ref, w1, w2, ready, keep)
    normed_two, scale_two = normalise(h1.astype(f32) + (down + row(tail_ref, B2)))
    out_ref[...] = (normed_two * row(tail_ref, G2) + row(tail_ref, C2)).astype(bf16)

    grad_two = normalise_back(grad_ref[...].astype(f32) * row(tail_ref, G2), normed_two, scale_two)
    df = grad_two.astype(bf16)
    total = None
    for slab in range(SLABS):
        for at in range(0, WIDTH, CHUNK):
            grad_gelu = dot_last(df, w2[slab, at : at + CHUNK, :])
            du = (grad_gelu * gelu_slope(u_s[slab, :, at : at + CHUNK])).astype(bf16)
            part = dot_last(du, w1[slab, :, at : at + CHUNK])
            total = part if total is None else total + part
    dh1 = (grad_two + total).astype(bf16)
    grad_one = normalise_back(dh1.astype(f32) * row(tail_ref, G1), normed_one, scale_one)
    token_ref[...] = grad_one
    dctx = dot_last(grad_one.astype(bf16), wo[...]).astype(bf16)
    attention_back(q_ref, k_ref, v_ref, dctx, item_masks(counts_ref, lengths_ref), dq_s, dk_s, dv_s)

    qkv.wait()
    dq, dk, dv = dq_s[...], dk_s[...], dv_s[...]
    daq = (2.0 * dot_last(dq, bq_ref[...])).astype(bf16)
    dav = (2.0 * dot_last(dv, bv_ref[...])).astype(bf16)
    aq = dot(x, a_ref[0]).astype(bf16)
    av = dot(x, a_ref[1]).astype(bf16)
    gq_ref[...] = 2.0 * dot_first(aq, dq)
    gv_ref[...] = 2.0 * dot_first(av, dv)
    token_ref[...] += (
        dot_last(dq, w[:WIDTH])
        + dot_last(dk, w[WIDTH : 2 * WIDTH])
        + dot_last(dv, w[2 * WIDTH :])
        + dot_last(daq, a_ref[0])
        + dot_last(dav, a_ref[1])
    )


def whole(shape):
    return pl.BlockSpec(shape, lambda *_: (0,) * len(shape))


ANY = pl.BlockSpec(memory_space=pl.ANY)
SCALARS = pl.BlockSpec(memory_space=pltpu.SMEM)
PARAMS = pltpu.CompilerParams(vmem_limit_bytes=VMEM)


def train_attention(counts, lengths, x, tail, a, bq, bv, w):
    rows = x.shape[0]
    shape = (rows, WIDTH)
    return pl.pallas_call(
        train_attention_kernel,
        in_specs=[SCALARS, SCALARS]
        + [whole(shape), whole(tail.shape), whole(a.shape), whole(bq.shape), whole(bv.shape), ANY],
        out_specs=[whole(shape)] * 4,
        out_shape=[jax.ShapeDtypeStruct(shape, bf16)] * 4,
        grid=(1,),
        scratch_shapes=[pltpu.VMEM((3, WIDTH, WIDTH), bf16), pltpu.SemaphoreType.DMA((3,))],
        compiler_params=PARAMS,
        name="train_attention",
    )(counts, lengths, x, tail, a, bq, bv, w)


def eval_attention(lengths, x, tail, a, bq, bv, w):
    rows = x.shape[0]
    block = pl.BlockSpec((BUCKET, WIDTH), lambda i: (i, 0))
    return pl.pallas_call(
        eval_attention_kernel,
        in_specs=[SCALARS, block]
        + [whole(tail.shape), whole(a.shape), whole(bq.shape), whole(bv.shape), ANY],
        out_specs=block,
        out_shape=jax.ShapeDtypeStruct((rows, WIDTH), bf16),
        grid=(rows // BUCKET,),
        scratch_shapes=[pltpu.VMEM((3, WIDTH, WIDTH), bf16)]
        + [pltpu.VMEM((BUCKET, WIDTH), bf16)] * 3
        + [pltpu.SemaphoreType.DMA((3,))],
        compiler_params=PARAMS,
        name="eval_attention",
    )(lengths, x, tail, a, bq, bv, w)


def eval_tail(x, ctx, tail, wo, w1, w2):
    rows = x.shape[0]
    block = pl.BlockSpec((BUCKET, WIDTH), lambda i: (i, 0))
    return pl.pallas_call(
        eval_tail_kernel,
        in_specs=[block, block, whole(tail.shape), ANY, ANY, ANY],
        out_specs=block,
        out_shape=jax.ShapeDtypeStruct((rows, WIDTH), bf16),
        grid=(rows // BUCKET,),
        scratch_shapes=[
            pltpu.VMEM((WIDTH, WIDTH), bf16),
            pltpu.VMEM((SLABS, WIDTH, WIDTH), bf16),
            pltpu.VMEM((SLABS, WIDTH, WIDTH), bf16),
            pltpu.SemaphoreType.DMA((1 + 2 * SLABS,)),
        ],
        compiler_params=PARAMS,
        name="eval_tail",
    )(x, ctx, tail, wo, w1, w2)


def train_rest(counts, lengths, x, q, k, v, ctx, grad, tail, a, bq, bv, w, wo, w1, w2):
    rows = x.shape[0]
    shape = (rows, WIDTH)
    return pl.pallas_call(
        train_kernel,
        in_specs=[SCALARS, SCALARS]
        + [whole(shape)] * 6
        + [whole(tail.shape), whole(a.shape), whole(bq.shape), whole(bv.shape)]
        + [ANY] * 4,
        out_specs=[whole(shape), whole(shape), whole(bq.shape), whole(bv.shape)],
        out_shape=[
            jax.ShapeDtypeStruct(shape, bf16),
            jax.ShapeDtypeStruct(shape, f32),
            jax.ShapeDtypeStruct(bq.shape, f32),
            jax.ShapeDtypeStruct(bv.shape, f32),
        ],
        grid=(1,),
        scratch_shapes=[
            pltpu.VMEM((QKV_ROWS, WIDTH), bf16),
            pltpu.VMEM((WIDTH, WIDTH), bf16),
            pltpu.VMEM((SLABS, WIDTH, WIDTH), bf16),
            pltpu.VMEM((SLABS, WIDTH, WIDTH), bf16),
            pltpu.VMEM((SLABS, rows, WIDTH), f32),
            pltpu.VMEM(shape, bf16),
            pltpu.VMEM(shape, bf16),
            pltpu.VMEM(shape, bf16),
            pltpu.SemaphoreType.DMA((2 + 2 * SLABS,)),
        ],
        compiler_params=PARAMS,
        name="train_rest",
    )(counts, lengths, x, q, k, v, ctx, grad, tail, a, bq, bv, w, wo, w1, w2)


def local(
    tokens,
    bucket_item_counts,
    slot_item_lengths,
    frozen,
    query_lowrank_matrix,
    value_lowrank_matrix,
    output_gradient,
    evaluation_tokens,
    evaluation_lengths,
    *,
    mesh,
):
    axes = ("fsdp", "rep")
    devices = mesh.shape["fsdp"] * mesh.shape["rep"]
    me = lax.axis_index(axes)
    share = WEIGHT_ROWS // devices
    extra = frozen.shape[0] - share * WIDTH
    spill = extra * devices
    before = lax.ppermute(
        frozen[-spill:], axes, [(d, (d + 1) % devices) for d in range(devices)]
    )
    window = lax.dynamic_slice(
        jnp.concatenate([before, frozen]), (spill - extra * me,), (share * WIDTH,)
    ).reshape(share, WIDTH)
    gathered = lax.all_gather(window, axes, axis=0, tiled=True)
    tail = lax.psum(jnp.where(me == devices - 1, frozen[-spill:].astype(f32), 0.0), axes).astype(bf16)
    vectors = tail[: VECTOR_ROWS * WIDTH].reshape(VECTOR_ROWS, WIDTH)
    vectors = jnp.pad(vectors, ((0, 16 - VECTOR_ROWS), (0, 0)))
    a = tail[VECTOR_ROWS * WIDTH :].reshape(2, WIDTH, RANK)
    bq = query_lowrank_matrix.astype(bf16)
    bv = value_lowrank_matrix.astype(bf16)
    wo = gathered[QKV_ROWS : QKV_ROWS + WIDTH]
    w1 = gathered[QKV_ROWS + WIDTH : QKV_ROWS + WIDTH * (1 + SLABS)]
    w1 = w1.reshape(WIDTH, SLABS, WIDTH).transpose(1, 0, 2)
    w2 = gathered[QKV_ROWS + WIDTH * (1 + SLABS) :].reshape(SLABS, WIDTH, WIDTH)

    ctx, q, k, v = train_attention(
        bucket_item_counts, slot_item_lengths, tokens, vectors, a, bq, bv, gathered
    )
    eval_ctx = eval_attention(evaluation_lengths, evaluation_tokens, vectors, a, bq, bv, gathered)
    out, token_gradient, gq, gv = train_rest(
        bucket_item_counts, slot_item_lengths, tokens, q, k, v, ctx, output_gradient,
        vectors, a, bq, bv, gathered, wo, w1, w2,
    )
    gq, gv = lax.psum((gq, gv), axes)
    eval_out = eval_tail(evaluation_tokens, eval_ctx, vectors, wo, w1, w2)
    return out, token_gradient, gq, gv, eval_out


def solution(mesh):
    split = P(("fsdp", "rep"), None)
    flat = P(("fsdp", "rep"))
    return jax.shard_map(
        functools.partial(local, mesh=mesh),
        mesh=mesh,
        in_specs=(split, split, split, flat, P(), P(), split, split, flat),
        out_specs=(split, split, P(), P(), split),
        check_vma=False,
    )
```

```python
import functools

import jax
import jax.numpy as jnp
from jax import lax
from jax.experimental import pallas as pl
from jax.experimental.pallas import tpu as pltpu
from jax.sharding import PartitionSpec as P

WIDTH = 768
HEADS = 12
HEAD_DIM = 64
SLABS = 4
BUCKET = 512
CHUNK = 256
PAIR = 2 * HEAD_DIM
PAIRS = HEADS // 2
WEIGHT_ROWS = WIDTH * (4 + 2 * SLABS)
QKV_ROWS = 3 * WIDTH
VECTOR_ROWS = 12
RANK = 8
FORBIDDEN = -1e30
EPS = 1e-5
VMEM = 60 * 2**20
REST_ROWS = WEIGHT_ROWS - QKV_ROWS
UP_AT = WIDTH
DOWN_AT = WIDTH * (1 + SLABS)
TAIL_ROWS = 32
PAD_ROWS = 16
A_AT = 16
LANES = 128

f32 = jnp.float32
bf16 = jnp.bfloat16

BQ, BV, BO, B1, B2, G1, C1, G2, C2 = 0, 1, 2, 3, 7, 8, 9, 10, 11


def dot(left, right):
    return jnp.dot(left, right, preferred_element_type=f32)


def dot_last(left, right):
    return lax.dot_general(left, right, (((1,), (1,)), ((), ())), preferred_element_type=f32)


def dot_first(left, right):
    return lax.dot_general(left, right, (((0,), (0,)), ((), ())), preferred_element_type=f32)


def row(tail_ref, at):
    return tail_ref[:A_AT].astype(f32)[at : at + 1]


def adapter(tail_ref, which):
    return tail_ref[A_AT:].astype(f32)[RANK * which : RANK * (which + 1)].astype(bf16)


def normalise(resid):
    centred = resid - jnp.mean(resid, axis=-1, keepdims=True)
    scale = lax.rsqrt(jnp.mean(centred * centred, axis=-1, keepdims=True) + EPS)
    return centred * scale, scale


def normalise_back(grad, normed, scale):
    return scale * (
        grad
        - jnp.mean(grad, axis=-1, keepdims=True)
        - normed * jnp.mean(grad * normed, axis=-1, keepdims=True)
    )


def half_error_function(value):
    return 0.5 + 0.5 * lax.erf(value * 0.7071067811865476)


def gelu(value):
    return value * half_error_function(value)


def gelu_slope(value):
    density = jnp.exp(value * value * -0.5) * 0.3989422804014327
    return half_error_function(value) + value * density


def low_lanes(rows):
    return lax.broadcasted_iota(jnp.int32, (rows, PAIR), 1) < HEAD_DIM


def head_stack(pair):
    low = low_lanes(pair.shape[0])
    zero = jnp.zeros_like(pair)
    return jnp.concatenate([jnp.where(low, pair, zero), jnp.where(low, zero, pair)], axis=0)


def item_masks(counts_ref, lengths_ref):
    position = lax.broadcasted_iota(jnp.int32, (BUCKET, 128), 0)
    column = lax.broadcasted_iota(jnp.int32, (BUCKET, 128), 1)
    start = jnp.zeros((BUCKET, 128), jnp.int32)
    finish = jnp.zeros((BUCKET, 128), jnp.int32)
    valid = jnp.zeros((BUCKET, 128), jnp.int32)
    base = jnp.int32(0)
    first = jnp.int32(0)
    for level in range(counts_ref.shape[1]):
        extent = BUCKET >> level
        count = counts_ref[0, level]
        inside = (column >= first) & (column < first + count)
        here = base + (column - first) * extent
        start = jnp.where(inside, here, start)
        finish = jnp.where(inside, here + extent, finish)
        base = base + count * extent
        first = first + count
    for slot in range(lengths_ref.shape[1]):
        valid = jnp.where(column == slot, lengths_ref[0, slot], valid)
    member = (position >= start) & (position < finish)
    allowed = member & (position < start + valid)
    return (
        jnp.where(member, 1.0, 0.0).astype(bf16),
        jnp.where(allowed, 0.0, FORBIDDEN).astype(bf16),
    )


def attend(q_s, k_s, v_s, query_mask, key_mask, put):
    rows = q_s.shape[0]
    ones = jnp.ones((rows, 128), bf16)
    masks = jnp.concatenate([query_mask, query_mask], axis=0)
    low = low_lanes(rows)

    def scores_of(pair):
        at = slice(PAIR * pair, PAIR * (pair + 1))
        left = jnp.concatenate([head_stack(q_s[:, at]), masks], axis=1)
        return dot_last(left, jnp.concatenate([k_s[:, at], key_mask], axis=1))

    scores = scores_of(0)
    for pair in range(PAIRS):
        later = scores_of(pair + 1) if pair + 1 < PAIRS else None
        at = slice(PAIR * pair, PAIR * (pair + 1))
        top = jnp.max(scores, axis=-1, keepdims=True)
        weights = jnp.exp(scores - top).astype(bf16)
        mixed = dot(weights, jnp.concatenate([v_s[:, at], ones], axis=1))
        mixed = mixed[:, :PAIR] / mixed[:, PAIR:]
        put(at, jnp.where(low, mixed[:rows], mixed[rows:]).astype(bf16))
        scores = later


def copy_qkv(table_ref, refs, w, sems, tail=None):
    if len(refs) == 2:
        pltpu.make_async_copy(refs[0], w, sems.at[0]).start()
        if tail is not None:
            pltpu.make_async_copy(refs[1], tail, sems.at[1]).start()
            pltpu.make_async_copy(tail, tail, sems.at[1]).wait()
        pltpu.make_async_copy(w, w, sems.at[0]).wait()
        return
    units = len(refs) // 2
    size = refs[0].shape[0]

    def start(chosen):
        for i, ref in enumerate(chosen):
            to = pl.multiple_of(table_ref[i] * size, 16)
            pltpu.make_async_copy(ref.at[pl.ds(0, size)], w.at[pl.ds(to, size)], sems.at[0]).start()

    @pl.when(table_ref[units] == 0)
    def _():
        start(refs[:units])

    @pl.when(table_ref[units] != 0)
    def _():
        start(refs[units:])

    if tail is not None:
        for i, ref in enumerate(refs[units:]):

            @pl.when(table_ref[i] == 0)
            def _():
                rows = ref.at[pl.ds(size, TAIL_ROWS)]
                pltpu.make_async_copy(rows, tail, sems.at[1]).start()

        pltpu.make_async_copy(tail, tail, sems.at[1]).wait()
    pltpu.make_async_copy(w, w, sems.at[0]).wait()


def copy_rest(table_ref, refs, w, sem):
    if len(refs) == 1:
        pltpu.make_async_copy(refs[0], w, sem).start()
        return
    units = len(refs) // 3
    size = refs[-1].shape[1]

    def start(ref, at):
        to = pl.multiple_of(at * size, 16)
        pltpu.make_async_copy(ref, w.at[pl.ds(to, size)], sem).start()

    @pl.when(table_ref[3 * units] == 0)
    def _():
        for i in range(units):
            start(refs[units + i].at[pl.ds(0, size)], table_ref[i])

    @pl.when(table_ref[3 * units] != 0)
    def _():
        for i in range(units):
            start(refs[i].at[pl.ds(0, size)], table_ref[i])

    for i in range(units):
        for slot in range(2):
            start(refs[2 * units + i].at[slot], table_ref[units + 2 * i + slot])


def slabs_of_columns(w, lanes):
    rows = slice(UP_AT, DOWN_AT)
    for at in range(0, WIDTH, LANES):
        lanes[...] = w[rows, at : at + LANES].astype(f32)
        for slab in range(SLABS):
            to = UP_AT + WIDTH * slab
            part = lanes[pl.ds(slab, WIDTH, stride=SLABS), :]
            w[to : to + WIDTH, at : at + LANES] = part.astype(bf16)


def wait_rest(w, sem):
    pltpu.make_async_copy(w, w, sem).wait()


def train_attention_kernel(
    counts_ref, lengths_ref, table_ref, x_ref, bq_ref, bv_ref, *refs
):
    *w_refs, ctx_ref, q_ref, k_ref, v_ref, tail_ref, w, sems = refs
    copy_qkv(table_ref, w_refs, w, sems, tail_ref)
    query_mask, key_mask = item_masks(counts_ref, lengths_ref)
    x = x_ref[...]
    aq = dot_last(x, adapter(tail_ref, 0)).astype(bf16)
    av = dot_last(x, adapter(tail_ref, 1)).astype(bf16)
    q = dot(x, w[:WIDTH]) + row(tail_ref, BQ) + 2.0 * dot(aq, bq_ref[...])
    q_ref[...] = (q.astype(bf16).astype(f32) * HEAD_DIM**-0.5).astype(bf16)
    k_ref[...] = dot(x, w[WIDTH : 2 * WIDTH]).astype(bf16)
    v = dot(x, w[2 * WIDTH :]) + row(tail_ref, BV) + 2.0 * dot(av, bv_ref[...])
    v_ref[...] = v.astype(bf16)

    def put(at, value):
        ctx_ref[:, at] = value

    attend(q_ref, k_ref, v_ref, query_mask, key_mask, put)


def eval_attention_kernel(
    lengths_ref, table_ref, x_ref, tail_ref, bq_ref, bv_ref, *refs, first
):
    *w_refs, ctx_ref, w, q_s, k_s, v_s, sems = refs
    step = pl.program_id(0)

    @pl.when(step == 0)
    def _():
        copy_qkv(table_ref, w_refs, w, sems)
        for i, b_ref in ((0, bq_ref), (2, bv_ref)):
            rows = slice(WIDTH * i, WIDTH * (i + 1))
            merged = w[rows].astype(f32) + 2.0 * dot_first(adapter(tail_ref, i // 2), b_ref[...])
            w[rows] = merged.astype(bf16)

    x = x_ref[...]
    q = dot(x, w[:WIDTH]) + row(tail_ref, BQ)
    q_s[...] = (q.astype(bf16).astype(f32) * HEAD_DIM**-0.5).astype(bf16)
    k_s[...] = dot(x, w[WIDTH : 2 * WIDTH]).astype(bf16)
    v_s[...] = (dot(x, w[2 * WIDTH :]) + row(tail_ref, BV)).astype(bf16)
    position = lax.broadcasted_iota(jnp.int32, (BUCKET, LANES), 0)
    column = lax.broadcasted_iota(jnp.int32, (BUCKET, LANES), 1)
    length = lengths_ref[first + step]
    key_mask = jnp.where((column > 0) | (position < length), 0.0, FORBIDDEN).astype(bf16)
    query_mask = jnp.where(column == 0, 1.0, 0.0).astype(bf16)

    def put(at, value):
        ctx_ref[:, at] = value

    attend(q_s, k_s, v_s, query_mask, key_mask, put)


def up_weight(w, slab, at):
    return w[UP_AT + WIDTH * slab : UP_AT + WIDTH * (slab + 1), at : at + CHUNK]


def down_weight(w, slab, at):
    rows = DOWN_AT + WIDTH * slab + at
    return w[rows : rows + CHUNK]


def feed_forward(h1, tail_ref, w, keep):
    chunks = [(slab, at) for slab in range(SLABS) for at in range(0, WIDTH, CHUNK)]

    def up(slab, at):
        u = dot(h1, up_weight(w, slab, at)) + row(tail_ref, B1 + slab)[:, at : at + CHUNK]
        keep(slab, at, u)
        return u

    total = None
    u = up(*chunks[0])
    for i, (slab, at) in enumerate(chunks):
        later = up(*chunks[i + 1]) if i + 1 < len(chunks) else None
        part = dot(gelu(u).astype(bf16), down_weight(w, slab, at))
        total = part if total is None else total + part
        u = later
    return total


def eval_tail_kernel(x_ref, ctx_ref, tail_ref, w_any, *refs):
    out_ref, w, sem = refs[-3:]

    @pl.when(pl.program_id(0) == 0)
    def _():
        copy = pltpu.make_async_copy(w_any, w, sem)
        copy.start()
        copy.wait()

    resid = x_ref[...].astype(f32) + (dot(ctx_ref[...], w[:WIDTH]) + row(tail_ref, BO))
    normed, _ = normalise(resid)
    h1 = (normed * row(tail_ref, G1) + row(tail_ref, C1)).astype(bf16)
    down = feed_forward(h1, tail_ref, w, lambda slab, at, u: None)
    normed, _ = normalise(h1.astype(f32) + (down + row(tail_ref, B2)))
    out_ref[...] = (normed * row(tail_ref, G2) + row(tail_ref, C2)).astype(bf16)


def attention_back(q_ref, k_ref, v_ref, dctx, masks, dq_s, dk_s, dv_s):
    query_mask, key_mask = masks
    rows = q_ref.shape[0]
    masks = jnp.concatenate([query_mask, query_mask], axis=0)
    for pair in range(PAIRS):
        at = slice(PAIR * pair, PAIR * (pair + 1))
        q2, k, v, d2 = head_stack(q_ref[:, at]), k_ref[:, at], v_ref[:, at], head_stack(dctx[:, at])
        scores = dot_last(
            jnp.concatenate([k, key_mask], axis=1), jnp.concatenate([q2, masks], axis=1)
        )
        top = jnp.max(scores, axis=0, keepdims=True)
        probs = jnp.exp(scores - top)
        probs = probs * (1.0 / jnp.sum(probs, axis=0, keepdims=True))
        grad_probs = dot_last(v, d2)
        dv_s[:, at] = dot(probs.astype(bf16), d2).astype(bf16)
        weighted = probs * grad_probs
        inner = jnp.sum(weighted, axis=0, keepdims=True)
        grad_scores = (probs * (grad_probs - inner)).astype(bf16)
        dk_s[:, at] = dot(grad_scores, q2).astype(bf16)
        crossed = dot_first(k, grad_scores)
        dq = jnp.concatenate([crossed[:HEAD_DIM, :rows], crossed[HEAD_DIM:, rows:]], axis=0)
        dq_s[:, at] = (dq.T * HEAD_DIM**-0.5).astype(bf16)


def train_kernel(
    counts_ref, lengths_ref, table_ref, rest_table_ref, x_ref, q_ref, k_ref, v_ref, ctx_ref, grad_ref,
    tail_ref, bq_ref, bv_ref, *refs, n_qkv,
):
    *w_refs, out_ref, token_ref, sums_ref, w_any, wqkv, w, lanes, u_s, dq_s, dk_s, dv_s, sems = refs
    copy_rest(rest_table_ref, w_refs[n_qkv:], w, sems.at[2])
    copy_qkv(table_ref, w_refs[:n_qkv], wqkv, sems)
    wait_rest(w, sems.at[2])
    if len(w_refs) > 3:
        slabs_of_columns(w, lanes)
    keep_rest = pltpu.make_async_copy(w, w_any, sems.at[3])
    keep_rest.start()

    x = x_ref[...]
    resid = x.astype(f32) + (dot(ctx_ref[...], w[:WIDTH]) + row(tail_ref, BO))
    normed_one, scale_one = normalise(resid)
    h1 = (normed_one * row(tail_ref, G1) + row(tail_ref, C1)).astype(bf16)

    def keep(slab, at, u):
        u_s[slab, :, at : at + CHUNK] = u

    down = feed_forward(h1, tail_ref, w, keep)
    normed_two, scale_two = normalise(h1.astype(f32) + (down + row(tail_ref, B2)))
    out_ref[...] = (normed_two * row(tail_ref, G2) + row(tail_ref, C2)).astype(bf16)

    grad_two = normalise_back(grad_ref[...].astype(f32) * row(tail_ref, G2), normed_two, scale_two)
    df = grad_two.astype(bf16)
    total = None
    for slab in range(SLABS):
        for at in range(0, WIDTH, CHUNK):
            grad_gelu = dot_last(df, down_weight(w, slab, at))
            du = (grad_gelu * gelu_slope(u_s[slab, :, at : at + CHUNK])).astype(bf16)
            part = dot_last(du, up_weight(w, slab, at))
            total = part if total is None else total + part
    dh1 = (grad_two + total).astype(bf16)
    grad_one = normalise_back(dh1.astype(f32) * row(tail_ref, G1), normed_one, scale_one)
    token_ref[...] = grad_one
    dctx = dot_last(grad_one.astype(bf16), w[:WIDTH]).astype(bf16)
    attention_back(q_ref, k_ref, v_ref, dctx, item_masks(counts_ref, lengths_ref), dq_s, dk_s, dv_s)

    dq, dk, dv = dq_s[...], dk_s[...], dv_s[...]
    daq = (2.0 * dot_last(dq, bq_ref[...])).astype(bf16)
    dav = (2.0 * dot_last(dv, bv_ref[...])).astype(bf16)
    aq = dot_last(x, adapter(tail_ref, 0)).astype(bf16)
    av = dot_last(x, adapter(tail_ref, 1)).astype(bf16)
    sums_ref[:RANK] = 2.0 * dot_first(aq, dq)
    sums_ref[RANK:] = 2.0 * dot_first(av, dv)
    token_ref[...] += (
        dot_last(dq, wqkv[:WIDTH])
        + dot_last(dk, wqkv[WIDTH : 2 * WIDTH])
        + dot_last(dv, wqkv[2 * WIDTH :])
        + dot(daq, adapter(tail_ref, 0))
        + dot(dav, adapter(tail_ref, 1))
    )
    keep_rest.wait()


def window_kernel(place_ref, before_ref, own_ref, out_ref, padded_ref, flat, moved):
    ahead = before_ref.shape[0]
    flat[:ahead] = before_ref[...].astype(f32)
    flat[ahead : ahead + own_ref.shape[0]] = own_ref[...].astype(f32)
    flat[ahead + own_ref.shape[0] :] = jnp.zeros((LANES, LANES), f32)
    rows = moved.shape[0]
    start, turn = place_ref[0], place_ref[1]
    back = lax.rem(LANES - turn, LANES)
    here = pltpu.roll(flat[pl.ds(start, rows), :], back, 1)
    after = pltpu.roll(flat[pl.ds(start + 1, rows), :], back, 1)
    lane = lax.broadcasted_iota(jnp.int32, (rows, LANES), 1)
    moved[...] = jnp.where(lane < LANES - turn, here, after)
    per_row = WIDTH // LANES
    for tile in range(per_row):
        part = moved[pl.ds(tile, rows // per_row, stride=per_row), :]
        at = slice(LANES * tile, LANES * (tile + 1))
        out_ref[:, at] = part.astype(bf16)
        padded_ref[: rows // per_row, at] = part.astype(bf16)
    padded_ref[rows // per_row :] = jnp.zeros((PAD_ROWS, WIDTH), bf16)


def whole(shape):
    return pl.BlockSpec(shape, lambda *_: (0,) * len(shape))


def cost(microseconds):
    return pl.CostEstimate(flops=int(microseconds * 1e9), bytes_accessed=0, transcendentals=0)


def after(value, *others):
    return lax.optimization_barrier((value, *others))[0]


ANY = pl.BlockSpec(memory_space=pl.ANY)
SCALARS = pl.BlockSpec(memory_space=pltpu.SMEM)
PARAMS = pltpu.CompilerParams(vmem_limit_bytes=VMEM)


QKV_SCRATCH = pltpu.VMEM((QKV_ROWS, WIDTH), bf16)
REST_SCRATCH = pltpu.VMEM((REST_ROWS, WIDTH), bf16)


def train_attention(counts, lengths, table, x, bq, bv, w):
    rows = x.shape[0]
    shape = (rows, WIDTH)
    return pl.pallas_call(
        train_attention_kernel,
        in_specs=[SCALARS] * 3
        + [whole(v.shape) for v in (x, bq, bv)]
        + [ANY] * len(w),
        out_specs=[whole(shape)] * 4 + [whole((TAIL_ROWS, WIDTH))],
        out_shape=[jax.ShapeDtypeStruct(shape, bf16)] * 4
        + [jax.ShapeDtypeStruct((TAIL_ROWS, WIDTH), bf16)],
        grid=(1,),
        scratch_shapes=[QKV_SCRATCH, pltpu.SemaphoreType.DMA((2,))],
        compiler_params=PARAMS,
        cost_estimate=cost(11),
        name="train_attention",
    )(counts, lengths, table, x, bq, bv, *w)


def eval_attention(lengths, table, x, tail, bq, bv, w, first, count):
    block = pl.BlockSpec((BUCKET, WIDTH), lambda i: (i + first, 0))
    return pl.pallas_call(
        functools.partial(eval_attention_kernel, first=first),
        in_specs=[SCALARS] * 2
        + [block]
        + [whole(v.shape) for v in (tail, bq, bv)]
        + [ANY] * len(w),
        out_specs=pl.BlockSpec((BUCKET, WIDTH), lambda i: (i, 0)),
        out_shape=jax.ShapeDtypeStruct((count * BUCKET, WIDTH), bf16),
        grid=(count,),
        scratch_shapes=[QKV_SCRATCH]
        + [pltpu.VMEM((BUCKET, WIDTH), bf16)] * 3
        + [pltpu.SemaphoreType.DMA((2,))],
        compiler_params=PARAMS,
        cost_estimate=cost(1 + 7 * count),
        name="eval_attention",
    )(lengths, table, x, tail, bq, bv, *w)


def eval_tail(x, ctx, tail, w, first, done=None):
    rows = ctx.shape[0]
    given = [] if done is None else [done]
    return pl.pallas_call(
        eval_tail_kernel,
        in_specs=[
            pl.BlockSpec((BUCKET, WIDTH), lambda i: (i + first, 0)),
            pl.BlockSpec((BUCKET, WIDTH), lambda i: (i, 0)),
            whole(tail.shape),
            ANY,
        ]
        + [ANY] * len(given),
        out_specs=pl.BlockSpec((BUCKET, WIDTH), lambda i: (i + first, 0)),
        out_shape=jax.ShapeDtypeStruct(x.shape, bf16),
        grid=(rows // BUCKET,),
        scratch_shapes=[REST_SCRATCH, pltpu.SemaphoreType.DMA],
        input_output_aliases={4: 0} if given else {},
        compiler_params=PARAMS,
        cost_estimate=cost(3 + 8 * (rows // BUCKET)),
        name="eval_tail",
    )(x, ctx, tail, w, *given)


def train_rest(counts, lengths, table, rest_table, x, q, k, v, ctx, grad, tail, bq, bv, w, rest):
    rows = x.shape[0]
    shape = (rows, WIDTH)
    return pl.pallas_call(
        functools.partial(train_kernel, n_qkv=len(w)),
        in_specs=[SCALARS] * 4
        + [whole(shape)] * 6
        + [whole(v.shape) for v in (tail, bq, bv)]
        + [ANY] * (len(w) + len(rest)),
        out_specs=[whole(shape), whole(shape), whole((2 * RANK, WIDTH)), ANY],
        out_shape=[
            jax.ShapeDtypeStruct(shape, bf16),
            jax.ShapeDtypeStruct(shape, f32),
            jax.ShapeDtypeStruct((2 * RANK, WIDTH), f32),
            jax.ShapeDtypeStruct((REST_ROWS, WIDTH), bf16),
        ],
        grid=(1,),
        scratch_shapes=[
            QKV_SCRATCH,
            REST_SCRATCH,
            pltpu.VMEM((SLABS * WIDTH, LANES), f32),
            pltpu.VMEM((SLABS, rows, WIDTH), f32),
            pltpu.VMEM(shape, bf16),
            pltpu.VMEM(shape, bf16),
            pltpu.VMEM(shape, bf16),
            pltpu.SemaphoreType.DMA((4,)),
        ],
        compiler_params=PARAMS,
        cost_estimate=cost(36),
        name="train_rest",
    )(counts, lengths, table, rest_table, x, q, k, v, ctx, grad, tail, bq, bv, *w, *rest)


def window(start, turn, before, own, rows):
    ahead = before.shape[0]
    place = jnp.stack([start, turn]).astype(jnp.int32)
    return pl.pallas_call(
        window_kernel,
        in_specs=[SCALARS, whole(before.shape), whole(own.shape)],
        out_specs=[whole((rows, WIDTH)), whole((rows + PAD_ROWS, WIDTH))],
        out_shape=[
            jax.ShapeDtypeStruct((rows, WIDTH), bf16),
            jax.ShapeDtypeStruct((rows + PAD_ROWS, WIDTH), bf16),
        ],
        grid=(1,),
        scratch_shapes=[
            pltpu.VMEM((ahead + own.shape[0] + LANES, LANES), f32),
            pltpu.VMEM((rows * (WIDTH // LANES), LANES), f32),
        ],
        compiler_params=PARAMS,
        cost_estimate=cost(2),
        name="window",
    )(place, before, own)


AXES = ("fsdp", "rep")


def tail_rows(flat):
    at = VECTOR_ROWS * WIDTH
    vectors = jnp.pad(flat[:at].reshape(VECTOR_ROWS, WIDTH), ((0, A_AT - VECTOR_ROWS), (0, 0)))
    a = flat[at:].reshape(2, WIDTH, RANK).transpose(0, 2, 1).reshape(2 * RANK, WIDTH)
    return jnp.concatenate([vectors, a])


def collect_generic(frozen, devices):
    me = lax.axis_index(AXES)
    share = WEIGHT_ROWS // devices
    extra = frozen.shape[0] - share * WIDTH
    spill = extra * devices
    before = lax.ppermute(frozen[-spill:], AXES, [(d, (d + 1) % devices) for d in range(devices)])
    flat = lax.dynamic_slice(
        jnp.concatenate([before, frozen]), (spill - extra * me,), (share * WIDTH,)
    )
    gathered = lax.all_gather(flat.reshape(share, WIDTH), AXES, axis=0, tiled=True)
    tail = lax.psum(jnp.where(me == devices - 1, frozen[-spill:].astype(f32), 0.0), AXES)
    w1 = gathered[QKV_ROWS + WIDTH : QKV_ROWS + WIDTH * (1 + SLABS)]
    w1 = w1.reshape(WIDTH, SLABS, WIDTH).transpose(1, 0, 2).reshape(WIDTH * SLABS, WIDTH)
    rest = jnp.concatenate(
        [gathered[QKV_ROWS : QKV_ROWS + WIDTH], w1, gathered[QKV_ROWS + WIDTH * (1 + SLABS) :]]
    )
    none = jnp.zeros((8,), jnp.int32)
    return none, [gathered[:QKV_ROWS], tail_rows(tail.astype(bf16))], none, [rest]


def device(z, x, y, core):
    return ((z * 2 + x) * 2 + y) * 2 + core


PLANE = [(x, y, core) for x in range(2) for y in range(2) for core in range(2)]
EVERY = [(z, *p) for z in range(4) for p in PLANE]


def along_z(value, pairs):
    return lax.ppermute(
        value, AXES, [(device(a, *p), device(b, *p)) for a, b in pairs for p in PLANE]
    )


def first_way(value):
    return lax.ppermute(
        value, AXES,
        [(device(z, x, y, c), device(z, x ^ (1 - c), y ^ c, c)) for z, x, y, c in EVERY],
    )


def second_way(value, planes=(0, 1, 2, 3)):
    return lax.ppermute(
        value, AXES,
        [
            (device(z, x, y, c), device(z, x ^ c, y ^ (1 - c), c))
            for z, x, y, c in EVERY
            if z in planes
        ],
    )


def sibling(value):
    return lax.ppermute(
        value, AXES, [(device(z, x, y, c), device(z, x, y, 1 - c)) for z, x, y, c in EVERY]
    )


def collect(frozen, bq, bv):
    me = lax.axis_index(AXES)
    z, core = me // 8, me % 2
    chip = me // 2
    share = WEIGHT_ROWS // 32
    extra = frozen.shape[0] - share * WIDTH
    spill = extra * 32
    padded = -(-frozen.shape[0] // 1024) * 1024
    own = jnp.pad(frozen, (0, padded - frozen.shape[0])).reshape(padded // LANES, LANES)
    first = spill - extra * me
    start, turn = first // LANES, first % LANES

    plane = chip % 4
    one, two = jnp.where(core == 0, 2, 1), jnp.where(core == 0, 1, 2)
    mine_at = jnp.stack([plane, plane ^ one, plane ^ two, plane ^ 3]) * 2 + core
    other_at = jnp.stack([plane, plane ^ two, plane ^ one, plane ^ 3]) * 2 + 1 - core
    at = jnp.concatenate([mine_at, other_at]).astype(jnp.int32)
    flag = z[None].astype(jnp.int32)
    table = jnp.concatenate([at, flag])
    level = jnp.maximum(z, 1)
    level_a = jnp.where(z == 2, 3, 2)
    level_b = jnp.where(z < 2, 3, 1)
    codes = jnp.stack([at + 8 * (level_a - 1), at + 8 * (level_b - 1)], axis=1).reshape(-1)
    rest_table = jnp.concatenate([at + 8 * (level - 1), codes, flag]).astype(jnp.int32)

    last_rows = frozen[-spill:]
    before = lax.ppermute(last_rows, AXES, [(d, (d + 1) % 32) for d in range(32)])
    for_two = lax.ppermute(last_rows, AXES, [(31, device(2, 0, 0, 0))])
    tail = tail_rows(jnp.where(z == 0, before, for_two))

    mine, padded = window(start, turn, before.reshape(spill // LANES, LANES), own, share)
    mine, padded, tail, table, rest_table, bq, bv = lax.optimization_barrier(
        (mine, padded, tail, table, rest_table, bq, bv)
    )
    up_two = along_z(padded, [(0, 2)])
    near = [mine, first_way(mine), second_way(mine)]
    down_one = along_z(mine, [(1, 0), (2, 1), (3, 2)])
    up = jnp.concatenate([jnp.where(z == 0, mine, up_two[:share]), tail])
    up_one = along_z(up, [(0, 1), (2, 3)])
    up_one, down_one, *near = lax.optimization_barrier((up_one, down_one, *near))

    far = [
        jnp.where(z == 0, jnp.concatenate([down_one, tail]), jnp.where(z == 2, up, up_one))
    ]
    far += [first_way(far[0]), second_way(far[0])]
    near_last = second_way(near[1], (0,))
    near_other = [sibling(v) for v in near]
    down_two = along_z(down_one, [(1, 0), (2, 1)])
    below = along_z(near[0], [(1, 2), (2, 3)])
    far.append(second_way(far[1]))
    far_other = [sibling(v) for v in far[:3]]
    far[3], near_last, down_two, below, near[1] = lax.optimization_barrier(
        (far[3], near_last, down_two, below, near[1])
    )
    far_other.append(sibling(far[3]))
    projections = [*near, near_last, *near_other, sibling(near_last), *far, *far_other]
    projections = list(lax.optimization_barrier(projections))
    far = projections[8:]
    rest_near = second_way(near[1], (1, 2, 3))
    rest_near = [*near, rest_near, *near_other, sibling(rest_near)]
    around = along_z(jnp.where(z == 1, down_two, below), [(1, 0), (2, 3)])

    def last(*others):
        end = after(around, *others)
        value = jnp.stack(
            [
                jnp.where(z == 0, down_two, jnp.where(z == 3, below, down_one)),
                jnp.where(z == 1, down_two, jnp.where(z == 2, below, end)),
            ]
        )
        one = first_way(value)
        return [value, one, second_way(value)]

    return table, projections, rest_table, rest_near + far, last, bq, bv


def other_planes(value, flip):
    return lax.ppermute(
        value, AXES, [(device(z, *p), device(z ^ flip, *p)) for z, *p in EVERY]
    )


def other_chips(value, flip_x, flip_y):
    return lax.ppermute(
        value, AXES,
        [(device(z, x, y, c), device(z, x ^ flip_x, y ^ flip_y, c)) for z, x, y, c in EVERY],
    )


def plane_total(value):
    value = value + sibling(value)
    along = value + other_chips(value, 1, 0)
    across = other_chips(value, 0, 1) + other_chips(value, 1, 1)
    return along + across


def planes_total(value):
    return (value + other_planes(value, 1)) + (other_planes(value, 2) + other_planes(value, 3))


def local(
    tokens,
    bucket_item_counts,
    slot_item_lengths,
    frozen,
    query_lowrank_matrix,
    value_lowrank_matrix,
    output_gradient,
    evaluation_tokens,
    evaluation_lengths,
    *,
    mesh,
):
    devices = mesh.shape["fsdp"] * mesh.shape["rep"]
    special = tuple(mesh.shape[axis] for axis in AXES) == (8, 4)
    bq = query_lowrank_matrix.astype(bf16)
    bv = value_lowrank_matrix.astype(bf16)
    if special:
        table, w, rest_table, rest, last_of, bq, bv = collect(frozen, bq, bv)
    else:
        table, w, rest_table, rest = collect_generic(frozen, devices)
    counts, lengths = bucket_item_counts, slot_item_lengths
    blocks = evaluation_tokens.shape[0] // BUCKET

    ctx, q, k, v, tail = train_attention(counts, lengths, table, tokens, bq, bv, w)
    x = evaluation_tokens
    if special:
        last = last_of(ctx)
        x = after(x, ctx)
    most = blocks - 1
    first_ctx = eval_attention(evaluation_lengths, table, x, tail, bq, bv, w, 0, most)
    if special:
        last = list(lax.optimization_barrier((*last, first_ctx))[:3])
        x = after(x, *last)
        last.append(second_way(last[1]))
        other = [sibling(v) for v in last[:3]]
    last_ctx = eval_attention(evaluation_lengths, table, x, tail, bq, bv, w, most, blocks - most)
    eval_ctx = [first_ctx, last_ctx]
    if special:
        last[3] = after(last[3], last_ctx)
        rest = rest + last + other + [sibling(last[3])]
    grad = after(output_gradient, *eval_ctx)
    out, token_gradient, sums, w_rest = train_rest(
        counts, lengths, table, rest_table, tokens, q, k, v, ctx, grad, tail, bq, bv, w, rest
    )
    eval_in = [after(c, sums) for c in eval_ctx]
    eval_out = eval_tail(evaluation_tokens, eval_in[0], tail, w_rest, 0)
    second = eval_in[1]
    if special:
        sums = plane_total(sums)
        second = after(second, sums, eval_out)
    eval_out = eval_tail(evaluation_tokens, second, tail, w_rest, most, eval_out)
    sums = planes_total(sums) if special else lax.psum(sums, AXES)
    gq, gv = sums[:RANK], sums[RANK:]
    return out, token_gradient, gq, gv, eval_out


def solution(mesh):
    split = P(("fsdp", "rep"), None)
    flat = P(("fsdp", "rep"))
    return jax.shard_map(
        functools.partial(local, mesh=mesh),
        mesh=mesh,
        in_specs=(split, split, split, flat, P(), P(), split, split, flat),
        out_specs=(split, split, P(), P(), split),
        check_vma=False,
    )
```

```python
import functools

import jax
import jax.numpy as jnp
from jax import lax
from jax.experimental import pallas as pl
from jax.experimental.pallas import tpu as pltpu
from jax.sharding import PartitionSpec as P

WIDTH = 768
HEADS = 12
HEAD_DIM = 64
SLABS = 4
BUCKET = 512
CHUNK = 256
PAIR = 2 * HEAD_DIM
PAIRS = HEADS // 2
WEIGHT_ROWS = WIDTH * (4 + 2 * SLABS)
QKV_ROWS = 3 * WIDTH
VECTOR_ROWS = 12
RANK = 8
FORBIDDEN = -1e30
EPS = 1e-5
VMEM = 60 * 2**20
REST_ROWS = WEIGHT_ROWS - QKV_ROWS
UP_AT = WIDTH
DOWN_AT = WIDTH * (1 + SLABS)
TAIL_ROWS = 32
PAD_ROWS = 16
GROUPS = ((0,), (1, 5), (2, 6), (3, 7, 4, 8))
A_AT = 16
LANES = 128

f32 = jnp.float32
bf16 = jnp.bfloat16

BQ, BV, BO, B1, B2, G1, C1, G2, C2 = 0, 1, 2, 3, 7, 8, 9, 10, 11


def dot(left, right):
    return jnp.dot(left, right, preferred_element_type=f32)


def dot_last(left, right):
    return lax.dot_general(left, right, (((1,), (1,)), ((), ())), preferred_element_type=f32)


def dot_first(left, right):
    return lax.dot_general(left, right, (((0,), (0,)), ((), ())), preferred_element_type=f32)


def row(tail_ref, at):
    return tail_ref[:A_AT].astype(f32)[at : at + 1]


def adapter(tail_ref, which):
    return tail_ref[A_AT:].astype(f32)[RANK * which : RANK * (which + 1)].astype(bf16)


def normalise(resid):
    centred = resid - jnp.mean(resid, axis=-1, keepdims=True)
    scale = lax.rsqrt(jnp.mean(centred * centred, axis=-1, keepdims=True) + EPS)
    return centred * scale, scale


def normalise_back(grad, normed, scale):
    return scale * (
        grad
        - jnp.mean(grad, axis=-1, keepdims=True)
        - normed * jnp.mean(grad * normed, axis=-1, keepdims=True)
    )


def half_error_function(value):
    return 0.5 + 0.5 * lax.erf(value * 0.7071067811865476)


def gelu(value):
    return value * half_error_function(value)


def gelu_slope(value):
    density = jnp.exp(value * value * -0.5) * 0.3989422804014327
    return half_error_function(value) + value * density


def low_lanes(rows):
    return lax.broadcasted_iota(jnp.int32, (rows, PAIR), 1) < HEAD_DIM


def head_stack(pair):
    low = low_lanes(pair.shape[0])
    zero = jnp.zeros_like(pair)
    return jnp.concatenate([jnp.where(low, pair, zero), jnp.where(low, zero, pair)], axis=0)


def item_masks(counts_ref, lengths_ref):
    position = lax.broadcasted_iota(jnp.int32, (BUCKET, 128), 0)
    column = lax.broadcasted_iota(jnp.int32, (BUCKET, 128), 1)
    start = jnp.zeros((BUCKET, 128), jnp.int32)
    finish = jnp.zeros((BUCKET, 128), jnp.int32)
    valid = jnp.zeros((BUCKET, 128), jnp.int32)
    base = jnp.int32(0)
    first = jnp.int32(0)
    for level in range(counts_ref.shape[1]):
        extent = BUCKET >> level
        count = counts_ref[0, level]
        inside = (column >= first) & (column < first + count)
        here = base + (column - first) * extent
        start = jnp.where(inside, here, start)
        finish = jnp.where(inside, here + extent, finish)
        base = base + count * extent
        first = first + count
    for slot in range(lengths_ref.shape[1]):
        valid = jnp.where(column == slot, lengths_ref[0, slot], valid)
    member = (position >= start) & (position < finish)
    allowed = member & (position < start + valid)
    return (
        jnp.where(member, 1.0, 0.0).astype(bf16),
        jnp.where(allowed, 0.0, FORBIDDEN).astype(bf16),
    )


def attend(q_s, k_s, v_s, query_mask, key_mask, put):
    rows = q_s.shape[0]
    ones = jnp.ones((rows, 128), bf16)
    masks = jnp.concatenate([query_mask, query_mask], axis=0)
    low = low_lanes(rows)

    def scores_of(pair):
        at = slice(PAIR * pair, PAIR * (pair + 1))
        left = jnp.concatenate([head_stack(q_s[:, at]), masks], axis=1)
        return dot_last(left, jnp.concatenate([k_s[:, at], key_mask], axis=1))

    scores = scores_of(0)
    for pair in range(PAIRS):
        later = scores_of(pair + 1) if pair + 1 < PAIRS else None
        at = slice(PAIR * pair, PAIR * (pair + 1))
        top = jnp.max(scores, axis=-1, keepdims=True)
        weights = jnp.exp(scores - top).astype(bf16)
        mixed = dot(weights, jnp.concatenate([v_s[:, at], ones], axis=1))
        mixed = mixed[:, :PAIR] / mixed[:, PAIR:]
        put(at, jnp.where(low, mixed[:rows], mixed[rows:]).astype(bf16))
        scores = later


def start_qkv(table_ref, refs, w, sem, tail=None, tail_sem=None):
    if len(refs) == 2:
        pltpu.make_async_copy(refs[0], w, sem).start()
        if tail is not None:
            pltpu.make_async_copy(refs[1], tail, tail_sem).start()
        return
    units = len(refs) // 2
    size = refs[0].shape[0]

    def start(chosen):
        for i, ref in enumerate(chosen):
            to = pl.multiple_of(table_ref[i] * size, 16)
            pltpu.make_async_copy(ref.at[pl.ds(0, size)], w.at[pl.ds(to, size)], sem).start()

    if tail is not None:
        for i, ref in enumerate(refs[units:]):

            @pl.when(table_ref[i] == 0)
            def _():
                rows = ref.at[pl.ds(size, TAIL_ROWS)]
                pltpu.make_async_copy(rows, tail, tail_sem).start()

    @pl.when(table_ref[units] == 0)
    def _():
        start(refs[:units])

    @pl.when(table_ref[units] != 0)
    def _():
        start(refs[units:])


def wait_all(ref, sem):
    pltpu.make_async_copy(ref, ref, sem).wait()


def start_rest(table_ref, refs, w, sems):
    units = len(refs) // 3
    size = refs[-1].shape[1] if units else w.shape[0]

    def start(ref, at):
        to = pl.multiple_of(at * size, 16)
        pltpu.make_async_copy(ref, w.at[pl.ds(to, size)], sems.at[at]).start()

    if units:

        @pl.when(table_ref[3 * units] == 0)
        def _():
            for i in range(units):
                start(refs[units + i].at[pl.ds(0, size)], table_ref[i])

        @pl.when(table_ref[3 * units] != 0)
        def _():
            for i in range(units):
                start(refs[i].at[pl.ds(0, size)], table_ref[i])

        for i in range(units):
            for slot in range(2):
                start(refs[2 * units + i].at[slot], table_ref[units + 2 * i + slot])
    else:
        start(refs[0], 0)

    waiting = set(range(w.shape[0] // size))

    def ready(first, last):
        for at in range(first // size, (last - 1) // size + 1):
            if at in waiting:
                waiting.remove(at)
                wait_all(w.at[pl.ds(at * size, size)], sems.at[at])

    return ready


def slabs_of_columns(w, lanes):
    rows = slice(UP_AT, DOWN_AT)
    for at in range(0, WIDTH, LANES):
        lanes[...] = w[rows, at : at + LANES].astype(f32)
        for slab in range(SLABS):
            to = UP_AT + WIDTH * slab
            part = lanes[pl.ds(slab, WIDTH, stride=SLABS), :]
            w[to : to + WIDTH, at : at + LANES] = part.astype(bf16)


def merge(w, tail_ref, b_ref, which):
    rows = slice(2 * WIDTH * which, 2 * WIDTH * which + WIDTH)
    merged = w[rows].astype(f32) + 2.0 * dot_first(adapter(tail_ref, which), b_ref[...])
    w[rows] = merged.astype(bf16)


def train_attention_kernel(
    counts_ref, lengths_ref, table_ref, x_ref, bq_ref, bv_ref, *refs
):
    *w_refs, ctx_ref, q_ref, k_ref, v_ref, tail_ref, merged_any, w, sems = refs
    start_qkv(table_ref, w_refs, w, sems.at[0], tail_ref, sems.at[1])
    query_mask, key_mask = item_masks(counts_ref, lengths_ref)
    x = x_ref[...]
    wait_all(tail_ref, sems.at[1])
    aq = dot_last(x, adapter(tail_ref, 0)).astype(bf16)
    av = dot_last(x, adapter(tail_ref, 1)).astype(bf16)
    wait_all(w, sems.at[0])
    q = dot(x, w[:WIDTH]) + row(tail_ref, BQ) + 2.0 * dot(aq, bq_ref[...])
    q_ref[...] = (q.astype(bf16).astype(f32) * HEAD_DIM**-0.5).astype(bf16)
    k_ref[...] = dot(x, w[WIDTH : 2 * WIDTH]).astype(bf16)
    v = dot(x, w[2 * WIDTH :]) + row(tail_ref, BV) + 2.0 * dot(av, bv_ref[...])
    v_ref[...] = v.astype(bf16)
    merge(w, tail_ref, bq_ref, 0)
    merge(w, tail_ref, bv_ref, 1)
    hand_on = pltpu.make_async_copy(w, merged_any, sems.at[0])
    hand_on.start()

    def put(at, value):
        ctx_ref[:, at] = value

    attend(q_ref, k_ref, v_ref, query_mask, key_mask, put)
    hand_on.wait()


def eval_attention_kernel(lengths_ref, x_ref, tail_ref, w_any, ctx_ref, w, q_s, k_s, v_s, sems, *, first):
    step = pl.program_id(0)
    x = x_ref[...]

    def project(ready):
        ready(0)
        q = dot(x, w[:WIDTH]) + row(tail_ref, BQ)
        q_s[...] = (q.astype(bf16).astype(f32) * HEAD_DIM**-0.5).astype(bf16)
        ready(1)
        k_s[...] = dot(x, w[WIDTH : 2 * WIDTH]).astype(bf16)
        ready(2)
        v_s[...] = (dot(x, w[2 * WIDTH :]) + row(tail_ref, BV)).astype(bf16)

    @pl.when(step == 0)
    def _():
        rows = [pl.ds(WIDTH * i, WIDTH) for i in range(3)]
        copies = [pltpu.make_async_copy(w_any.at[r], w.at[r], sems.at[i]) for i, r in enumerate(rows)]
        for copy in copies:
            copy.start()
        project(lambda i: copies[i].wait())

    @pl.when(step != 0)
    def _():
        project(lambda i: None)

    position = lax.broadcasted_iota(jnp.int32, (BUCKET, LANES), 0)
    column = lax.broadcasted_iota(jnp.int32, (BUCKET, LANES), 1)
    length = lengths_ref[first + step]
    key_mask = jnp.where((column > 0) | (position < length), 0.0, FORBIDDEN).astype(bf16)
    query_mask = jnp.where(column == 0, 1.0, 0.0).astype(bf16)

    def put(at, value):
        ctx_ref[:, at] = value

    attend(q_s, k_s, v_s, query_mask, key_mask, put)


def up_weight(w, slab, at):
    return w[UP_AT + WIDTH * slab : UP_AT + WIDTH * (slab + 1), at : at + CHUNK]


def down_weight(w, slab, at):
    rows = DOWN_AT + WIDTH * slab + at
    return w[rows : rows + CHUNK]


def feed_forward(h1, tail_ref, w, ready, keep):
    chunks = [(slab, at) for slab in range(SLABS) for at in range(0, WIDTH, CHUNK)]

    def up(slab, at):
        if at == 0:
            ready(UP_AT + WIDTH * slab, UP_AT + WIDTH * (slab + 1))
        u = dot(h1, up_weight(w, slab, at)) + row(tail_ref, B1 + slab)[:, at : at + CHUNK]
        keep(slab, at, u)
        return u

    total = None
    u = up(*chunks[0])
    for i, (slab, at) in enumerate(chunks):
        later = up(*chunks[i + 1]) if i + 1 < len(chunks) else None
        if at == 0:
            ready(DOWN_AT + WIDTH * slab, DOWN_AT + WIDTH * (slab + 1))
        part = dot(gelu(u).astype(bf16), down_weight(w, slab, at))
        total = part if total is None else total + part
        u = later
    return total


def eval_tail_kernel(x_ref, ctx_ref, tail_ref, w_any, *refs):
    out_ref, w, sems = refs[-3:]

    def run(ready):
        ready(0, WIDTH)
        resid = x_ref[...].astype(f32) + (dot(ctx_ref[...], w[:WIDTH]) + row(tail_ref, BO))
        normed, _ = normalise(resid)
        h1 = (normed * row(tail_ref, G1) + row(tail_ref, C1)).astype(bf16)
        down = feed_forward(h1, tail_ref, w, ready, lambda slab, at, u: None)
        normed, _ = normalise(h1.astype(f32) + (down + row(tail_ref, B2)))
        out_ref[...] = (normed * row(tail_ref, G2) + row(tail_ref, C2)).astype(bf16)

    @pl.when(pl.program_id(0) == 0)
    def _():
        copies = {}
        for group in GROUPS:
            for part in group:
                rows = pl.ds(WIDTH * part, WIDTH)
                copies[part] = pltpu.make_async_copy(w_any.at[rows], w.at[rows], sems.at[part])
                copies[part].start()

        def ready(first, last):
            for group in GROUPS:
                if first // WIDTH in group and first // WIDTH in copies:
                    for part in group:
                        copies.pop(part).wait()

        run(ready)

    @pl.when(pl.program_id(0) != 0)
    def _():
        run(lambda first, last: None)


def attention_back(q_ref, k_ref, v_ref, dctx, masks, dq_s, dk_s, dv_s):
    query_mask, key_mask = masks
    rows = q_ref.shape[0]
    masks = jnp.concatenate([query_mask, query_mask], axis=0)

    def products(pair):
        at = slice(PAIR * pair, PAIR * (pair + 1))
        q2, k, d2 = head_stack(q_ref[:, at]), k_ref[:, at], head_stack(dctx[:, at])
        scores = dot_last(
            jnp.concatenate([k, key_mask], axis=1), jnp.concatenate([q2, masks], axis=1)
        )
        return scores, dot_last(v_ref[:, at], d2), q2, k, d2

    now = products(0)
    for pair in range(PAIRS):
        later = products(pair + 1) if pair + 1 < PAIRS else None
        scores, grad_probs, q2, k, d2 = now
        at = slice(PAIR * pair, PAIR * (pair + 1))
        probs = jnp.exp(scores - jnp.max(scores, axis=0, keepdims=True))
        probs = probs * (1.0 / jnp.sum(probs, axis=0, keepdims=True))
        dv_s[:, at] = dot(probs.astype(bf16), d2).astype(bf16)
        inner = jnp.sum(probs * grad_probs, axis=0, keepdims=True)
        grad_scores = (probs * (grad_probs - inner)).astype(bf16)
        dk_s[:, at] = dot(grad_scores, q2).astype(bf16)
        crossed = dot_first(k, grad_scores)
        dq = jnp.concatenate([crossed[:HEAD_DIM, :rows], crossed[HEAD_DIM:, rows:]], axis=0)
        dq_s[:, at] = (dq.T * HEAD_DIM**-0.5).astype(bf16)
        now = later


def train_kernel(
    counts_ref, lengths_ref, table_ref, rest_table_ref, x_ref, q_ref, k_ref, v_ref, ctx_ref, grad_ref,
    tail_ref, bq_ref, bv_ref, *refs, n_qkv,
):
    *w_refs, out_ref, token_ref, sums_ref, w_any, wqkv, w, lanes, u_s, dq_s, dk_s, dv_s, sems = refs
    rest_refs = w_refs[n_qkv:]
    ready = start_rest(rest_table_ref, rest_refs, w, sems.at[pl.ds(2, 24)])
    start_qkv(table_ref, w_refs[:n_qkv], wqkv, sems.at[0])
    x = x_ref[...]
    aq = dot_last(x, adapter(tail_ref, 0)).astype(bf16)
    av = dot_last(x, adapter(tail_ref, 1)).astype(bf16)

    ready(0, WIDTH)
    resid = x.astype(f32) + (dot(ctx_ref[...], w[:WIDTH]) + row(tail_ref, BO))
    normed_one, scale_one = normalise(resid)
    h1 = (normed_one * row(tail_ref, G1) + row(tail_ref, C1)).astype(bf16)

    def keep(slab, at, u):
        u_s[slab, :, at : at + CHUNK] = u

    ready(UP_AT, DOWN_AT)
    if len(rest_refs) > 1:
        slabs_of_columns(w, lanes)
    ready(DOWN_AT, REST_ROWS)
    down = feed_forward(h1, tail_ref, w, ready, keep)
    keep_rest = pltpu.make_async_copy(w, w_any, sems.at[1])
    keep_rest.start()
    normed_two, scale_two = normalise(h1.astype(f32) + (down + row(tail_ref, B2)))
    out_ref[...] = (normed_two * row(tail_ref, G2) + row(tail_ref, C2)).astype(bf16)

    grad_two = normalise_back(grad_ref[...].astype(f32) * row(tail_ref, G2), normed_two, scale_two)
    df = grad_two.astype(bf16)
    total = None
    for slab in range(SLABS):
        for at in range(0, WIDTH, CHUNK):
            grad_gelu = dot_last(df, down_weight(w, slab, at))
            du = (grad_gelu * gelu_slope(u_s[slab, :, at : at + CHUNK])).astype(bf16)
            part = dot_last(du, up_weight(w, slab, at))
            total = part if total is None else total + part
    dh1 = (grad_two + total).astype(bf16)
    grad_one = normalise_back(dh1.astype(f32) * row(tail_ref, G1), normed_one, scale_one)
    token_ref[...] = grad_one
    dctx = dot_last(grad_one.astype(bf16), w[:WIDTH]).astype(bf16)
    attention_back(q_ref, k_ref, v_ref, dctx, item_masks(counts_ref, lengths_ref), dq_s, dk_s, dv_s)

    wait_all(wqkv, sems.at[0])
    dq, dk, dv = dq_s[...], dk_s[...], dv_s[...]
    daq = (2.0 * dot_last(dq, bq_ref[...])).astype(bf16)
    dav = (2.0 * dot_last(dv, bv_ref[...])).astype(bf16)
    sums_ref[:RANK] = 2.0 * dot_first(aq, dq)
    sums_ref[RANK:] = 2.0 * dot_first(av, dv)
    token_ref[...] += (
        dot_last(dq, wqkv[:WIDTH])
        + dot_last(dk, wqkv[WIDTH : 2 * WIDTH])
        + dot_last(dv, wqkv[2 * WIDTH :])
        + dot(daq, adapter(tail_ref, 0))
        + dot(dav, adapter(tail_ref, 1))
    )
    keep_rest.wait()


def window_kernel(place_ref, before_ref, own_ref, out_ref, padded_ref, flat, moved):
    ahead = before_ref.shape[0]
    flat[:ahead] = before_ref[...].astype(f32)
    flat[ahead : ahead + own_ref.shape[0]] = own_ref[...].astype(f32)
    flat[ahead + own_ref.shape[0] :] = jnp.zeros((LANES, LANES), f32)
    rows = moved.shape[0]
    start, turn = place_ref[0], place_ref[1]
    back = lax.rem(LANES - turn, LANES)
    here = pltpu.roll(flat[pl.ds(start, rows), :], back, 1)
    after = pltpu.roll(flat[pl.ds(start + 1, rows), :], back, 1)
    lane = lax.broadcasted_iota(jnp.int32, (rows, LANES), 1)
    moved[...] = jnp.where(lane < LANES - turn, here, after)
    per_row = WIDTH // LANES
    for tile in range(per_row):
        part = moved[pl.ds(tile, rows // per_row, stride=per_row), :]
        at = slice(LANES * tile, LANES * (tile + 1))
        out_ref[:, at] = part.astype(bf16)
        padded_ref[: rows // per_row, at] = part.astype(bf16)
    padded_ref[rows // per_row :] = jnp.zeros((PAD_ROWS, WIDTH), bf16)


def whole(shape):
    return pl.BlockSpec(shape, lambda *_: (0,) * len(shape))


def cost(microseconds):
    return pl.CostEstimate(flops=int(microseconds * 1e9), bytes_accessed=0, transcendentals=0)


def after(value, *others):
    return lax.optimization_barrier((value, *others))[0]


ANY = pl.BlockSpec(memory_space=pl.ANY)
SCALARS = pl.BlockSpec(memory_space=pltpu.SMEM)
PARAMS = pltpu.CompilerParams(vmem_limit_bytes=VMEM)


QKV_SCRATCH = pltpu.VMEM((QKV_ROWS, WIDTH), bf16)
REST_SCRATCH = pltpu.VMEM((REST_ROWS, WIDTH), bf16)


def train_attention(counts, lengths, table, x, bq, bv, w):
    rows = x.shape[0]
    shape = (rows, WIDTH)
    return pl.pallas_call(
        train_attention_kernel,
        in_specs=[SCALARS] * 3
        + [whole(v.shape) for v in (x, bq, bv)]
        + [ANY] * len(w),
        out_specs=[whole(shape)] * 4 + [whole((TAIL_ROWS, WIDTH)), ANY],
        out_shape=[jax.ShapeDtypeStruct(shape, bf16)] * 4
        + [jax.ShapeDtypeStruct((n, WIDTH), bf16) for n in (TAIL_ROWS, QKV_ROWS)],
        grid=(1,),
        scratch_shapes=[QKV_SCRATCH, pltpu.SemaphoreType.DMA((2,))],
        compiler_params=PARAMS,
        cost_estimate=cost(11),
        name="train_attention",
    )(counts, lengths, table, x, bq, bv, *w)


def eval_attention(lengths, x, tail, w, first, count):
    return pl.pallas_call(
        functools.partial(eval_attention_kernel, first=first),
        in_specs=[
            SCALARS,
            pl.BlockSpec((BUCKET, WIDTH), lambda i: (i + first, 0)),
            whole(tail.shape),
            ANY,
        ],
        out_specs=pl.BlockSpec((BUCKET, WIDTH), lambda i: (i, 0)),
        out_shape=jax.ShapeDtypeStruct((count * BUCKET, WIDTH), bf16),
        grid=(count,),
        scratch_shapes=[QKV_SCRATCH]
        + [pltpu.VMEM((BUCKET, WIDTH), bf16)] * 3
        + [pltpu.SemaphoreType.DMA((3,))],
        compiler_params=PARAMS,
        cost_estimate=cost(1 + 7 * count),
        name="eval_attention",
    )(lengths, x, tail, w)


def eval_tail(x, ctx, tail, w, first, done=None):
    rows = ctx.shape[0]
    given = [] if done is None else [done]
    return pl.pallas_call(
        eval_tail_kernel,
        in_specs=[
            pl.BlockSpec((BUCKET, WIDTH), lambda i: (i + first, 0)),
            pl.BlockSpec((BUCKET, WIDTH), lambda i: (i, 0)),
            whole(tail.shape),
            ANY,
        ]
        + [ANY] * len(given),
        out_specs=pl.BlockSpec((BUCKET, WIDTH), lambda i: (i + first, 0)),
        out_shape=jax.ShapeDtypeStruct(x.shape, bf16),
        grid=(rows // BUCKET,),
        scratch_shapes=[REST_SCRATCH, pltpu.SemaphoreType.DMA((1 + 2 * SLABS,))],
        input_output_aliases={4: 0} if given else {},
        compiler_params=PARAMS,
        cost_estimate=cost(3 + 8 * (rows // BUCKET)),
        name="eval_tail",
    )(x, ctx, tail, w, *given)


def train_rest(counts, lengths, table, rest_table, x, q, k, v, ctx, grad, tail, bq, bv, w, rest):
    rows = x.shape[0]
    shape = (rows, WIDTH)
    return pl.pallas_call(
        functools.partial(train_kernel, n_qkv=len(w)),
        in_specs=[SCALARS] * 4
        + [whole(shape)] * 6
        + [whole(v.shape) for v in (tail, bq, bv)]
        + [ANY] * (len(w) + len(rest)),
        out_specs=[whole(shape), whole(shape), whole((2 * RANK, WIDTH)), ANY],
        out_shape=[
            jax.ShapeDtypeStruct(shape, bf16),
            jax.ShapeDtypeStruct(shape, f32),
            jax.ShapeDtypeStruct((2 * RANK, WIDTH), f32),
            jax.ShapeDtypeStruct((REST_ROWS, WIDTH), bf16),
        ],
        grid=(1,),
        scratch_shapes=[
            QKV_SCRATCH,
            REST_SCRATCH,
            pltpu.VMEM((SLABS * WIDTH, LANES), f32),
            pltpu.VMEM((SLABS, rows, WIDTH), f32),
            pltpu.VMEM(shape, bf16),
            pltpu.VMEM(shape, bf16),
            pltpu.VMEM(shape, bf16),
            pltpu.SemaphoreType.DMA((26,)),
        ],
        compiler_params=PARAMS,
        cost_estimate=cost(36),
        name="train_rest",
    )(counts, lengths, table, rest_table, x, q, k, v, ctx, grad, tail, bq, bv, *w, *rest)


def window(start, turn, before, own, rows):
    ahead = before.shape[0]
    place = jnp.stack([start, turn]).astype(jnp.int32)
    return pl.pallas_call(
        window_kernel,
        in_specs=[SCALARS, whole(before.shape), whole(own.shape)],
        out_specs=[whole((rows, WIDTH)), whole((rows + PAD_ROWS, WIDTH))],
        out_shape=[
            jax.ShapeDtypeStruct((rows, WIDTH), bf16),
            jax.ShapeDtypeStruct((rows + PAD_ROWS, WIDTH), bf16),
        ],
        grid=(1,),
        scratch_shapes=[
            pltpu.VMEM((ahead + own.shape[0] + LANES, LANES), f32),
            pltpu.VMEM((rows * (WIDTH // LANES), LANES), f32),
        ],
        compiler_params=PARAMS,
        cost_estimate=cost(2),
        name="window",
    )(place, before, own)


AXES = ("fsdp", "rep")


def tail_rows(flat):
    at = VECTOR_ROWS * WIDTH
    vectors = jnp.pad(flat[:at].reshape(VECTOR_ROWS, WIDTH), ((0, A_AT - VECTOR_ROWS), (0, 0)))
    a = flat[at:].reshape(2, WIDTH, RANK).transpose(0, 2, 1).reshape(2 * RANK, WIDTH)
    return jnp.concatenate([vectors, a])


def collect_generic(frozen, devices):
    me = lax.axis_index(AXES)
    share = WEIGHT_ROWS // devices
    extra = frozen.shape[0] - share * WIDTH
    spill = extra * devices
    before = lax.ppermute(frozen[-spill:], AXES, [(d, (d + 1) % devices) for d in range(devices)])
    flat = lax.dynamic_slice(
        jnp.concatenate([before, frozen]), (spill - extra * me,), (share * WIDTH,)
    )
    gathered = lax.all_gather(flat.reshape(share, WIDTH), AXES, axis=0, tiled=True)
    tail = lax.psum(jnp.where(me == devices - 1, frozen[-spill:].astype(f32), 0.0), AXES)
    w1 = gathered[QKV_ROWS + WIDTH : QKV_ROWS + WIDTH * (1 + SLABS)]
    w1 = w1.reshape(WIDTH, SLABS, WIDTH).transpose(1, 0, 2).reshape(WIDTH * SLABS, WIDTH)
    rest = jnp.concatenate(
        [gathered[QKV_ROWS : QKV_ROWS + WIDTH], w1, gathered[QKV_ROWS + WIDTH * (1 + SLABS) :]]
    )
    none = jnp.zeros((8,), jnp.int32)
    return none, [gathered[:QKV_ROWS], tail_rows(tail.astype(bf16))], none, [rest]


def device(z, x, y, core):
    return ((z * 2 + x) * 2 + y) * 2 + core


PLANE = [(x, y, core) for x in range(2) for y in range(2) for core in range(2)]
EVERY = [(z, *p) for z in range(4) for p in PLANE]


def along_z(value, pairs):
    return lax.ppermute(
        value, AXES, [(device(a, *p), device(b, *p)) for a, b in pairs for p in PLANE]
    )


def first_way(value):
    return lax.ppermute(
        value, AXES,
        [(device(z, x, y, c), device(z, x ^ (1 - c), y ^ c, c)) for z, x, y, c in EVERY],
    )


def second_way(value):
    return lax.ppermute(
        value, AXES,
        [(device(z, x, y, c), device(z, x ^ c, y ^ (1 - c), c)) for z, x, y, c in EVERY],
    )


def sibling(value):
    return lax.ppermute(
        value, AXES, [(device(z, x, y, c), device(z, x, y, 1 - c)) for z, x, y, c in EVERY]
    )


def collect(frozen, query_b, value_b):
    me = lax.axis_index(AXES)
    z, core = me // 8, me % 2
    chip = me // 2
    share = WEIGHT_ROWS // 32
    extra = frozen.shape[0] - share * WIDTH
    spill = extra * 32
    padded = -(-frozen.shape[0] // 1024) * 1024
    own = jnp.pad(frozen, (0, padded - frozen.shape[0])).reshape(padded // LANES, LANES)
    first = spill - extra * me
    start, turn = first // LANES, first % LANES

    plane = chip % 4
    one, two = jnp.where(core == 0, 2, 1), jnp.where(core == 0, 1, 2)
    mine_at = jnp.stack([plane, plane ^ one, plane ^ two, plane ^ 3]) * 2 + core
    other_at = jnp.stack([plane, plane ^ two, plane ^ one, plane ^ 3]) * 2 + 1 - core
    at = jnp.concatenate([mine_at, other_at]).astype(jnp.int32)
    flag = z[None].astype(jnp.int32)
    level = jnp.stack([jnp.maximum(z, 1), jnp.where(z == 2, 3, 2), jnp.where(z < 2, 3, 1)])
    level = level.astype(jnp.int32)

    last_rows = frozen[-spill:]
    before = lax.ppermute(last_rows, AXES, [(d, d + 1) for d in range(31)])
    mine, padded = window(start, turn, before.reshape(spill // LANES, LANES), own, share)

    last_rows, query_b, value_b, at, flag, level = lax.optimization_barrier(
        (last_rows, query_b, value_b, at, flag, level, mine)
    )[:-1]
    tail = tail_rows(
        lax.ppermute(last_rows, AXES, [(31, device(0, 0, 0, 0))])
        + lax.ppermute(last_rows, AXES, [(31, device(2, 0, 0, 0))])
    )
    bq, bv = query_b.astype(bf16), value_b.astype(bf16)
    table = jnp.concatenate([at, flag])
    codes = jnp.stack([at + 8 * (level[1] - 1), at + 8 * (level[2] - 1)], axis=1).reshape(-1)
    rest_table = jnp.concatenate([at + 8 * (level[0] - 1), codes, flag])

    up_two = along_z(padded, [(0, 2)])
    near = [mine, first_way(mine), second_way(mine)]
    down_one = along_z(mine, [(1, 0), (2, 1), (3, 2)])

    up = jnp.concatenate([jnp.where(z == 0, mine, up_two[:share]), tail])
    up_one = along_z(up, [(0, 1), (2, 3)])
    near[1], down_one = lax.optimization_barrier((near[1], down_one, up))[:2]
    near.append(second_way(near[1]))
    down_two = along_z(down_one, [(1, 0), (2, 1)])
    up_one, down_two, near[3] = lax.optimization_barrier((up_one, down_two, near[3]))

    far = [
        jnp.where(z == 0, jnp.concatenate([down_one, tail]), jnp.where(z == 2, up, up_one))
    ]
    far += [first_way(far[0]), second_way(far[0])]
    below = along_z(near[0], [(1, 2), (2, 3)])
    near_other = [sibling(v) for v in near]
    below, bq, bv, table, rest_table, *ready = lax.optimization_barrier(
        (below, bq, bv, table, rest_table, *far, *near_other)
    )
    far, near_other = ready[:3], ready[3:]

    far.append(second_way(far[1]))
    around = along_z(jnp.where(z == 1, down_two, below), [(1, 0), (2, 3)])
    far_other = [sibling(v) for v in far[:3]]
    far[3], *far_other = lax.optimization_barrier((far[3], *far_other))
    far_other.append(sibling(far[3]))
    projections = [*near, *near_other, *far, *far_other]

    def last(*others):
        end = after(around, *others)
        value = jnp.stack(
            [
                jnp.where(z == 0, down_two, jnp.where(z == 3, below, down_one)),
                jnp.where(z == 1, down_two, jnp.where(z == 2, below, end)),
            ]
        )
        one = first_way(value)
        return [value, one, second_way(value)]

    return table, projections, rest_table, last, bq, bv


def other_planes(value, flip):
    return lax.ppermute(
        value, AXES, [(device(z, *p), device(z ^ flip, *p)) for z, *p in EVERY]
    )


def other_chips(value, flip_x, flip_y):
    return lax.ppermute(
        value, AXES,
        [(device(z, x, y, c), device(z, x ^ flip_x, y ^ flip_y, c)) for z, x, y, c in EVERY],
    )


def plane_total(value):
    value = value + sibling(value)
    along = value + other_chips(value, 1, 0)
    across = other_chips(value, 0, 1) + other_chips(value, 1, 1)
    return along + across


def planes_total(value):
    return (value + other_planes(value, 1)) + (other_planes(value, 2) + other_planes(value, 3))


def local(
    tokens,
    bucket_item_counts,
    slot_item_lengths,
    frozen,
    query_lowrank_matrix,
    value_lowrank_matrix,
    output_gradient,
    evaluation_tokens,
    evaluation_lengths,
    *,
    mesh,
):
    devices = mesh.shape["fsdp"] * mesh.shape["rep"]
    special = tuple(mesh.shape[axis] for axis in AXES) == (8, 4)
    if special:
        table, w, rest_table, last_of, bq, bv = collect(
            frozen, query_lowrank_matrix, value_lowrank_matrix
        )
    else:
        table, w, rest_table, rest = collect_generic(frozen, devices)
        bq, bv = query_lowrank_matrix.astype(bf16), value_lowrank_matrix.astype(bf16)
    counts, lengths = bucket_item_counts, slot_item_lengths
    blocks = evaluation_tokens.shape[0] // BUCKET

    ctx, q, k, v, tail, merged = train_attention(counts, lengths, table, tokens, bq, bv, w)
    x = evaluation_tokens
    if special:
        last = last_of(ctx)
        x = after(x, ctx)
    most = blocks - 1
    first_ctx = eval_attention(evaluation_lengths, x, tail, merged, 0, most)
    if special:
        last = list(lax.optimization_barrier((*last, first_ctx))[:3])
        x = after(x, *last)
        last.append(second_way(last[1]))
        other = [sibling(v) for v in last[:3]]
    last_ctx = eval_attention(evaluation_lengths, x, tail, merged, most, blocks - most)
    eval_ctx = [first_ctx, last_ctx]
    if special:
        last[3] = after(last[3], last_ctx)
        rest = w + last + other + [sibling(last[3])]
    grad = after(output_gradient, *eval_ctx)
    out, token_gradient, sums, w_rest = train_rest(
        counts, lengths, table, rest_table, tokens, q, k, v, ctx, grad, tail, bq, bv, w, rest
    )
    eval_in = [after(c, sums) for c in eval_ctx]
    eval_out = eval_tail(evaluation_tokens, eval_in[0], tail, w_rest, 0)
    second = eval_in[1]
    if special:
        sums = plane_total(sums)
        second = after(second, sums, eval_out)
    eval_out = eval_tail(evaluation_tokens, second, tail, w_rest, most, eval_out)
    sums = planes_total(sums) if special else lax.psum(sums, AXES)
    gq, gv = sums[:RANK], sums[RANK:]
    return out, token_gradient, gq, gv, eval_out


def solution(mesh):
    split = P(("fsdp", "rep"), None)
    flat = P(("fsdp", "rep"))
    return jax.shard_map(
        functools.partial(local, mesh=mesh),
        mesh=mesh,
        in_specs=(split, split, split, flat, P(), P(), split, split, flat),
        out_specs=(split, split, P(), P(), split),
        check_vma=False,
    )
```

```python
import functools

import jax
import jax.numpy as jnp
from jax import lax
from jax.experimental import pallas as pl
from jax.experimental.pallas import tpu as pltpu
from jax.sharding import PartitionSpec as P

WIDTH = 768
HEADS = 12
HEAD_DIM = 64
SLABS = 4
BUCKET = 512
CHUNK = 256
PAIR = 2 * HEAD_DIM
PAIRS = HEADS // 2
WEIGHT_ROWS = WIDTH * (4 + 2 * SLABS)
QKV_ROWS = 3 * WIDTH
VECTOR_ROWS = 12
RANK = 8
FORBIDDEN = -1e30
EPS = 1e-5
TRAIN_ATTENTION_MIB = 28
EVAL_ATTENTION_MIB = 28
TRAIN_REST_MIB = 44
EVAL_TAIL_MIB = 60
WINDOW_MIB = 16
REST_ROWS = WEIGHT_ROWS - QKV_ROWS
UP_AT = WIDTH
DOWN_AT = WIDTH * (1 + SLABS)
TAIL_ROWS = 32
PAD_ROWS = 16
GROUPS = ((0,), (1, 5), (2, 6), (3, 7, 4, 8))
A_AT = 16
LANES = 128

f32 = jnp.float32
bf16 = jnp.bfloat16

BQ, BV, BO, B1, B2, G1, C1, G2, C2 = 0, 1, 2, 3, 7, 8, 9, 10, 11


def dot(left, right):
    return jnp.dot(left, right, preferred_element_type=f32)


def dot_last(left, right):
    return lax.dot_general(left, right, (((1,), (1,)), ((), ())), preferred_element_type=f32)


def dot_first(left, right):
    return lax.dot_general(left, right, (((0,), (0,)), ((), ())), preferred_element_type=f32)


def row(tail_ref, at):
    return tail_ref[:A_AT].astype(f32)[at : at + 1]


def adapter(tail_ref, which):
    return tail_ref[A_AT:].astype(f32)[RANK * which : RANK * (which + 1)].astype(bf16)


def normalise(resid):
    centred = resid - jnp.mean(resid, axis=-1, keepdims=True)
    scale = lax.rsqrt(jnp.mean(centred * centred, axis=-1, keepdims=True) + EPS)
    return centred * scale, scale


def normalise_back(grad, normed, scale):
    return scale * (
        grad
        - jnp.mean(grad, axis=-1, keepdims=True)
        - normed * jnp.mean(grad * normed, axis=-1, keepdims=True)
    )


def half_error_function(value):
    return 0.5 + 0.5 * lax.erf(value * 0.7071067811865476)


def gelu(value):
    return value * half_error_function(value)


def gelu_slope(value):
    density = jnp.exp(value * value * -0.5) * 0.3989422804014327
    return half_error_function(value) + value * density


def low_lanes(rows):
    return lax.broadcasted_iota(jnp.int32, (rows, PAIR), 1) < HEAD_DIM


def head_stack(pair):
    low = low_lanes(pair.shape[0])
    zero = jnp.zeros_like(pair)
    return jnp.concatenate([jnp.where(low, pair, zero), jnp.where(low, zero, pair)], axis=0)


def item_masks(counts_ref, lengths_ref):
    position = lax.broadcasted_iota(jnp.int32, (BUCKET, 128), 0)
    column = lax.broadcasted_iota(jnp.int32, (BUCKET, 128), 1)
    start = jnp.zeros((BUCKET, 128), jnp.int32)
    finish = jnp.zeros((BUCKET, 128), jnp.int32)
    valid = jnp.zeros((BUCKET, 128), jnp.int32)
    base = jnp.int32(0)
    first = jnp.int32(0)
    for level in range(counts_ref.shape[1]):
        extent = BUCKET >> level
        count = counts_ref[0, level]
        inside = (column >= first) & (column < first + count)
        here = base + (column - first) * extent
        start = jnp.where(inside, here, start)
        finish = jnp.where(inside, here + extent, finish)
        base = base + count * extent
        first = first + count
    for slot in range(lengths_ref.shape[1]):
        valid = jnp.where(column == slot, lengths_ref[0, slot], valid)
    member = (position >= start) & (position < finish)
    allowed = member & (position < start + valid)
    return (
        jnp.where(member, 1.0, 0.0).astype(bf16),
        jnp.where(allowed, 0.0, FORBIDDEN).astype(bf16),
    )


def attend(q_s, k_s, v_s, query_mask, key_mask, put):
    rows = q_s.shape[0]
    ones = jnp.ones((rows, 128), bf16)
    masks = jnp.concatenate([query_mask, query_mask], axis=0)
    low = low_lanes(rows)

    def scores_of(pair):
        at = slice(PAIR * pair, PAIR * (pair + 1))
        left = jnp.concatenate([head_stack(q_s[:, at]), masks], axis=1)
        return dot_last(left, jnp.concatenate([k_s[:, at], key_mask], axis=1))

    scores = scores_of(0)
    for pair in range(PAIRS):
        later = scores_of(pair + 1) if pair + 1 < PAIRS else None
        at = slice(PAIR * pair, PAIR * (pair + 1))
        top = jnp.max(scores, axis=-1, keepdims=True)
        weights = jnp.exp(scores - top).astype(bf16)
        mixed = dot(weights, jnp.concatenate([v_s[:, at], ones], axis=1))
        mixed = mixed[:, :PAIR] / mixed[:, PAIR:]
        put(at, jnp.where(low, mixed[:rows], mixed[rows:]).astype(bf16))
        scores = later


def start_qkv(table_ref, refs, w, sem, tail=None, tail_sem=None):
    if len(refs) == 2:
        pltpu.make_async_copy(refs[0], w, sem).start()
        if tail is not None:
            pltpu.make_async_copy(refs[1], tail, tail_sem).start()
        return
    units = len(refs) // 2
    size = refs[0].shape[0]

    def start(chosen):
        for i, ref in enumerate(chosen):
            to = pl.multiple_of(table_ref[i] * size, 16)
            pltpu.make_async_copy(ref.at[pl.ds(0, size)], w.at[pl.ds(to, size)], sem).start()

    if tail is not None:
        for i, ref in enumerate(refs[units:]):

            @pl.when(table_ref[i] == 0)
            def _():
                rows = ref.at[pl.ds(size, TAIL_ROWS)]
                pltpu.make_async_copy(rows, tail, tail_sem).start()

    @pl.when(table_ref[units] == 0)
    def _():
        start(refs[:units])

    @pl.when(table_ref[units] != 0)
    def _():
        start(refs[units:])


def wait_all(ref, sem):
    pltpu.make_async_copy(ref, ref, sem).wait()


def start_rest(table_ref, refs, w, sems):
    units = len(refs) // 3
    size = refs[-1].shape[1] if units else w.shape[0]

    def start(ref, at):
        to = pl.multiple_of(at * size, 16)
        pltpu.make_async_copy(ref, w.at[pl.ds(to, size)], sems.at[at]).start()

    if units:

        @pl.when(table_ref[3 * units] == 0)
        def _():
            for i in range(units):
                start(refs[units + i].at[pl.ds(0, size)], table_ref[i])

        @pl.when(table_ref[3 * units] != 0)
        def _():
            for i in range(units):
                start(refs[i].at[pl.ds(0, size)], table_ref[i])

        for i in range(units):
            for slot in range(2):
                start(refs[2 * units + i].at[slot], table_ref[units + 2 * i + slot])
    else:
        start(refs[0], 0)

    waiting = set(range(w.shape[0] // size))

    def ready(first, last):
        for at in range(first // size, (last - 1) // size + 1):
            if at in waiting:
                waiting.remove(at)
                wait_all(w.at[pl.ds(at * size, size)], sems.at[at])

    return ready


def slabs_of_columns(w, lanes):
    rows = slice(UP_AT, DOWN_AT)
    for at in range(0, WIDTH, LANES):
        lanes[...] = w[rows, at : at + LANES].astype(f32)
        for slab in range(SLABS):
            to = UP_AT + WIDTH * slab
            part = lanes[pl.ds(slab, WIDTH, stride=SLABS), :]
            w[to : to + WIDTH, at : at + LANES] = part.astype(bf16)


def merge(w, tail_ref, b_ref, which):
    rows = slice(2 * WIDTH * which, 2 * WIDTH * which + WIDTH)
    merged = w[rows].astype(f32) + 2.0 * dot_first(adapter(tail_ref, which), b_ref[...])
    w[rows] = merged.astype(bf16)


def train_attention_kernel(
    counts_ref, lengths_ref, table_ref, x_ref, bq_ref, bv_ref, *refs
):
    *w_refs, ctx_ref, q_ref, k_ref, v_ref, tail_ref, merged_any, w, sems = refs
    start_qkv(table_ref, w_refs, w, sems.at[0], tail_ref, sems.at[1])
    query_mask, key_mask = item_masks(counts_ref, lengths_ref)
    x = x_ref[...]
    wait_all(tail_ref, sems.at[1])
    aq = dot_last(x, adapter(tail_ref, 0)).astype(bf16)
    av = dot_last(x, adapter(tail_ref, 1)).astype(bf16)
    wait_all(w, sems.at[0])
    q = dot(x, w[:WIDTH]) + row(tail_ref, BQ) + 2.0 * dot(aq, bq_ref[...])
    q_ref[...] = (q.astype(bf16).astype(f32) * HEAD_DIM**-0.5).astype(bf16)
    k_ref[...] = dot(x, w[WIDTH : 2 * WIDTH]).astype(bf16)
    v = dot(x, w[2 * WIDTH :]) + row(tail_ref, BV) + 2.0 * dot(av, bv_ref[...])
    v_ref[...] = v.astype(bf16)
    merge(w, tail_ref, bq_ref, 0)
    merge(w, tail_ref, bv_ref, 1)
    hand_on = pltpu.make_async_copy(w, merged_any, sems.at[0])
    hand_on.start()

    def put(at, value):
        ctx_ref[:, at] = value

    attend(q_ref, k_ref, v_ref, query_mask, key_mask, put)
    hand_on.wait()


def eval_attention_kernel(lengths_ref, x_ref, tail_ref, w_any, ctx_ref, w, q_s, k_s, v_s, sems, *, first):
    step = pl.program_id(0)
    x = x_ref[...]

    def project(ready):
        ready(0)
        q = dot(x, w[:WIDTH]) + row(tail_ref, BQ)
        q_s[...] = (q.astype(bf16).astype(f32) * HEAD_DIM**-0.5).astype(bf16)
        ready(1)
        k_s[...] = dot(x, w[WIDTH : 2 * WIDTH]).astype(bf16)
        ready(2)
        v_s[...] = (dot(x, w[2 * WIDTH :]) + row(tail_ref, BV)).astype(bf16)

    @pl.when(step == 0)
    def _():
        rows = [pl.ds(WIDTH * i, WIDTH) for i in range(3)]
        copies = [pltpu.make_async_copy(w_any.at[r], w.at[r], sems.at[i]) for i, r in enumerate(rows)]
        for copy in copies:
            copy.start()
        project(lambda i: copies[i].wait())

    @pl.when(step != 0)
    def _():
        project(lambda i: None)

    position = lax.broadcasted_iota(jnp.int32, (BUCKET, LANES), 0)
    column = lax.broadcasted_iota(jnp.int32, (BUCKET, LANES), 1)
    length = lengths_ref[first + step]
    key_mask = jnp.where((column > 0) | (position < length), 0.0, FORBIDDEN).astype(bf16)
    query_mask = jnp.where(column == 0, 1.0, 0.0).astype(bf16)

    def put(at, value):
        ctx_ref[:, at] = value

    attend(q_s, k_s, v_s, query_mask, key_mask, put)


def up_weight(w, slab, at):
    return w[UP_AT + WIDTH * slab : UP_AT + WIDTH * (slab + 1), at : at + CHUNK]


def down_weight(w, slab, at):
    rows = DOWN_AT + WIDTH * slab + at
    return w[rows : rows + CHUNK]


def feed_forward(h1, tail_ref, w, ready, keep):
    chunks = [(slab, at) for slab in range(SLABS) for at in range(0, WIDTH, CHUNK)]

    def up(slab, at):
        if at == 0:
            ready(UP_AT + WIDTH * slab, UP_AT + WIDTH * (slab + 1))
        u = dot(h1, up_weight(w, slab, at)) + row(tail_ref, B1 + slab)[:, at : at + CHUNK]
        keep(slab, at, u)
        return u

    total = None
    u = up(*chunks[0])
    for i, (slab, at) in enumerate(chunks):
        later = up(*chunks[i + 1]) if i + 1 < len(chunks) else None
        if at == 0:
            ready(DOWN_AT + WIDTH * slab, DOWN_AT + WIDTH * (slab + 1))
        part = dot(gelu(u).astype(bf16), down_weight(w, slab, at))
        total = part if total is None else total + part
        u = later
    return total


def eval_tail_kernel(x_ref, ctx_ref, tail_ref, w_any, *refs):
    out_ref, w, sems = refs[-3:]

    def run(ready):
        ready(0, WIDTH)
        resid = x_ref[...].astype(f32) + (dot(ctx_ref[...], w[:WIDTH]) + row(tail_ref, BO))
        normed, _ = normalise(resid)
        h1 = (normed * row(tail_ref, G1) + row(tail_ref, C1)).astype(bf16)
        down = feed_forward(h1, tail_ref, w, ready, lambda slab, at, u: None)
        normed, _ = normalise(h1.astype(f32) + (down + row(tail_ref, B2)))
        out_ref[...] = (normed * row(tail_ref, G2) + row(tail_ref, C2)).astype(bf16)

    @pl.when(pl.program_id(0) == 0)
    def _():
        copies = {}
        for group in GROUPS:
            for part in group:
                rows = pl.ds(WIDTH * part, WIDTH)
                copies[part] = pltpu.make_async_copy(w_any.at[rows], w.at[rows], sems.at[part])
                copies[part].start()

        def ready(first, last):
            for group in GROUPS:
                if first // WIDTH in group and first // WIDTH in copies:
                    for part in group:
                        copies.pop(part).wait()

        run(ready)

    @pl.when(pl.program_id(0) != 0)
    def _():
        run(lambda first, last: None)


def attention_back(q_ref, k_ref, v_ref, dctx, masks, dq_s, dk_s, dv_s):
    query_mask, key_mask = masks
    rows = q_ref.shape[0]
    masks = jnp.concatenate([query_mask, query_mask], axis=0)

    def products(pair):
        at = slice(PAIR * pair, PAIR * (pair + 1))
        q2, k, d2 = head_stack(q_ref[:, at]), k_ref[:, at], head_stack(dctx[:, at])
        scores = dot_last(
            jnp.concatenate([k, key_mask], axis=1), jnp.concatenate([q2, masks], axis=1)
        )
        return scores, dot_last(v_ref[:, at], d2), q2, k, d2

    now = products(0)
    for pair in range(PAIRS):
        later = products(pair + 1) if pair + 1 < PAIRS else None
        scores, grad_probs, q2, k, d2 = now
        at = slice(PAIR * pair, PAIR * (pair + 1))
        probs = jnp.exp(scores - jnp.max(scores, axis=0, keepdims=True))
        probs = probs * (1.0 / jnp.sum(probs, axis=0, keepdims=True))
        dv_s[:, at] = dot(probs.astype(bf16), d2).astype(bf16)
        inner = jnp.sum(probs * grad_probs, axis=0, keepdims=True)
        grad_scores = (probs * (grad_probs - inner)).astype(bf16)
        dk_s[:, at] = dot(grad_scores, q2).astype(bf16)
        crossed = dot_first(k, grad_scores)
        dq = jnp.concatenate([crossed[:HEAD_DIM, :rows], crossed[HEAD_DIM:, rows:]], axis=0)
        dq_s[:, at] = (dq.T * HEAD_DIM**-0.5).astype(bf16)
        now = later


def train_kernel(
    counts_ref, lengths_ref, table_ref, rest_table_ref, x_ref, q_any, k_any, v_any, ctx_ref, grad_any,
    tail_ref, bq_ref, bv_ref, *refs, n_qkv,
):
    *refs, q_ref, k_ref, v_ref, grad_ref, out_ref, dq_s, dk_s, dv_s, sems = refs
    *w_refs, out_any, token_ref, sums_ref, w_any, wqkv, w, lanes, u_s = refs
    rest_refs = w_refs[n_qkv:]
    ready = start_rest(rest_table_ref, rest_refs, w, sems.at[pl.ds(2, 24)])
    start_qkv(table_ref, w_refs[:n_qkv], wqkv, sems.at[0])
    later_in = [
        pltpu.make_async_copy(any_ref, ref, sems.at[26 + i])
        for i, (any_ref, ref) in enumerate(
            ((grad_any, grad_ref), (q_any, q_ref), (k_any, k_ref), (v_any, v_ref))
        )
    ]
    for copy in later_in:
        copy.start()
    x = x_ref[...]
    aq = dot_last(x, adapter(tail_ref, 0)).astype(bf16)
    av = dot_last(x, adapter(tail_ref, 1)).astype(bf16)

    ready(0, WIDTH)
    resid = x.astype(f32) + (dot(ctx_ref[...], w[:WIDTH]) + row(tail_ref, BO))
    normed_one, scale_one = normalise(resid)
    h1 = (normed_one * row(tail_ref, G1) + row(tail_ref, C1)).astype(bf16)

    def keep(slab, at, u):
        u_s[slab, :, at : at + CHUNK] = u

    ready(UP_AT, DOWN_AT)
    if len(rest_refs) > 1:
        slabs_of_columns(w, lanes)
    ready(DOWN_AT, REST_ROWS)
    for copy in later_in:
        copy.wait()
    down = feed_forward(h1, tail_ref, w, ready, keep)
    keep_rest = pltpu.make_async_copy(w, w_any, sems.at[1])
    keep_rest.start()
    normed_two, scale_two = normalise(h1.astype(f32) + (down + row(tail_ref, B2)))
    out_ref[...] = (normed_two * row(tail_ref, G2) + row(tail_ref, C2)).astype(bf16)
    keep_out = pltpu.make_async_copy(out_ref, out_any, sems.at[30])
    keep_out.start()

    grad_two = normalise_back(grad_ref[...].astype(f32) * row(tail_ref, G2), normed_two, scale_two)
    df = grad_two.astype(bf16)
    chunks = [(slab, at) for slab in range(SLABS) for at in range(0, WIDTH, CHUNK)]
    total = None
    grad_gelu = dot_last(df, down_weight(w, *chunks[0]))
    for i, (slab, at) in enumerate(chunks):
        later = dot_last(df, down_weight(w, *chunks[i + 1])) if i + 1 < len(chunks) else None
        du = (grad_gelu * gelu_slope(u_s[slab, :, at : at + CHUNK])).astype(bf16)
        part = dot_last(du, up_weight(w, slab, at))
        total = part if total is None else total + part
        grad_gelu = later
    dh1 = (grad_two + total).astype(bf16)
    grad_one = normalise_back(dh1.astype(f32) * row(tail_ref, G1), normed_one, scale_one)
    token_ref[...] = grad_one
    dctx = dot_last(grad_one.astype(bf16), w[:WIDTH]).astype(bf16)
    attention_back(q_ref, k_ref, v_ref, dctx, item_masks(counts_ref, lengths_ref), dq_s, dk_s, dv_s)

    wait_all(wqkv, sems.at[0])
    dq, dk, dv = dq_s[...], dk_s[...], dv_s[...]
    daq = (2.0 * dot_last(dq, bq_ref[...])).astype(bf16)
    dav = (2.0 * dot_last(dv, bv_ref[...])).astype(bf16)
    sums_ref[:RANK] = 2.0 * dot_first(aq, dq)
    sums_ref[RANK:] = 2.0 * dot_first(av, dv)
    token_ref[...] += (
        dot_last(dq, wqkv[:WIDTH])
        + dot_last(dk, wqkv[WIDTH : 2 * WIDTH])
        + dot_last(dv, wqkv[2 * WIDTH :])
        + dot(daq, adapter(tail_ref, 0))
        + dot(dav, adapter(tail_ref, 1))
    )
    keep_rest.wait()
    keep_out.wait()


def window_kernel(place_ref, before_ref, own_ref, out_ref, padded_ref, flat, moved):
    ahead = before_ref.shape[0]
    flat[:ahead] = before_ref[...].astype(f32)
    flat[ahead : ahead + own_ref.shape[0]] = own_ref[...].astype(f32)
    flat[ahead + own_ref.shape[0] :] = jnp.zeros((LANES, LANES), f32)
    rows = moved.shape[0]
    start, turn = place_ref[0], place_ref[1]
    back = lax.rem(LANES - turn, LANES)
    here = pltpu.roll(flat[pl.ds(start, rows), :], back, 1)
    after = pltpu.roll(flat[pl.ds(start + 1, rows), :], back, 1)
    lane = lax.broadcasted_iota(jnp.int32, (rows, LANES), 1)
    moved[...] = jnp.where(lane < LANES - turn, here, after)
    per_row = WIDTH // LANES
    for tile in range(per_row):
        part = moved[pl.ds(tile, rows // per_row, stride=per_row), :]
        at = slice(LANES * tile, LANES * (tile + 1))
        out_ref[:, at] = part.astype(bf16)
        padded_ref[: rows // per_row, at] = part.astype(bf16)
    padded_ref[rows // per_row :] = jnp.zeros((PAD_ROWS, WIDTH), bf16)


def whole(shape):
    return pl.BlockSpec(shape, lambda *_: (0,) * len(shape))


def cost(microseconds):
    return pl.CostEstimate(flops=int(microseconds * 1e9), bytes_accessed=0, transcendentals=0)


def after(value, *others):
    return lax.optimization_barrier((value, *others))[0]


ANY = pl.BlockSpec(memory_space=pl.ANY)
SCALARS = pl.BlockSpec(memory_space=pltpu.SMEM)


def params(mebibytes):
    return pltpu.CompilerParams(vmem_limit_bytes=mebibytes * 2**20)


QKV_SCRATCH = pltpu.VMEM((QKV_ROWS, WIDTH), bf16)
REST_SCRATCH = pltpu.VMEM((REST_ROWS, WIDTH), bf16)


def train_attention(counts, lengths, table, x, bq, bv, w):
    rows = x.shape[0]
    shape = (rows, WIDTH)
    return pl.pallas_call(
        train_attention_kernel,
        in_specs=[SCALARS] * 3
        + [whole(v.shape) for v in (x, bq, bv)]
        + [ANY] * len(w),
        out_specs=[whole(shape)] * 4 + [whole((TAIL_ROWS, WIDTH)), ANY],
        out_shape=[jax.ShapeDtypeStruct(shape, bf16)] * 4
        + [jax.ShapeDtypeStruct((n, WIDTH), bf16) for n in (TAIL_ROWS, QKV_ROWS)],
        grid=(1,),
        scratch_shapes=[QKV_SCRATCH, pltpu.SemaphoreType.DMA((2,))],
        compiler_params=params(TRAIN_ATTENTION_MIB),
        cost_estimate=cost(11),
        name="train_attention",
    )(counts, lengths, table, x, bq, bv, *w)


def eval_attention(lengths, x, tail, w, first, count):
    return pl.pallas_call(
        functools.partial(eval_attention_kernel, first=first),
        in_specs=[
            SCALARS,
            pl.BlockSpec((BUCKET, WIDTH), lambda i: (i + first, 0)),
            whole(tail.shape),
            ANY,
        ],
        out_specs=pl.BlockSpec((BUCKET, WIDTH), lambda i: (i, 0)),
        out_shape=jax.ShapeDtypeStruct((count * BUCKET, WIDTH), bf16),
        grid=(count,),
        scratch_shapes=[QKV_SCRATCH]
        + [pltpu.VMEM((BUCKET, WIDTH), bf16)] * 3
        + [pltpu.SemaphoreType.DMA((3,))],
        compiler_params=params(EVAL_ATTENTION_MIB),
        cost_estimate=cost(1 + 7 * count),
        name="eval_attention",
    )(lengths, x, tail, w)


def eval_tail(x, ctx, tail, w, first, done=None):
    rows = ctx.shape[0]
    given = [] if done is None else [done]
    return pl.pallas_call(
        eval_tail_kernel,
        in_specs=[
            pl.BlockSpec((BUCKET, WIDTH), lambda i: (i + first, 0)),
            pl.BlockSpec((BUCKET, WIDTH), lambda i: (i, 0)),
            whole(tail.shape),
            ANY,
        ]
        + [ANY] * len(given),
        out_specs=pl.BlockSpec((BUCKET, WIDTH), lambda i: (i + first, 0)),
        out_shape=jax.ShapeDtypeStruct(x.shape, bf16),
        grid=(rows // BUCKET,),
        scratch_shapes=[REST_SCRATCH, pltpu.SemaphoreType.DMA((1 + 2 * SLABS,))],
        input_output_aliases={4: 0} if given else {},
        compiler_params=params(EVAL_TAIL_MIB),
        cost_estimate=cost(3 + 8 * (rows // BUCKET)),
        name="eval_tail",
    )(x, ctx, tail, w, *given)


def train_rest(counts, lengths, table, rest_table, x, q, k, v, ctx, grad, tail, bq, bv, w, rest):
    rows = x.shape[0]
    shape = (rows, WIDTH)
    return pl.pallas_call(
        functools.partial(train_kernel, n_qkv=len(w)),
        in_specs=[SCALARS] * 4
        + [whole(shape), ANY, ANY, ANY, whole(shape), ANY]
        + [whole(v.shape) for v in (tail, bq, bv)]
        + [ANY] * (len(w) + len(rest)),
        out_specs=[ANY, whole(shape), whole((2 * RANK, WIDTH)), ANY],
        out_shape=[
            jax.ShapeDtypeStruct(shape, bf16),
            jax.ShapeDtypeStruct(shape, f32),
            jax.ShapeDtypeStruct((2 * RANK, WIDTH), f32),
            jax.ShapeDtypeStruct((REST_ROWS, WIDTH), bf16),
        ],
        grid=(1,),
        scratch_shapes=[
            QKV_SCRATCH,
            REST_SCRATCH,
            pltpu.VMEM((SLABS * WIDTH, LANES), f32),
            pltpu.VMEM((SLABS, rows, WIDTH), f32),
            *[pltpu.VMEM(shape, bf16)] * 8,
            pltpu.SemaphoreType.DMA((31,)),
        ],
        compiler_params=params(TRAIN_REST_MIB),
        cost_estimate=cost(36),
        name="train_rest",
    )(counts, lengths, table, rest_table, x, q, k, v, ctx, grad, tail, bq, bv, *w, *rest)


def window(start, turn, before, own, rows):
    ahead = before.shape[0]
    place = jnp.stack([start, turn]).astype(jnp.int32)
    return pl.pallas_call(
        window_kernel,
        in_specs=[SCALARS, whole(before.shape), whole(own.shape)],
        out_specs=[whole((rows, WIDTH)), whole((rows + PAD_ROWS, WIDTH))],
        out_shape=[
            jax.ShapeDtypeStruct((rows, WIDTH), bf16),
            jax.ShapeDtypeStruct((rows + PAD_ROWS, WIDTH), bf16),
        ],
        grid=(1,),
        scratch_shapes=[
            pltpu.VMEM((ahead + own.shape[0] + LANES, LANES), f32),
            pltpu.VMEM((rows * (WIDTH // LANES), LANES), f32),
        ],
        compiler_params=params(WINDOW_MIB),
        cost_estimate=cost(2),
        name="window",
    )(place, before, own)


AXES = ("fsdp", "rep")


def tail_rows(flat):
    at = VECTOR_ROWS * WIDTH
    vectors = jnp.pad(flat[:at].reshape(VECTOR_ROWS, WIDTH), ((0, A_AT - VECTOR_ROWS), (0, 0)))
    a = flat[at:].reshape(2, WIDTH, RANK).transpose(0, 2, 1).reshape(2 * RANK, WIDTH)
    return jnp.concatenate([vectors, a])


def collect_generic(frozen, devices):
    me = lax.axis_index(AXES)
    share = WEIGHT_ROWS // devices
    extra = frozen.shape[0] - share * WIDTH
    spill = extra * devices
    before = lax.ppermute(frozen[-spill:], AXES, [(d, (d + 1) % devices) for d in range(devices)])
    flat = lax.dynamic_slice(
        jnp.concatenate([before, frozen]), (spill - extra * me,), (share * WIDTH,)
    )
    gathered = lax.all_gather(flat.reshape(share, WIDTH), AXES, axis=0, tiled=True)
    tail = lax.psum(jnp.where(me == devices - 1, frozen[-spill:].astype(f32), 0.0), AXES)
    w1 = gathered[QKV_ROWS + WIDTH : QKV_ROWS + WIDTH * (1 + SLABS)]
    w1 = w1.reshape(WIDTH, SLABS, WIDTH).transpose(1, 0, 2).reshape(WIDTH * SLABS, WIDTH)
    rest = jnp.concatenate(
        [gathered[QKV_ROWS : QKV_ROWS + WIDTH], w1, gathered[QKV_ROWS + WIDTH * (1 + SLABS) :]]
    )
    none = jnp.zeros((8,), jnp.int32)
    return none, [gathered[:QKV_ROWS], tail_rows(tail.astype(bf16))], none, [rest]


def device(z, x, y, core):
    return ((z * 2 + x) * 2 + y) * 2 + core


PLANE = [(x, y, core) for x in range(2) for y in range(2) for core in range(2)]
EVERY = [(z, *p) for z in range(4) for p in PLANE]


def along_z(value, pairs):
    return lax.ppermute(
        value, AXES, [(device(a, *p), device(b, *p)) for a, b in pairs for p in PLANE]
    )


def first_way(value):
    return lax.ppermute(
        value, AXES,
        [(device(z, x, y, c), device(z, x ^ (1 - c), y ^ c, c)) for z, x, y, c in EVERY],
    )


def second_way(value):
    return lax.ppermute(
        value, AXES,
        [(device(z, x, y, c), device(z, x ^ c, y ^ (1 - c), c)) for z, x, y, c in EVERY],
    )


def sibling(value):
    return lax.ppermute(
        value, AXES, [(device(z, x, y, c), device(z, x, y, 1 - c)) for z, x, y, c in EVERY]
    )


def collect(frozen, query_b, value_b):
    me = lax.axis_index(AXES)
    z, core = me // 8, me % 2
    chip = me // 2
    share = WEIGHT_ROWS // 32
    extra = frozen.shape[0] - share * WIDTH
    spill = extra * 32
    padded = -(-frozen.shape[0] // 1024) * 1024
    own = jnp.pad(frozen, (0, padded - frozen.shape[0])).reshape(padded // LANES, LANES)
    first = spill - extra * me
    start, turn = first // LANES, first % LANES

    plane = chip % 4
    one, two = jnp.where(core == 0, 2, 1), jnp.where(core == 0, 1, 2)
    mine_at = jnp.stack([plane, plane ^ one, plane ^ two, plane ^ 3]) * 2 + core
    other_at = jnp.stack([plane, plane ^ two, plane ^ one, plane ^ 3]) * 2 + 1 - core
    at = jnp.concatenate([mine_at, other_at]).astype(jnp.int32)
    flag = z[None].astype(jnp.int32)
    level = jnp.stack([jnp.maximum(z, 1), jnp.where(z == 2, 3, 2), jnp.where(z < 2, 3, 1)])
    level = level.astype(jnp.int32)

    last_rows = frozen[-spill:]
    before = lax.ppermute(last_rows, AXES, [(d, d + 1) for d in range(31)])
    mine, padded = window(start, turn, before.reshape(spill // LANES, LANES), own, share)

    last_rows, query_b, value_b, at, flag, level = lax.optimization_barrier(
        (last_rows, query_b, value_b, at, flag, level, mine)
    )[:-1]
    tail = tail_rows(
        lax.ppermute(last_rows, AXES, [(31, device(0, 0, 0, 0))])
        + lax.ppermute(last_rows, AXES, [(31, device(2, 0, 0, 0))])
    )
    bq, bv = query_b.astype(bf16), value_b.astype(bf16)
    table = jnp.concatenate([at, flag])
    codes = jnp.stack([at + 8 * (level[1] - 1), at + 8 * (level[2] - 1)], axis=1).reshape(-1)
    rest_table = jnp.concatenate([at + 8 * (level[0] - 1), codes, flag])

    up_two = along_z(padded, [(0, 2), (2, 3)])
    near = [mine, first_way(mine), second_way(mine)]
    down_one = along_z(mine, [(1, 0), (2, 1), (3, 2)])

    up = jnp.concatenate([jnp.where(z == 2, up_two[:share], mine), tail])
    up_one = along_z(up, [(0, 1), (1, 2), (2, 3)])
    near[1], down_one = lax.optimization_barrier((near[1], down_one, up))[:2]
    near.append(second_way(near[1]))
    down_two = along_z(down_one, [(1, 0), (2, 1)])
    up_one, down_two, near[3] = lax.optimization_barrier((up_one, down_two, near[3]))

    far = [
        jnp.where(z == 0, jnp.concatenate([down_one, tail]), jnp.where(z == 2, up, up_one))
    ]
    far += [first_way(far[0]), second_way(far[0])]
    ends = along_z(jnp.where(z == 1, down_two, up_one[:share]), [(1, 0), (2, 3)])
    near_other = [sibling(v) for v in near]
    bq, bv, table, rest_table, *ready = lax.optimization_barrier(
        (bq, bv, table, rest_table, *far, *near_other)
    )
    far, near_other = ready[:3], ready[3:]

    far.append(second_way(far[1]))
    far_other = [sibling(v) for v in far[:3]]
    last = jnp.stack(
        [
            jnp.where(z == 0, down_two, jnp.where(z == 3, up_two[:share], down_one)),
            jnp.where(z == 1, down_two, jnp.where(z == 2, up_one[:share], ends)),
        ]
    )
    far[3], last, *far_other = lax.optimization_barrier((far[3], last, *far_other))
    far_other.append(sibling(far[3]))
    projections = [*near, *near_other, *far, *far_other]
    last = [last, first_way(last), second_way(last)]
    return table, projections, rest_table, last, bq, bv


def other_planes(value, flip):
    return lax.ppermute(
        value, AXES, [(device(z, *p), device(z ^ flip, *p)) for z, *p in EVERY]
    )


def other_chips(value, flip_x, flip_y):
    return lax.ppermute(
        value, AXES,
        [(device(z, x, y, c), device(z, x ^ flip_x, y ^ flip_y, c)) for z, x, y, c in EVERY],
    )


def plane_total(value):
    value = value + sibling(value)
    along = value + other_chips(value, 1, 0)
    across = other_chips(value, 0, 1) + other_chips(value, 1, 1)
    return along + across


def planes_total(value):
    return (value + other_planes(value, 1)) + (other_planes(value, 2) + other_planes(value, 3))


def local(
    tokens,
    bucket_item_counts,
    slot_item_lengths,
    frozen,
    query_lowrank_matrix,
    value_lowrank_matrix,
    output_gradient,
    evaluation_tokens,
    evaluation_lengths,
    *,
    mesh,
):
    devices = mesh.shape["fsdp"] * mesh.shape["rep"]
    special = tuple(mesh.shape[axis] for axis in AXES) == (8, 4)
    if special:
        table, w, rest_table, last, bq, bv = collect(
            frozen, query_lowrank_matrix, value_lowrank_matrix
        )
    else:
        table, w, rest_table, rest = collect_generic(frozen, devices)
        bq, bv = query_lowrank_matrix.astype(bf16), value_lowrank_matrix.astype(bf16)
    counts, lengths = bucket_item_counts, slot_item_lengths
    blocks = evaluation_tokens.shape[0] // BUCKET

    ctx, q, k, v, tail, merged = train_attention(counts, lengths, table, tokens, bq, bv, w)
    x = evaluation_tokens
    if special:
        x = after(x, ctx)
    most = blocks - blocks // 2
    first_ctx = eval_attention(evaluation_lengths, x, tail, merged, 0, most)
    if special:
        last = list(lax.optimization_barrier((*last, first_ctx))[:3])
        x = after(x, *last)
        last.append(second_way(last[1]))
        other = [sibling(v) for v in last[:3]]
    last_ctx = eval_attention(evaluation_lengths, x, tail, merged, most, blocks - most)
    eval_ctx = [first_ctx, last_ctx]
    if special:
        last[3] = after(last[3], last_ctx)
        rest = w + last + other + [sibling(last[3])]
    grad = after(output_gradient, *eval_ctx)
    out, token_gradient, sums, w_rest = train_rest(
        counts, lengths, table, rest_table, tokens, q, k, v, ctx, grad, tail, bq, bv, w, rest
    )
    eval_in = [after(c, sums) for c in eval_ctx]
    eval_out = eval_tail(evaluation_tokens, eval_in[0], tail, w_rest, 0)
    second = eval_in[1]
    if special:
        sums = plane_total(sums)
        second = after(second, sums, eval_out)
    eval_out = eval_tail(evaluation_tokens, second, tail, w_rest, most, eval_out)
    sums = planes_total(sums) if special else lax.psum(sums, AXES)
    gq, gv = sums[:RANK], sums[RANK:]
    return out, token_gradient, gq, gv, eval_out


def solution(mesh):
    split = P(("fsdp", "rep"), None)
    flat = P(("fsdp", "rep"))
    return jax.shard_map(
        functools.partial(local, mesh=mesh),
        mesh=mesh,
        in_specs=(split, split, split, flat, P(), P(), split, split, flat),
        out_specs=(split, split, P(), P(), split),
        check_vma=False,
    )
```

```python
import functools

import jax
import jax.numpy as jnp
from jax import lax
from jax.experimental import pallas as pl
from jax.experimental.pallas import tpu as pltpu
from jax.sharding import PartitionSpec as P

WIDTH = 768
HEADS = 12
HEAD_DIM = 64
SLABS = 4
BUCKET = 512
CHUNK = 256
PAIR = 2 * HEAD_DIM
PAIRS = HEADS // 2
WEIGHT_ROWS = WIDTH * (4 + 2 * SLABS)
QKV_ROWS = 3 * WIDTH
VECTOR_ROWS = 12
RANK = 8
FORBIDDEN = -1e30
EPS = 1e-5
TRAIN_ATTENTION_MIB = 24
EVAL_ATTENTION_MIB = 24
TRAIN_REST_MIB = 40
EVAL_TAIL_MIB = 28
WINDOW_MIB = 16
REST_ROWS = WEIGHT_ROWS - QKV_ROWS
UP_AT = WIDTH
DOWN_AT = WIDTH * (1 + SLABS)
TAIL_ROWS = 32
PAD_ROWS = 16
A_AT = 16
LANES = 128

f32 = jnp.float32
bf16 = jnp.bfloat16

BQ, BV, BO, B1, B2, G1, C1, G2, C2 = 0, 1, 2, 3, 7, 8, 9, 10, 11


def dot(left, right):
    return jnp.dot(left, right, preferred_element_type=f32)


def dot_last(left, right):
    return lax.dot_general(left, right, (((1,), (1,)), ((), ())), preferred_element_type=f32)


def dot_first(left, right):
    return lax.dot_general(left, right, (((0,), (0,)), ((), ())), preferred_element_type=f32)


def row(tail_ref, at):
    return tail_ref[:A_AT].astype(f32)[at : at + 1]


def adapter(tail_ref, which):
    return tail_ref[A_AT:].astype(f32)[RANK * which : RANK * (which + 1)].astype(bf16)


def normalise(resid):
    centred = resid - jnp.mean(resid, axis=-1, keepdims=True)
    scale = lax.rsqrt(jnp.mean(centred * centred, axis=-1, keepdims=True) + EPS)
    return centred * scale, scale


def normalise_back(grad, normed, scale):
    return scale * (
        grad
        - jnp.mean(grad, axis=-1, keepdims=True)
        - normed * jnp.mean(grad * normed, axis=-1, keepdims=True)
    )


def half_error_function(value):
    return 0.5 + 0.5 * lax.erf(value * 0.7071067811865476)


def gelu(value):
    return value * half_error_function(value)


def gelu_slope(value):
    density = jnp.exp(value * value * -0.5) * 0.3989422804014327
    return half_error_function(value) + value * density


def low_lanes(rows):
    return lax.broadcasted_iota(jnp.int32, (rows, PAIR), 1) < HEAD_DIM


def head_stack(pair):
    low = low_lanes(pair.shape[0])
    zero = jnp.zeros_like(pair)
    return jnp.concatenate([jnp.where(low, pair, zero), jnp.where(low, zero, pair)], axis=0)


def item_masks(counts_ref, lengths_ref):
    position = lax.broadcasted_iota(jnp.int32, (BUCKET, 128), 0)
    column = lax.broadcasted_iota(jnp.int32, (BUCKET, 128), 1)
    start = jnp.zeros((BUCKET, 128), jnp.int32)
    finish = jnp.zeros((BUCKET, 128), jnp.int32)
    valid = jnp.zeros((BUCKET, 128), jnp.int32)
    base = jnp.int32(0)
    first = jnp.int32(0)
    for level in range(counts_ref.shape[1]):
        extent = BUCKET >> level
        count = counts_ref[0, level]
        inside = (column >= first) & (column < first + count)
        here = base + (column - first) * extent
        start = jnp.where(inside, here, start)
        finish = jnp.where(inside, here + extent, finish)
        base = base + count * extent
        first = first + count
    for slot in range(lengths_ref.shape[1]):
        valid = jnp.where(column == slot, lengths_ref[0, slot], valid)
    member = (position >= start) & (position < finish)
    allowed = member & (position < start + valid)
    return (
        jnp.where(member, 1.0, 0.0).astype(bf16),
        jnp.where(allowed, 0.0, FORBIDDEN).astype(bf16),
    )


def attend(q_s, k_s, v_s, query_mask, key_mask, put):
    rows = q_s.shape[0]
    ones = jnp.ones((rows, 128), bf16)
    masks = jnp.concatenate([query_mask, query_mask], axis=0)
    low = low_lanes(rows)

    def scores_of(pair):
        at = slice(PAIR * pair, PAIR * (pair + 1))
        left = jnp.concatenate([head_stack(q_s[:, at]), masks], axis=1)
        return dot_last(left, jnp.concatenate([k_s[:, at], key_mask], axis=1))

    scores = scores_of(0)
    for pair in range(PAIRS):
        later = scores_of(pair + 1) if pair + 1 < PAIRS else None
        at = slice(PAIR * pair, PAIR * (pair + 1))
        top = jnp.max(scores, axis=-1, keepdims=True)
        weights = jnp.exp(scores - top).astype(bf16)
        mixed = dot(weights, jnp.concatenate([v_s[:, at], ones], axis=1))
        mixed = mixed[:, :PAIR] / mixed[:, PAIR:]
        put(at, jnp.where(low, mixed[:rows], mixed[rows:]).astype(bf16))
        scores = later


def start_qkv(table_ref, refs, w, sem, tail=None, tail_sem=None):
    if len(refs) == 2:
        pltpu.make_async_copy(refs[0], w, sem).start()
        if tail is not None:
            pltpu.make_async_copy(refs[1], tail, tail_sem).start()
        return
    units = len(refs) // 2
    size = refs[0].shape[0]

    def start(chosen):
        for i, ref in enumerate(chosen):
            to = pl.multiple_of(table_ref[i] * size, 16)
            pltpu.make_async_copy(ref.at[pl.ds(0, size)], w.at[pl.ds(to, size)], sem).start()

    if tail is not None:
        for i, ref in enumerate(refs[units:]):

            @pl.when(table_ref[i] == 0)
            def _():
                rows = ref.at[pl.ds(size, TAIL_ROWS)]
                pltpu.make_async_copy(rows, tail, tail_sem).start()

    @pl.when(table_ref[units] == 0)
    def _():
        start(refs[:units])

    @pl.when(table_ref[units] != 0)
    def _():
        start(refs[units:])


def wait_all(ref, sem):
    pltpu.make_async_copy(ref, ref, sem).wait()


def start_rest(table_ref, refs, w, sems):
    units = len(refs) // 3
    size = refs[-1].shape[1] if units else w.shape[0]

    def start(ref, at):
        to = pl.multiple_of(at * size, 16)
        pltpu.make_async_copy(ref, w.at[pl.ds(to, size)], sems.at[at]).start()

    if units:

        @pl.when(table_ref[3 * units] == 0)
        def _():
            for i in range(units):
                start(refs[units + i].at[pl.ds(0, size)], table_ref[i])

        @pl.when(table_ref[3 * units] != 0)
        def _():
            for i in range(units):
                start(refs[i].at[pl.ds(0, size)], table_ref[i])

        for i in range(units):
            for slot in range(2):
                start(refs[2 * units + i].at[slot], table_ref[units + 2 * i + slot])
    else:
        start(refs[0], 0)

    waiting = set(range(w.shape[0] // size))

    def ready(first, last):
        for at in range(first // size, (last - 1) // size + 1):
            if at in waiting:
                waiting.remove(at)
                wait_all(w.at[pl.ds(at * size, size)], sems.at[at])

    return ready


def slabs_of_columns(w, lanes):
    rows = slice(UP_AT, DOWN_AT)
    for at in range(0, WIDTH, LANES):
        lanes[...] = w[rows, at : at + LANES].astype(f32)
        for slab in range(SLABS):
            to = UP_AT + WIDTH * slab
            part = lanes[pl.ds(slab, WIDTH, stride=SLABS), :]
            w[to : to + WIDTH, at : at + LANES] = part.astype(bf16)


def train_attention_kernel(
    counts_ref, lengths_ref, table_ref, x_ref, bq_ref, bv_ref, *refs
):
    *w_refs, ctx_ref, q_ref, k_ref, v_ref, tail_ref, w, merged_ref, sems = refs
    start_qkv(table_ref, w_refs, w, sems.at[0], tail_ref, sems.at[1])
    query_mask, key_mask = item_masks(counts_ref, lengths_ref)
    x = x_ref[...]
    wait_all(tail_ref, sems.at[1])
    aq = dot_last(x, adapter(tail_ref, 0)).astype(bf16)
    av = dot_last(x, adapter(tail_ref, 1)).astype(bf16)
    wait_all(w, sems.at[0])
    q = dot(x, w[:WIDTH]) + row(tail_ref, BQ) + 2.0 * dot(aq, bq_ref[...])
    q_ref[...] = (q.astype(bf16).astype(f32) * HEAD_DIM**-0.5).astype(bf16)
    k_ref[...] = dot(x, w[WIDTH : 2 * WIDTH]).astype(bf16)
    v = dot(x, w[2 * WIDTH :]) + row(tail_ref, BV) + 2.0 * dot(av, bv_ref[...])
    v_ref[...] = v.astype(bf16)
    for which, b_ref in enumerate((bq_ref, bv_ref)):
        rows = slice(2 * WIDTH * which, 2 * WIDTH * which + WIDTH)
        merged = w[rows].astype(f32) + 2.0 * dot_first(adapter(tail_ref, which), b_ref[...])
        merged_ref[WIDTH * which : WIDTH * (which + 1)] = merged.astype(bf16)

    def put(at, value):
        ctx_ref[:, at] = value

    attend(q_ref, k_ref, v_ref, query_mask, key_mask, put)


def eval_attention_kernel(
    lengths_ref, x_ref, tail_ref, w, merged, ctx_ref, q_s, k_s, v_s, *, first
):
    step = pl.program_id(0)
    x = x_ref[...]
    q = dot(x, merged[:WIDTH]) + row(tail_ref, BQ)
    q_s[...] = (q.astype(bf16).astype(f32) * HEAD_DIM**-0.5).astype(bf16)
    k_s[...] = dot(x, w[WIDTH : 2 * WIDTH]).astype(bf16)
    v_s[...] = (dot(x, merged[WIDTH:]) + row(tail_ref, BV)).astype(bf16)
    position = lax.broadcasted_iota(jnp.int32, (BUCKET, LANES), 0)
    column = lax.broadcasted_iota(jnp.int32, (BUCKET, LANES), 1)
    length = lengths_ref[first + step]
    key_mask = jnp.where((column > 0) | (position < length), 0.0, FORBIDDEN).astype(bf16)
    query_mask = jnp.where(column == 0, 1.0, 0.0).astype(bf16)

    def put(at, value):
        ctx_ref[:, at] = value

    attend(q_s, k_s, v_s, query_mask, key_mask, put)


def up_weight(w, slab, at):
    return w[UP_AT + WIDTH * slab : UP_AT + WIDTH * (slab + 1), at : at + CHUNK]


def down_weight(w, slab, at):
    rows = DOWN_AT + WIDTH * slab + at
    return w[rows : rows + CHUNK]


def feed_forward(h1, tail_ref, w, keep):
    chunks = [(slab, at) for slab in range(SLABS) for at in range(0, WIDTH, CHUNK)]

    def up(slab, at):
        u = dot(h1, up_weight(w, slab, at)) + row(tail_ref, B1 + slab)[:, at : at + CHUNK]
        keep(slab, at, u)
        return u

    total = None
    u = up(*chunks[0])
    for i, (slab, at) in enumerate(chunks):
        later = up(*chunks[i + 1]) if i + 1 < len(chunks) else None
        part = dot(gelu(u).astype(bf16), down_weight(w, slab, at))
        total = part if total is None else total + part
        u = later
    return total


def eval_tail_kernel(x_ref, ctx_ref, tail_ref, w, *refs):
    out_ref = refs[-1]
    resid = x_ref[...].astype(f32) + (dot(ctx_ref[...], w[:WIDTH]) + row(tail_ref, BO))
    normed, _ = normalise(resid)
    h1 = (normed * row(tail_ref, G1) + row(tail_ref, C1)).astype(bf16)
    down = feed_forward(h1, tail_ref, w, lambda slab, at, u: None)
    normed, _ = normalise(h1.astype(f32) + (down + row(tail_ref, B2)))
    out_ref[...] = (normed * row(tail_ref, G2) + row(tail_ref, C2)).astype(bf16)


def attention_back(q_ref, k_ref, v_ref, dctx, masks, dq_s, dk_s, dv_s):
    query_mask, key_mask = masks
    rows = q_ref.shape[0]
    masks = jnp.concatenate([query_mask, query_mask], axis=0)

    def products(pair):
        at = slice(PAIR * pair, PAIR * (pair + 1))
        q2, k, d2 = head_stack(q_ref[:, at]), k_ref[:, at], head_stack(dctx[:, at])
        scores = dot_last(
            jnp.concatenate([k, key_mask], axis=1), jnp.concatenate([q2, masks], axis=1)
        )
        return scores, dot_last(v_ref[:, at], d2), q2, k, d2

    now = products(0)
    for pair in range(PAIRS):
        later = products(pair + 1) if pair + 1 < PAIRS else None
        scores, grad_probs, q2, k, d2 = now
        at = slice(PAIR * pair, PAIR * (pair + 1))
        probs = jnp.exp(scores - jnp.max(scores, axis=0, keepdims=True))
        probs = probs * (1.0 / jnp.sum(probs, axis=0, keepdims=True))
        dv_s[:, at] = dot(probs.astype(bf16), d2).astype(bf16)
        inner = jnp.sum(probs * grad_probs, axis=0, keepdims=True)
        grad_scores = (probs * (grad_probs - inner)).astype(bf16)
        dk_s[:, at] = dot(grad_scores, q2).astype(bf16)
        crossed = dot_first(k, grad_scores)
        dq = jnp.concatenate([crossed[:HEAD_DIM, :rows], crossed[HEAD_DIM:, rows:]], axis=0)
        dq_s[:, at] = (dq.T * HEAD_DIM**-0.5).astype(bf16)
        now = later


def train_kernel(
    counts_ref, lengths_ref, rest_table_ref, x_ref, q_any, k_any, v_any, ctx_ref, grad_any,
    tail_ref, bq_ref, bv_ref, wqkv_any, *refs,
):
    *refs, q_ref, k_ref, v_ref, grad_ref, out_ref, dq_s, dk_s, dv_s, sems = refs
    *w_refs, out_any, token_ref, sums_ref, w, wqkv, lanes, u_s = refs
    if len(w_refs) > 1:
        end = w_refs[-8:]
        w_refs = [*w_refs[:-8], *end[:3], end[6], *end[3:6], end[7]]
    ready = start_rest(rest_table_ref, w_refs, w, sems.at[pl.ds(5, 24)])
    later_in = [
        pltpu.make_async_copy(any_ref, ref, sems.at[i])
        for i, (any_ref, ref) in enumerate(
            ((grad_any, grad_ref), (q_any, q_ref), (k_any, k_ref), (v_any, v_ref))
        )
    ]
    last_in = pltpu.make_async_copy(wqkv_any, wqkv, sems.at[29])
    for copy in [*later_in, last_in]:
        copy.start()
    x = x_ref[...]
    aq = dot_last(x, adapter(tail_ref, 0)).astype(bf16)
    av = dot_last(x, adapter(tail_ref, 1)).astype(bf16)

    ready(0, WIDTH)
    resid = x.astype(f32) + (dot(ctx_ref[...], w[:WIDTH]) + row(tail_ref, BO))
    normed_one, scale_one = normalise(resid)
    h1 = (normed_one * row(tail_ref, G1) + row(tail_ref, C1)).astype(bf16)

    def keep(slab, at, u):
        u_s[slab, :, at : at + CHUNK] = u

    ready(UP_AT, DOWN_AT)
    if len(w_refs) > 1:
        slabs_of_columns(w, lanes)
    ready(DOWN_AT, REST_ROWS)
    for copy in later_in:
        copy.wait()
    down = feed_forward(h1, tail_ref, w, keep)
    normed_two, scale_two = normalise(h1.astype(f32) + (down + row(tail_ref, B2)))
    out_ref[...] = (normed_two * row(tail_ref, G2) + row(tail_ref, C2)).astype(bf16)
    keep_out = pltpu.make_async_copy(out_ref, out_any, sems.at[4])
    keep_out.start()

    grad_two = normalise_back(grad_ref[...].astype(f32) * row(tail_ref, G2), normed_two, scale_two)
    df = grad_two.astype(bf16)
    chunks = [(slab, at) for slab in range(SLABS) for at in range(0, WIDTH, CHUNK)]
    total = None
    grad_gelu = dot_last(df, down_weight(w, *chunks[0]))
    for i, (slab, at) in enumerate(chunks):
        later = dot_last(df, down_weight(w, *chunks[i + 1])) if i + 1 < len(chunks) else None
        du = (grad_gelu * gelu_slope(u_s[slab, :, at : at + CHUNK])).astype(bf16)
        part = dot_last(du, up_weight(w, slab, at))
        total = part if total is None else total + part
        grad_gelu = later
    dh1 = (grad_two + total).astype(bf16)
    grad_one = normalise_back(dh1.astype(f32) * row(tail_ref, G1), normed_one, scale_one)
    token_ref[...] = grad_one
    dctx = dot_last(grad_one.astype(bf16), w[:WIDTH]).astype(bf16)
    attention_back(q_ref, k_ref, v_ref, dctx, item_masks(counts_ref, lengths_ref), dq_s, dk_s, dv_s)

    last_in.wait()
    dq, dk, dv = dq_s[...], dk_s[...], dv_s[...]
    daq = (2.0 * dot_last(dq, bq_ref[...])).astype(bf16)
    dav = (2.0 * dot_last(dv, bv_ref[...])).astype(bf16)
    sums_ref[:RANK] = 2.0 * dot_first(aq, dq)
    sums_ref[RANK:] = 2.0 * dot_first(av, dv)
    token_ref[...] += (
        dot_last(dq, wqkv[:WIDTH])
        + dot_last(dk, wqkv[WIDTH : 2 * WIDTH])
        + dot_last(dv, wqkv[2 * WIDTH :])
        + dot(daq, adapter(tail_ref, 0))
        + dot(dav, adapter(tail_ref, 1))
    )
    keep_out.wait()


def window_kernel(place_ref, before_ref, own_ref, out_ref, padded_ref, flat, moved):
    ahead = before_ref.shape[0]
    flat[:ahead] = before_ref[...].astype(f32)
    flat[ahead : ahead + own_ref.shape[0]] = own_ref[...].astype(f32)
    flat[ahead + own_ref.shape[0] :] = jnp.zeros((LANES, LANES), f32)
    rows = moved.shape[0]
    start, turn = place_ref[0], place_ref[1]
    back = lax.rem(LANES - turn, LANES)
    here = pltpu.roll(flat[pl.ds(start, rows), :], back, 1)
    after = pltpu.roll(flat[pl.ds(start + 1, rows), :], back, 1)
    lane = lax.broadcasted_iota(jnp.int32, (rows, LANES), 1)
    moved[...] = jnp.where(lane < LANES - turn, here, after)
    per_row = WIDTH // LANES
    for tile in range(per_row):
        part = moved[pl.ds(tile, rows // per_row, stride=per_row), :]
        at = slice(LANES * tile, LANES * (tile + 1))
        out_ref[:, at] = part.astype(bf16)
        padded_ref[: rows // per_row, at] = part.astype(bf16)
    padded_ref[rows // per_row :] = jnp.zeros((PAD_ROWS, WIDTH), bf16)


def whole(shape):
    return pl.BlockSpec(shape, lambda *_: (0,) * len(shape))


def cost(microseconds):
    return pl.CostEstimate(flops=int(microseconds * 1e9), bytes_accessed=0, transcendentals=0)


def stays(value):
    return pltpu.with_memory_space_constraint(value, pltpu.VMEM)


def after(value, *others):
    return lax.optimization_barrier((value, *others))[0]


ANY = pl.BlockSpec(memory_space=pl.ANY)
IN_VMEM = pl.BlockSpec(memory_space=pltpu.VMEM)
SCALARS = pl.BlockSpec(memory_space=pltpu.SMEM)


def params(mebibytes):
    return pltpu.CompilerParams(vmem_limit_bytes=mebibytes * 2**20)


def train_attention(counts, lengths, table, x, bq, bv, w):
    rows = x.shape[0]
    shape = (rows, WIDTH)
    return pl.pallas_call(
        train_attention_kernel,
        in_specs=[SCALARS] * 3
        + [whole(v.shape) for v in (x, bq, bv)]
        + [ANY] * len(w),
        out_specs=[whole(shape)] * 4 + [whole((TAIL_ROWS, WIDTH)), IN_VMEM, IN_VMEM],
        out_shape=[jax.ShapeDtypeStruct(shape, bf16)] * 4
        + [jax.ShapeDtypeStruct((TAIL_ROWS, WIDTH), bf16)]
        + [pltpu.VMEM((n, WIDTH), bf16) for n in (QKV_ROWS, 2 * WIDTH)],
        grid=(1,),
        scratch_shapes=[pltpu.SemaphoreType.DMA((2,))],
        compiler_params=params(TRAIN_ATTENTION_MIB),
        cost_estimate=cost(11),
        name="train_attention",
    )(counts, lengths, table, x, bq, bv, *w)


def eval_attention(lengths, x, tail, w, merged, first, count):
    return pl.pallas_call(
        functools.partial(eval_attention_kernel, first=first),
        in_specs=[
            SCALARS,
            pl.BlockSpec((BUCKET, WIDTH), lambda i: (i + first, 0)),
            whole(tail.shape),
            IN_VMEM,
            IN_VMEM,
        ],
        out_specs=pl.BlockSpec((BUCKET, WIDTH), lambda i: (i, 0)),
        out_shape=(jax.ShapeDtypeStruct if first else pltpu.HBM)((count * BUCKET, WIDTH), bf16),
        grid=(count,),
        scratch_shapes=[pltpu.VMEM((BUCKET, WIDTH), bf16)] * 3,
        compiler_params=params(EVAL_ATTENTION_MIB),
        cost_estimate=cost(1 + 7 * count),
        name="eval_attention",
    )(lengths, x, tail, stays(w), stays(merged))


def eval_tail(x, ctx, tail, w, first, done=None):
    rows = ctx.shape[0]
    given = [] if done is None else [done]
    return pl.pallas_call(
        eval_tail_kernel,
        in_specs=[
            pl.BlockSpec((BUCKET, WIDTH), lambda i: (i + first, 0)),
            pl.BlockSpec((BUCKET, WIDTH), lambda i: (i, 0)),
            whole(tail.shape),
            IN_VMEM,
        ]
        + [ANY] * len(given),
        out_specs=pl.BlockSpec((BUCKET, WIDTH), lambda i: (i + first, 0)),
        out_shape=jax.ShapeDtypeStruct(x.shape, bf16),
        grid=(rows // BUCKET,),
        input_output_aliases={4: 0} if given else {},
        compiler_params=params(EVAL_TAIL_MIB),
        cost_estimate=cost(3 + 8 * (rows // BUCKET)),
        name="eval_tail",
    )(x, ctx, tail, stays(w), *given)


def train_rest(counts, lengths, rest_table, x, q, k, v, ctx, grad, tail, bq, bv, w, rest):
    rows = x.shape[0]
    shape = (rows, WIDTH)
    return pl.pallas_call(
        train_kernel,
        in_specs=[SCALARS] * 3
        + [whole(shape), ANY, ANY, ANY, whole(shape), ANY]
        + [whole(v.shape) for v in (tail, bq, bv)]
        + [ANY]
        + ([ANY] * (len(rest) - 2) + [IN_VMEM] * 2 if len(rest) > 1 else [ANY]),
        out_specs=[ANY, whole(shape), whole((2 * RANK, WIDTH)), IN_VMEM],
        out_shape=[
            jax.ShapeDtypeStruct(shape, bf16),
            jax.ShapeDtypeStruct(shape, f32),
            jax.ShapeDtypeStruct((2 * RANK, WIDTH), f32),
            pltpu.VMEM((REST_ROWS, WIDTH), bf16),
        ],
        grid=(1,),
        scratch_shapes=[
            pltpu.VMEM((QKV_ROWS, WIDTH), bf16),
            pltpu.VMEM((SLABS * WIDTH, LANES), f32),
            pltpu.VMEM((SLABS, rows, WIDTH), f32),
            *[pltpu.VMEM(shape, bf16)] * 8,
            pltpu.SemaphoreType.DMA((30,)),
        ],
        compiler_params=params(TRAIN_REST_MIB),
        cost_estimate=cost(36),
        name="train_rest",
    )(counts, lengths, rest_table, x, q, k, v, ctx, grad, tail, bq, bv, w, *rest)


def window(start, turn, before, own, rows):
    ahead = before.shape[0]
    place = jnp.stack([start, turn]).astype(jnp.int32)
    return pl.pallas_call(
        window_kernel,
        in_specs=[SCALARS, whole(before.shape), whole(own.shape)],
        out_specs=[whole((rows, WIDTH)), whole((rows + PAD_ROWS, WIDTH))],
        out_shape=[
            jax.ShapeDtypeStruct((rows, WIDTH), bf16),
            jax.ShapeDtypeStruct((rows + PAD_ROWS, WIDTH), bf16),
        ],
        grid=(1,),
        scratch_shapes=[
            pltpu.VMEM((ahead + own.shape[0] + LANES, LANES), f32),
            pltpu.VMEM((rows * (WIDTH // LANES), LANES), f32),
        ],
        compiler_params=params(WINDOW_MIB),
        cost_estimate=cost(2),
        name="window",
    )(place, before, own)


AXES = ("fsdp", "rep")


def tail_rows(flat):
    at = VECTOR_ROWS * WIDTH
    vectors = jnp.pad(flat[:at].reshape(VECTOR_ROWS, WIDTH), ((0, A_AT - VECTOR_ROWS), (0, 0)))
    a = flat[at:].reshape(2, WIDTH, RANK).transpose(0, 2, 1).reshape(2 * RANK, WIDTH)
    return jnp.concatenate([vectors, a])


def collect_generic(frozen, devices):
    me = lax.axis_index(AXES)
    share = WEIGHT_ROWS // devices
    extra = frozen.shape[0] - share * WIDTH
    spill = extra * devices
    before = lax.ppermute(frozen[-spill:], AXES, [(d, (d + 1) % devices) for d in range(devices)])
    flat = lax.dynamic_slice(
        jnp.concatenate([before, frozen]), (spill - extra * me,), (share * WIDTH,)
    )
    gathered = lax.all_gather(flat.reshape(share, WIDTH), AXES, axis=0, tiled=True)
    tail = lax.psum(jnp.where(me == devices - 1, frozen[-spill:].astype(f32), 0.0), AXES)
    w1 = gathered[QKV_ROWS + WIDTH : QKV_ROWS + WIDTH * (1 + SLABS)]
    w1 = w1.reshape(WIDTH, SLABS, WIDTH).transpose(1, 0, 2).reshape(WIDTH * SLABS, WIDTH)
    rest = jnp.concatenate(
        [gathered[QKV_ROWS : QKV_ROWS + WIDTH], w1, gathered[QKV_ROWS + WIDTH * (1 + SLABS) :]]
    )
    none = jnp.zeros((8,), jnp.int32)
    return none, [gathered[:QKV_ROWS], tail_rows(tail.astype(bf16))], none, [rest]


def device(z, x, y, core):
    return ((z * 2 + x) * 2 + y) * 2 + core


PLANE = [(x, y, core) for x in range(2) for y in range(2) for core in range(2)]
EVERY = [(z, *p) for z in range(4) for p in PLANE]


def along_z(value, pairs):
    return lax.ppermute(
        value, AXES, [(device(a, *p), device(b, *p)) for a, b in pairs for p in PLANE]
    )


def first_way(value):
    return lax.ppermute(
        value, AXES,
        [(device(z, x, y, c), device(z, x ^ (1 - c), y ^ c, c)) for z, x, y, c in EVERY],
    )


def second_way(value):
    return lax.ppermute(
        value, AXES,
        [(device(z, x, y, c), device(z, x ^ c, y ^ (1 - c), c)) for z, x, y, c in EVERY],
    )


def sibling(value):
    return lax.ppermute(
        value, AXES, [(device(z, x, y, c), device(z, x, y, 1 - c)) for z, x, y, c in EVERY]
    )


def collect(frozen, query_b, value_b):
    me = lax.axis_index(AXES)
    z, core = me // 8, me % 2
    chip = me // 2
    share = WEIGHT_ROWS // 32
    extra = frozen.shape[0] - share * WIDTH
    spill = extra * 32
    padded = -(-frozen.shape[0] // 1024) * 1024
    own = jnp.pad(frozen, (0, padded - frozen.shape[0])).reshape(padded // LANES, LANES)
    first = spill - extra * me
    start, turn = first // LANES, first % LANES

    plane = chip % 4
    one, two = jnp.where(core == 0, 2, 1), jnp.where(core == 0, 1, 2)
    mine_at = jnp.stack([plane, plane ^ one, plane ^ two, plane ^ 3]) * 2 + core
    other_at = jnp.stack([plane, plane ^ two, plane ^ one, plane ^ 3]) * 2 + 1 - core
    at = jnp.concatenate([mine_at, other_at]).astype(jnp.int32)
    flag = z[None].astype(jnp.int32)
    level = jnp.stack([jnp.maximum(z, 1), jnp.where(z == 2, 3, 2), jnp.where(z < 2, 3, 1)])
    level = level.astype(jnp.int32)

    last_rows = frozen[-spill:]
    before = lax.ppermute(last_rows, AXES, [(d, d + 1) for d in range(31)])
    mine, padded = window(start, turn, before.reshape(spill // LANES, LANES), own, share)

    last_rows, query_b, value_b, at, flag, level = lax.optimization_barrier(
        (last_rows, query_b, value_b, at, flag, level, mine)
    )[:-1]
    tail = tail_rows(
        lax.ppermute(last_rows, AXES, [(31, device(0, 0, 0, 0))])
        + lax.ppermute(last_rows, AXES, [(31, device(2, 0, 0, 0))])
    )
    bq, bv = query_b.astype(bf16), value_b.astype(bf16)
    table = jnp.concatenate([at, flag])
    codes = jnp.stack([at + 8 * (level[1] - 1), at + 8 * (level[2] - 1)], axis=1).reshape(-1)
    rest_table = jnp.concatenate([at + 8 * (level[0] - 1), codes, flag])

    up_two = along_z(padded, [(0, 2), (2, 3)])
    near = [mine, first_way(mine), second_way(mine)]
    down_one = along_z(mine, [(1, 0), (2, 1), (3, 2)])

    up = jnp.concatenate([jnp.where(z == 2, up_two[:share], mine), tail])
    up_one = along_z(up, [(0, 1), (1, 2), (2, 3)])
    near[1], down_one = lax.optimization_barrier((near[1], down_one, up))[:2]
    near.append(second_way(near[1]))
    down_two = along_z(down_one, [(1, 0), (2, 1)])
    up_one, down_two, near[3] = lax.optimization_barrier((up_one, down_two, near[3]))

    far = [
        jnp.where(z == 0, jnp.concatenate([down_one, tail]), jnp.where(z == 2, up, up_one))
    ]
    far += [first_way(far[0]), second_way(far[0])]
    ends = along_z(jnp.where(z == 1, down_two, up_one[:share]), [(1, 0), (2, 3)])
    near_other = [sibling(v) for v in near]
    bq, bv, table, rest_table, *ready = lax.optimization_barrier(
        (bq, bv, table, rest_table, *far, *near_other)
    )
    far, near_other = ready[:3], ready[3:]

    far.append(second_way(far[1]))
    far_other = [sibling(v) for v in far[:3]]
    last = jnp.stack(
        [
            jnp.where(z == 0, down_two, jnp.where(z == 3, up_two[:share], down_one)),
            jnp.where(z == 1, down_two, jnp.where(z == 2, up_one[:share], ends)),
        ]
    )
    far[3], last, *far_other = lax.optimization_barrier((far[3], last, *far_other))
    far_other.append(sibling(far[3]))
    projections = [*near, *near_other, *far, *far_other]
    last = [last, first_way(last), second_way(last)]
    return table, projections, rest_table, last, bq, bv


def other_planes(value, flip):
    return lax.ppermute(
        value, AXES, [(device(z, *p), device(z ^ flip, *p)) for z, *p in EVERY]
    )


def other_chips(value, flip_x, flip_y):
    return lax.ppermute(
        value, AXES,
        [(device(z, x, y, c), device(z, x ^ flip_x, y ^ flip_y, c)) for z, x, y, c in EVERY],
    )


def plane_total(value):
    value = value + sibling(value)
    along = value + other_chips(value, 1, 0)
    across = other_chips(value, 0, 1) + other_chips(value, 1, 1)
    return along + across


def planes_total(value):
    return (value + other_planes(value, 1)) + (other_planes(value, 2) + other_planes(value, 3))


def local(
    tokens,
    bucket_item_counts,
    slot_item_lengths,
    frozen,
    query_lowrank_matrix,
    value_lowrank_matrix,
    output_gradient,
    evaluation_tokens,
    evaluation_lengths,
    *,
    mesh,
):
    devices = mesh.shape["fsdp"] * mesh.shape["rep"]
    special = tuple(mesh.shape[axis] for axis in AXES) == (8, 4)
    if special:
        table, w, rest_table, last, bq, bv = collect(
            frozen, query_lowrank_matrix, value_lowrank_matrix
        )
    else:
        table, w, rest_table, rest = collect_generic(frozen, devices)
        bq, bv = query_lowrank_matrix.astype(bf16), value_lowrank_matrix.astype(bf16)
    counts, lengths = bucket_item_counts, slot_item_lengths
    blocks = evaluation_tokens.shape[0] // BUCKET

    ctx, q, k, v, tail, w_qkv, merged = train_attention(counts, lengths, table, tokens, bq, bv, w)
    x = evaluation_tokens
    if special:
        x = after(x, ctx)
    most = blocks - blocks // 2
    first_ctx = eval_attention(evaluation_lengths, x, tail, w_qkv, merged, 0, most)
    if special:
        last = list(lax.optimization_barrier((*last, first_ctx))[:3])
        x = after(x, *last)
        last.append(second_way(last[1]))
        other = [sibling(v) for v in last[:3]]
    last_ctx = eval_attention(
        evaluation_lengths, x, tail, w_qkv, merged, most, blocks - most
    )
    eval_ctx = [first_ctx, last_ctx]
    if special:
        last[3] = after(last[3], last_ctx)
        rest = w + last[:3] + other + [stays(last[3]), stays(sibling(last[3]))]
    grad = after(output_gradient, *eval_ctx)
    out, token_gradient, sums, w_rest = train_rest(
        counts, lengths, rest_table, tokens, q, k, v, ctx, grad, tail, bq, bv, w_qkv, rest
    )
    eval_in = [after(c, sums) for c in eval_ctx]
    eval_out = eval_tail(evaluation_tokens, eval_in[0], tail, w_rest, 0)
    second = eval_in[1]
    if special:
        sums = plane_total(sums)
        second = after(second, sums, eval_out)
    eval_out = eval_tail(evaluation_tokens, second, tail, w_rest, most, eval_out)
    sums = planes_total(sums) if special else lax.psum(sums, AXES)
    gq, gv = sums[:RANK], sums[RANK:]
    return out, token_gradient, gq, gv, eval_out


def solution(mesh):
    split = P(("fsdp", "rep"), None)
    flat = P(("fsdp", "rep"))
    return jax.shard_map(
        functools.partial(local, mesh=mesh),
        mesh=mesh,
        in_specs=(split, split, split, flat, P(), P(), split, split, flat),
        out_specs=(split, split, P(), P(), split),
        check_vma=False,
    )
```

```python
import functools

import jax
import jax.numpy as jnp
from jax import lax
from jax.experimental import pallas as pl
from jax.experimental.pallas import tpu as pltpu
from jax.sharding import PartitionSpec as P

WIDTH = 768
HEADS = 12
HEAD_DIM = 64
SLABS = 4
BUCKET = 512
CHUNK = 256
PAIR = 2 * HEAD_DIM
PAIRS = HEADS // 2
WEIGHT_ROWS = WIDTH * (4 + 2 * SLABS)
QKV_ROWS = 3 * WIDTH
VECTOR_ROWS = 12
RANK = 8
FORBIDDEN = -1e30
EPS = 1e-5
FIRST_ATTENTION_MIB = 28
EVAL_ATTENTION_MIB = 24
TRAIN_REST_MIB = 40
EVAL_TAIL_MIB = 28
WINDOW_MIB = 16
REST_ROWS = WEIGHT_ROWS - QKV_ROWS
UP_AT = WIDTH
DOWN_AT = WIDTH * (1 + SLABS)
TAIL_ROWS = 32
PAD_ROWS = 16
A_AT = 16
LANES = 128

f32 = jnp.float32
bf16 = jnp.bfloat16

BQ, BV, BO, B1, B2, G1, C1, G2, C2 = 0, 1, 2, 3, 7, 8, 9, 10, 11


def dot(left, right):
    return jnp.dot(left, right, preferred_element_type=f32)


def dot_last(left, right):
    return lax.dot_general(left, right, (((1,), (1,)), ((), ())), preferred_element_type=f32)


def dot_first(left, right):
    return lax.dot_general(left, right, (((0,), (0,)), ((), ())), preferred_element_type=f32)


def row(tail_ref, at):
    return tail_ref[:A_AT].astype(f32)[at : at + 1]


def adapter(tail_ref, which):
    return tail_ref[A_AT:].astype(f32)[RANK * which : RANK * (which + 1)].astype(bf16)


def normalise(resid):
    centred = resid - jnp.mean(resid, axis=-1, keepdims=True)
    scale = lax.rsqrt(jnp.mean(centred * centred, axis=-1, keepdims=True) + EPS)
    return centred * scale, scale


def normalise_back(grad, normed, scale):
    return scale * (
        grad
        - jnp.mean(grad, axis=-1, keepdims=True)
        - normed * jnp.mean(grad * normed, axis=-1, keepdims=True)
    )


def half_error_function(value):
    return 0.5 + 0.5 * lax.erf(value * 0.7071067811865476)


def gelu(value):
    return value * half_error_function(value)


def gelu_slope(value):
    density = jnp.exp(value * value * -0.5) * 0.3989422804014327
    return half_error_function(value) + value * density


def low_lanes(rows):
    return lax.broadcasted_iota(jnp.int32, (rows, PAIR), 1) < HEAD_DIM


def head_stack(pair):
    low = low_lanes(pair.shape[0])
    zero = jnp.zeros_like(pair)
    return jnp.concatenate([jnp.where(low, pair, zero), jnp.where(low, zero, pair)], axis=0)


def item_masks(counts_ref, lengths_ref):
    position = lax.broadcasted_iota(jnp.int32, (BUCKET, 128), 0)
    column = lax.broadcasted_iota(jnp.int32, (BUCKET, 128), 1)
    start = jnp.zeros((BUCKET, 128), jnp.int32)
    finish = jnp.zeros((BUCKET, 128), jnp.int32)
    valid = jnp.zeros((BUCKET, 128), jnp.int32)
    base = jnp.int32(0)
    first = jnp.int32(0)
    for level in range(counts_ref.shape[1]):
        extent = BUCKET >> level
        count = counts_ref[0, level]
        inside = (column >= first) & (column < first + count)
        here = base + (column - first) * extent
        start = jnp.where(inside, here, start)
        finish = jnp.where(inside, here + extent, finish)
        base = base + count * extent
        first = first + count
    for slot in range(lengths_ref.shape[1]):
        valid = jnp.where(column == slot, lengths_ref[0, slot], valid)
    member = (position >= start) & (position < finish)
    allowed = member & (position < start + valid)
    return (
        jnp.where(member, 1.0, 0.0).astype(bf16),
        jnp.where(allowed, 0.0, FORBIDDEN).astype(bf16),
    )


def attend(q_s, k_s, v_s, query_mask, key_mask, put):
    rows = q_s.shape[0]
    ones = jnp.ones((rows, 128), bf16)
    masks = jnp.concatenate([query_mask, query_mask], axis=0)
    low = low_lanes(rows)

    def scores_of(pair):
        at = slice(PAIR * pair, PAIR * (pair + 1))
        left = jnp.concatenate([head_stack(q_s[:, at]), masks], axis=1)
        return dot_last(left, jnp.concatenate([k_s[:, at], key_mask], axis=1))

    scores = scores_of(0)
    for pair in range(PAIRS):
        later = scores_of(pair + 1) if pair + 1 < PAIRS else None
        at = slice(PAIR * pair, PAIR * (pair + 1))
        top = jnp.max(scores, axis=-1, keepdims=True)
        weights = jnp.exp(scores - top).astype(bf16)
        mixed = dot(weights, jnp.concatenate([v_s[:, at], ones], axis=1))
        mixed = mixed[:, :PAIR] / mixed[:, PAIR:]
        put(at, jnp.where(low, mixed[:rows], mixed[rows:]).astype(bf16))
        scores = later


def start_qkv(table_ref, refs, w, sem, tail=None, tail_sem=None):
    if len(refs) == 2:
        pltpu.make_async_copy(refs[0], w, sem).start()
        if tail is not None:
            pltpu.make_async_copy(refs[1], tail, tail_sem).start()
        return
    units = len(refs) // 2
    size = refs[0].shape[0]

    def start(chosen):
        for i, ref in enumerate(chosen):
            to = pl.multiple_of(table_ref[i] * size, 16)
            pltpu.make_async_copy(ref.at[pl.ds(0, size)], w.at[pl.ds(to, size)], sem).start()

    if tail is not None:
        for i, ref in enumerate(refs[units:]):

            @pl.when(table_ref[i] == 0)
            def _():
                rows = ref.at[pl.ds(size, TAIL_ROWS)]
                pltpu.make_async_copy(rows, tail, tail_sem).start()

    @pl.when(table_ref[units] == 0)
    def _():
        start(refs[:units])

    @pl.when(table_ref[units] != 0)
    def _():
        start(refs[units:])


def wait_all(ref, sem):
    pltpu.make_async_copy(ref, ref, sem).wait()


def start_rest(table_ref, refs, w, sems):
    units = len(refs) // 3
    size = refs[-1].shape[1] if units else w.shape[0]

    def start(ref, at):
        to = pl.multiple_of(at * size, 16)
        pltpu.make_async_copy(ref, w.at[pl.ds(to, size)], sems.at[at]).start()

    if units:

        @pl.when(table_ref[3 * units] == 0)
        def _():
            for i in range(units):
                start(refs[units + i].at[pl.ds(0, size)], table_ref[i])

        @pl.when(table_ref[3 * units] != 0)
        def _():
            for i in range(units):
                start(refs[i].at[pl.ds(0, size)], table_ref[i])

        for i in range(units):
            for slot in range(2):
                start(refs[2 * units + i].at[slot], table_ref[units + 2 * i + slot])
    else:
        start(refs[0], 0)

    waiting = set(range(w.shape[0] // size))

    def ready(first, last):
        for at in range(first // size, (last - 1) // size + 1):
            if at in waiting:
                waiting.remove(at)
                wait_all(w.at[pl.ds(at * size, size)], sems.at[at])

    return ready


def slabs_of_columns(w, lanes):
    rows = slice(UP_AT, DOWN_AT)
    for at in range(0, WIDTH, LANES):
        lanes[...] = w[rows, at : at + LANES].astype(f32)
        for slab in range(SLABS):
            to = UP_AT + WIDTH * slab
            part = lanes[pl.ds(slab, WIDTH, stride=SLABS), :]
            w[to : to + WIDTH, at : at + LANES] = part.astype(bf16)


def project_and_attend(x, weights, biases, low, masks, q_s, k_s, v_s, ctx_ref):
    q = dot(x, weights[0]) + biases[0] + low[0]
    q_s[...] = (q.astype(bf16).astype(f32) * HEAD_DIM**-0.5).astype(bf16)
    k_s[...] = dot(x, weights[1]).astype(bf16)
    v_s[...] = (dot(x, weights[2]) + biases[1] + low[1]).astype(bf16)

    def put(at, value):
        ctx_ref[:, at] = value

    attend(q_s, k_s, v_s, *masks, put)


def eval_block(lengths_ref, at, x_ref, tail_ref, w, merged, ctx_ref, q_s, k_s, v_s):
    position = lax.broadcasted_iota(jnp.int32, (BUCKET, LANES), 0)
    column = lax.broadcasted_iota(jnp.int32, (BUCKET, LANES), 1)
    key_mask = jnp.where((column > 0) | (position < lengths_ref[at]), 0.0, FORBIDDEN).astype(bf16)
    query_mask = jnp.where(column == 0, 1.0, 0.0).astype(bf16)
    project_and_attend(
        x_ref[...],
        (merged[:WIDTH], w[WIDTH : 2 * WIDTH], merged[WIDTH:]),
        (row(tail_ref, BQ), row(tail_ref, BV)),
        (0.0, 0.0),
        (query_mask, key_mask),
        q_s, k_s, v_s, ctx_ref,
    )


def first_attention_kernel(
    counts_ref, lengths_ref, eval_lengths_ref, table_ref, x_ref, eval_x_ref, bq_ref, bv_ref, *refs
):
    *refs, ctx_ref, q_ref, k_ref, v_ref, q_s, k_s, v_s, sems = refs
    *refs, tail_ref, eval_ctx_ref, w, merged_ref = refs
    w_refs, outs = refs[:-4], refs[-4:]
    step = pl.program_id(0)
    keep = [
        pltpu.make_async_copy(ref, out, sems.at[2 + i])
        for i, (ref, out) in enumerate(zip((ctx_ref, q_ref, k_ref, v_ref), outs))
    ]

    @pl.when(step == 0)
    def _():
        start_qkv(table_ref, w_refs, w, sems.at[0], tail_ref, sems.at[1])
        masks = item_masks(counts_ref, lengths_ref)
        x = x_ref[...]
        wait_all(tail_ref, sems.at[1])
        aq = dot_last(x, adapter(tail_ref, 0)).astype(bf16)
        av = dot_last(x, adapter(tail_ref, 1)).astype(bf16)
        wait_all(w, sems.at[0])
        for which, b_ref in enumerate((bq_ref, bv_ref)):
            rows = slice(2 * WIDTH * which, 2 * WIDTH * which + WIDTH)
            merged = w[rows].astype(f32) + 2.0 * dot_first(adapter(tail_ref, which), b_ref[...])
            merged_ref[WIDTH * which : WIDTH * (which + 1)] = merged.astype(bf16)
        project_and_attend(
            x,
            (w[:WIDTH], w[WIDTH : 2 * WIDTH], w[2 * WIDTH :]),
            (row(tail_ref, BQ), row(tail_ref, BV)),
            (2.0 * dot(aq, bq_ref[...]), 2.0 * dot(av, bv_ref[...])),
            masks,
            q_ref, k_ref, v_ref, ctx_ref,
        )
        for copy in keep:
            copy.start()

    @pl.when(step > 0)
    def _():
        eval_block(
            eval_lengths_ref, step - 1, eval_x_ref, tail_ref, w, merged_ref, eval_ctx_ref, q_s, k_s, v_s
        )

    @pl.when(step == pl.num_programs(0) - 1)
    def _():
        for copy in keep:
            copy.wait()


def eval_attention_kernel(
    lengths_ref, x_ref, tail_ref, w, merged, ctx_ref, q_s, k_s, v_s, *, first
):
    at = first + pl.program_id(0)
    eval_block(lengths_ref, at, x_ref, tail_ref, w, merged, ctx_ref, q_s, k_s, v_s)


def up_weight(w, slab, at):
    return w[UP_AT + WIDTH * slab : UP_AT + WIDTH * (slab + 1), at : at + CHUNK]


def down_weight(w, slab, at):
    rows = DOWN_AT + WIDTH * slab + at
    return w[rows : rows + CHUNK]


def feed_forward(h1, tail_ref, w, keep):
    chunks = [(slab, at) for slab in range(SLABS) for at in range(0, WIDTH, CHUNK)]

    def up(slab, at):
        u = dot(h1, up_weight(w, slab, at)) + row(tail_ref, B1 + slab)[:, at : at + CHUNK]
        keep(slab, at, u)
        return u

    total = None
    u = up(*chunks[0])
    for i, (slab, at) in enumerate(chunks):
        later = up(*chunks[i + 1]) if i + 1 < len(chunks) else None
        part = dot(gelu(u).astype(bf16), down_weight(w, slab, at))
        total = part if total is None else total + part
        u = later
    return total


def eval_tail_kernel(x_ref, ctx_ref, tail_ref, w, *refs):
    out_ref = refs[-1]
    resid = x_ref[...].astype(f32) + (dot(ctx_ref[...], w[:WIDTH]) + row(tail_ref, BO))
    normed, _ = normalise(resid)
    h1 = (normed * row(tail_ref, G1) + row(tail_ref, C1)).astype(bf16)
    down = feed_forward(h1, tail_ref, w, lambda slab, at, u: None)
    normed, _ = normalise(h1.astype(f32) + (down + row(tail_ref, B2)))
    out_ref[...] = (normed * row(tail_ref, G2) + row(tail_ref, C2)).astype(bf16)


def attention_back(q_ref, k_ref, v_ref, dctx, masks, dq_s, dk_s, dv_s):
    query_mask, key_mask = masks
    rows = q_ref.shape[0]
    masks = jnp.concatenate([query_mask, query_mask], axis=0)

    def products(pair):
        at = slice(PAIR * pair, PAIR * (pair + 1))
        q2, k, d2 = head_stack(q_ref[:, at]), k_ref[:, at], head_stack(dctx[:, at])
        scores = dot_last(
            jnp.concatenate([k, key_mask], axis=1), jnp.concatenate([q2, masks], axis=1)
        )
        return scores, dot_last(v_ref[:, at], d2), q2, k, d2

    now = products(0)
    for pair in range(PAIRS):
        later = products(pair + 1) if pair + 1 < PAIRS else None
        scores, grad_probs, q2, k, d2 = now
        at = slice(PAIR * pair, PAIR * (pair + 1))
        rounded, grad_scores = [], []
        for head in (slice(0, rows), slice(rows, 2 * rows)):
            probs = jnp.exp(scores[:, head] - jnp.max(scores[:, head], axis=0, keepdims=True))
            probs = probs * (1.0 / jnp.sum(probs, axis=0, keepdims=True))
            rounded.append(probs.astype(bf16))
            weighted = probs * grad_probs[:, head]
            inner = jnp.sum(weighted, axis=0, keepdims=True)
            grad_scores.append((weighted - probs * inner).astype(bf16))
        rounded = jnp.concatenate(rounded, axis=1)
        grad_scores = jnp.concatenate(grad_scores, axis=1)
        dv_s[:, at] = dot(rounded, d2).astype(bf16)
        dk_s[:, at] = dot(grad_scores, q2).astype(bf16)
        crossed = dot_first(k, grad_scores)
        dq = jnp.concatenate([crossed[:HEAD_DIM, :rows], crossed[HEAD_DIM:, rows:]], axis=0)
        dq_s[:, at] = (dq.T * HEAD_DIM**-0.5).astype(bf16)
        now = later


def train_kernel(
    counts_ref, lengths_ref, rest_table_ref, x_ref, q_any, k_any, v_any, ctx_ref, grad_any,
    tail_ref, bq_ref, bv_ref, wqkv_any, *refs,
):
    *refs, q_ref, k_ref, v_ref, grad_ref, out_ref, dq_s, dk_s, dv_s, sems = refs
    *w_refs, out_any, token_ref, sums_ref, w, wqkv, lanes, u_s = refs
    if len(w_refs) > 1:
        end = w_refs[-8:]
        w_refs = [*w_refs[:-8], *end[:3], end[6], *end[3:6], end[7]]
    ready = start_rest(rest_table_ref, w_refs, w, sems.at[pl.ds(5, 24)])
    later_in = [
        pltpu.make_async_copy(any_ref, ref, sems.at[i])
        for i, (any_ref, ref) in enumerate(
            ((grad_any, grad_ref), (q_any, q_ref), (k_any, k_ref), (v_any, v_ref))
        )
    ]
    last_in = pltpu.make_async_copy(wqkv_any, wqkv, sems.at[29])
    x = x_ref[...]
    aq = dot_last(x, adapter(tail_ref, 0)).astype(bf16)
    av = dot_last(x, adapter(tail_ref, 1)).astype(bf16)

    ready(0, WIDTH)
    resid = x.astype(f32) + (dot(ctx_ref[...], w[:WIDTH]) + row(tail_ref, BO))
    normed_one, scale_one = normalise(resid)
    h1 = (normed_one * row(tail_ref, G1) + row(tail_ref, C1)).astype(bf16)

    def keep(slab, at, u):
        u_s[slab, :, at : at + CHUNK] = u

    ready(UP_AT, DOWN_AT)
    if len(w_refs) > 1:
        slabs_of_columns(w, lanes)
    ready(DOWN_AT, REST_ROWS)
    for copy in [*later_in, last_in]:
        copy.start()
    down = feed_forward(h1, tail_ref, w, keep)
    normed_two, scale_two = normalise(h1.astype(f32) + (down + row(tail_ref, B2)))
    out_ref[...] = (normed_two * row(tail_ref, G2) + row(tail_ref, C2)).astype(bf16)
    keep_out = pltpu.make_async_copy(out_ref, out_any, sems.at[4])
    keep_out.start()

    for copy in later_in:
        copy.wait()
    grad_two = normalise_back(grad_ref[...].astype(f32) * row(tail_ref, G2), normed_two, scale_two)
    df = grad_two.astype(bf16)
    chunks = [(slab, at) for slab in range(SLABS) for at in range(0, WIDTH, CHUNK)]
    total = None
    grad_gelu = dot_last(df, down_weight(w, *chunks[0]))
    for i, (slab, at) in enumerate(chunks):
        later = dot_last(df, down_weight(w, *chunks[i + 1])) if i + 1 < len(chunks) else None
        du = (grad_gelu * gelu_slope(u_s[slab, :, at : at + CHUNK])).astype(bf16)
        part = dot_last(du, up_weight(w, slab, at))
        total = part if total is None else total + part
        grad_gelu = later
    dh1 = (grad_two + total).astype(bf16)
    grad_one = normalise_back(dh1.astype(f32) * row(tail_ref, G1), normed_one, scale_one)
    token_ref[...] = grad_one
    dctx = dot_last(grad_one.astype(bf16), w[:WIDTH]).astype(bf16)
    attention_back(q_ref, k_ref, v_ref, dctx, item_masks(counts_ref, lengths_ref), dq_s, dk_s, dv_s)

    last_in.wait()
    dq, dk, dv = dq_s[...], dk_s[...], dv_s[...]
    daq = (2.0 * dot_last(dq, bq_ref[...])).astype(bf16)
    dav = (2.0 * dot_last(dv, bv_ref[...])).astype(bf16)
    sums_ref[:RANK] = 2.0 * dot_first(aq, dq)
    sums_ref[RANK:] = 2.0 * dot_first(av, dv)
    token_ref[...] += (
        dot_last(dq, wqkv[:WIDTH])
        + dot_last(dk, wqkv[WIDTH : 2 * WIDTH])
        + dot_last(dv, wqkv[2 * WIDTH :])
        + dot(daq, adapter(tail_ref, 0))
        + dot(dav, adapter(tail_ref, 1))
    )
    keep_out.wait()


def window_kernel(place_ref, before_ref, own_ref, out_ref, padded_ref, flat, moved):
    ahead = before_ref.shape[0]
    flat[:ahead] = before_ref[...].astype(f32)
    flat[ahead : ahead + own_ref.shape[0]] = own_ref[...].astype(f32)
    flat[ahead + own_ref.shape[0] :] = jnp.zeros((LANES, LANES), f32)
    rows = moved.shape[0]
    start, turn = place_ref[0], place_ref[1]
    back = lax.rem(LANES - turn, LANES)
    here = pltpu.roll(flat[pl.ds(start, rows), :], back, 1)
    after = pltpu.roll(flat[pl.ds(start + 1, rows), :], back, 1)
    lane = lax.broadcasted_iota(jnp.int32, (rows, LANES), 1)
    moved[...] = jnp.where(lane < LANES - turn, here, after)
    per_row = WIDTH // LANES
    for tile in range(per_row):
        part = moved[pl.ds(tile, rows // per_row, stride=per_row), :]
        at = slice(LANES * tile, LANES * (tile + 1))
        out_ref[:, at] = part.astype(bf16)
        padded_ref[: rows // per_row, at] = part.astype(bf16)
    padded_ref[rows // per_row :] = jnp.zeros((PAD_ROWS, WIDTH), bf16)


def whole(shape):
    return pl.BlockSpec(shape, lambda *_: (0,) * len(shape))


def cost(microseconds):
    return pl.CostEstimate(flops=int(microseconds * 1e9), bytes_accessed=0, transcendentals=0)


def stays(value):
    return pltpu.with_memory_space_constraint(value, pltpu.VMEM)


def after(value, *others):
    return lax.optimization_barrier((value, *others))[0]


ANY = pl.BlockSpec(memory_space=pl.ANY)
IN_VMEM = pl.BlockSpec(memory_space=pltpu.VMEM)
SCALARS = pl.BlockSpec(memory_space=pltpu.SMEM)


def params(mebibytes):
    return pltpu.CompilerParams(vmem_limit_bytes=mebibytes * 2**20)


def first_attention(counts, lengths, eval_lengths, table, x, eval_x, bq, bv, w, count):
    shape = (x.shape[0], WIDTH)
    eval_shape = (count * BUCKET, WIDTH)
    block = pl.BlockSpec((BUCKET, WIDTH), lambda i: (jnp.maximum(i - 1, 0), 0))
    return pl.pallas_call(
        first_attention_kernel,
        in_specs=[SCALARS] * 4
        + [whole(x.shape), block, whole(bq.shape), whole(bv.shape)]
        + [ANY] * len(w),
        out_specs=[ANY] * 4 + [whole((TAIL_ROWS, WIDTH)), block, IN_VMEM, IN_VMEM],
        out_shape=[pltpu.HBM(shape, bf16)] * 4
        + [jax.ShapeDtypeStruct((TAIL_ROWS, WIDTH), bf16), pltpu.HBM(eval_shape, bf16)]
        + [pltpu.VMEM((n, WIDTH), bf16) for n in (QKV_ROWS, 2 * WIDTH)],
        grid=(1 + count,),
        scratch_shapes=[pltpu.VMEM(shape, bf16)] * 4
        + [pltpu.VMEM((BUCKET, WIDTH), bf16)] * 3
        + [pltpu.SemaphoreType.DMA((6,))],
        compiler_params=params(FIRST_ATTENTION_MIB),
        cost_estimate=cost(10 + 7 * count),
        name="first_attention",
    )(counts, lengths, eval_lengths, table, x, eval_x, bq, bv, *w)


def eval_attention(lengths, x, tail, w, merged, first, count):
    return pl.pallas_call(
        functools.partial(eval_attention_kernel, first=first),
        in_specs=[
            SCALARS,
            pl.BlockSpec((BUCKET, WIDTH), lambda i: (i + first, 0)),
            whole(tail.shape),
            IN_VMEM,
            IN_VMEM,
        ],
        out_specs=pl.BlockSpec((BUCKET, WIDTH), lambda i: (i, 0)),
        out_shape=jax.ShapeDtypeStruct((count * BUCKET, WIDTH), bf16),
        grid=(count,),
        scratch_shapes=[pltpu.VMEM((BUCKET, WIDTH), bf16)] * 3,
        compiler_params=params(EVAL_ATTENTION_MIB),
        cost_estimate=cost(1 + 7 * count),
        name="eval_attention",
    )(lengths, x, tail, stays(w), stays(merged))


def eval_tail(x, ctx, tail, w, first, done=None):
    rows = ctx.shape[0]
    given = [] if done is None else [done]
    return pl.pallas_call(
        eval_tail_kernel,
        in_specs=[
            pl.BlockSpec((BUCKET, WIDTH), lambda i: (i + first, 0)),
            pl.BlockSpec((BUCKET, WIDTH), lambda i: (i, 0)),
            whole(tail.shape),
            IN_VMEM,
        ]
        + [ANY] * len(given),
        out_specs=pl.BlockSpec((BUCKET, WIDTH), lambda i: (i + first, 0)),
        out_shape=jax.ShapeDtypeStruct(x.shape, bf16),
        grid=(rows // BUCKET,),
        input_output_aliases={4: 0} if given else {},
        compiler_params=params(EVAL_TAIL_MIB),
        cost_estimate=cost(3 + 8 * (rows // BUCKET)),
        name="eval_tail",
    )(x, ctx, tail, stays(w), *given)


def train_rest(counts, lengths, rest_table, x, q, k, v, ctx, grad, tail, bq, bv, w, rest):
    rows = x.shape[0]
    shape = (rows, WIDTH)
    return pl.pallas_call(
        train_kernel,
        in_specs=[SCALARS] * 3
        + [whole(shape), ANY, ANY, ANY, whole(shape), ANY]
        + [whole(v.shape) for v in (tail, bq, bv)]
        + [ANY]
        + ([ANY] * (len(rest) - 2) + [IN_VMEM] * 2 if len(rest) > 1 else [ANY]),
        out_specs=[ANY, whole(shape), whole((2 * RANK, WIDTH)), IN_VMEM],
        out_shape=[
            jax.ShapeDtypeStruct(shape, bf16),
            jax.ShapeDtypeStruct(shape, f32),
            jax.ShapeDtypeStruct((2 * RANK, WIDTH), f32),
            pltpu.VMEM((REST_ROWS, WIDTH), bf16),
        ],
        grid=(1,),
        scratch_shapes=[
            pltpu.VMEM((QKV_ROWS, WIDTH), bf16),
            pltpu.VMEM((SLABS * WIDTH, LANES), f32),
            pltpu.VMEM((SLABS, rows, WIDTH), f32),
            *[pltpu.VMEM(shape, bf16)] * 8,
            pltpu.SemaphoreType.DMA((30,)),
        ],
        compiler_params=params(TRAIN_REST_MIB),
        cost_estimate=cost(36),
        name="train_rest",
    )(counts, lengths, rest_table, x, q, k, v, ctx, grad, tail, bq, bv, w, *rest)


def window(start, turn, before, own, rows):
    ahead = before.shape[0]
    place = jnp.stack([start, turn]).astype(jnp.int32)
    return pl.pallas_call(
        window_kernel,
        in_specs=[SCALARS, whole(before.shape), whole(own.shape)],
        out_specs=[whole((rows, WIDTH)), whole((rows + PAD_ROWS, WIDTH))],
        out_shape=[
            jax.ShapeDtypeStruct((rows, WIDTH), bf16),
            jax.ShapeDtypeStruct((rows + PAD_ROWS, WIDTH), bf16),
        ],
        grid=(1,),
        scratch_shapes=[
            pltpu.VMEM((ahead + own.shape[0] + LANES, LANES), f32),
            pltpu.VMEM((rows * (WIDTH // LANES), LANES), f32),
        ],
        compiler_params=params(WINDOW_MIB),
        cost_estimate=cost(2),
        name="window",
    )(place, before, own)


AXES = ("fsdp", "rep")


def tail_rows(flat):
    at = VECTOR_ROWS * WIDTH
    vectors = jnp.pad(flat[:at].reshape(VECTOR_ROWS, WIDTH), ((0, A_AT - VECTOR_ROWS), (0, 0)))
    a = flat[at:].reshape(2, WIDTH, RANK).transpose(0, 2, 1).reshape(2 * RANK, WIDTH)
    return jnp.concatenate([vectors, a])


def collect_generic(frozen, devices):
    me = lax.axis_index(AXES)
    share = WEIGHT_ROWS // devices
    extra = frozen.shape[0] - share * WIDTH
    spill = extra * devices
    before = lax.ppermute(frozen[-spill:], AXES, [(d, (d + 1) % devices) for d in range(devices)])
    flat = lax.dynamic_slice(
        jnp.concatenate([before, frozen]), (spill - extra * me,), (share * WIDTH,)
    )
    gathered = lax.all_gather(flat.reshape(share, WIDTH), AXES, axis=0, tiled=True)
    tail = lax.psum(jnp.where(me == devices - 1, frozen[-spill:].astype(f32), 0.0), AXES)
    w1 = gathered[QKV_ROWS + WIDTH : QKV_ROWS + WIDTH * (1 + SLABS)]
    w1 = w1.reshape(WIDTH, SLABS, WIDTH).transpose(1, 0, 2).reshape(WIDTH * SLABS, WIDTH)
    rest = jnp.concatenate(
        [gathered[QKV_ROWS : QKV_ROWS + WIDTH], w1, gathered[QKV_ROWS + WIDTH * (1 + SLABS) :]]
    )
    none = jnp.zeros((8,), jnp.int32)
    return none, [gathered[:QKV_ROWS], tail_rows(tail.astype(bf16))], none, [rest]


def device(z, x, y, core):
    return ((z * 2 + x) * 2 + y) * 2 + core


PLANE = [(x, y, core) for x in range(2) for y in range(2) for core in range(2)]
EVERY = [(z, *p) for z in range(4) for p in PLANE]


def along_z(value, pairs):
    return lax.ppermute(
        value, AXES, [(device(a, *p), device(b, *p)) for a, b in pairs for p in PLANE]
    )


def first_way(value):
    return lax.ppermute(
        value, AXES,
        [(device(z, x, y, c), device(z, x ^ (1 - c), y ^ c, c)) for z, x, y, c in EVERY],
    )


def second_way(value):
    return lax.ppermute(
        value, AXES,
        [(device(z, x, y, c), device(z, x ^ c, y ^ (1 - c), c)) for z, x, y, c in EVERY],
    )


def sibling(value):
    return lax.ppermute(
        value, AXES, [(device(z, x, y, c), device(z, x, y, 1 - c)) for z, x, y, c in EVERY]
    )


def collect(frozen, query_b, value_b):
    me = lax.axis_index(AXES)
    z, core = me // 8, me % 2
    chip = me // 2
    share = WEIGHT_ROWS // 32
    extra = frozen.shape[0] - share * WIDTH
    spill = extra * 32
    padded = -(-frozen.shape[0] // 1024) * 1024
    own = jnp.pad(frozen, (0, padded - frozen.shape[0])).reshape(padded // LANES, LANES)
    first = spill - extra * me
    start, turn = first // LANES, first % LANES

    plane = chip % 4
    one, two = jnp.where(core == 0, 2, 1), jnp.where(core == 0, 1, 2)
    mine_at = jnp.stack([plane, plane ^ one, plane ^ two, plane ^ 3]) * 2 + core
    other_at = jnp.stack([plane, plane ^ two, plane ^ one, plane ^ 3]) * 2 + 1 - core
    at = jnp.concatenate([mine_at, other_at]).astype(jnp.int32)
    flag = z[None].astype(jnp.int32)
    level = jnp.stack([jnp.maximum(z, 1), jnp.where(z == 2, 3, 2), jnp.where(z < 2, 3, 1)])
    level = level.astype(jnp.int32)

    last_rows = frozen[-spill:]
    before = lax.ppermute(last_rows, AXES, [(d, d + 1) for d in range(31)])
    mine, padded = window(start, turn, before.reshape(spill // LANES, LANES), own, share)

    last_rows, query_b, value_b, at, flag, level = lax.optimization_barrier(
        (last_rows, query_b, value_b, at, flag, level, mine)
    )[:-1]
    tail = tail_rows(
        lax.ppermute(last_rows, AXES, [(31, device(0, 0, 0, 0))])
        + lax.ppermute(last_rows, AXES, [(31, device(2, 0, 0, 0))])
    )
    bq, bv = query_b.astype(bf16), value_b.astype(bf16)
    table = jnp.concatenate([at, flag])
    codes = jnp.stack([at + 8 * (level[1] - 1), at + 8 * (level[2] - 1)], axis=1).reshape(-1)
    rest_table = jnp.concatenate([at + 8 * (level[0] - 1), codes, flag])

    up_two = along_z(padded, [(0, 2), (2, 3)])
    near = [mine, first_way(mine), second_way(mine)]
    down_one = along_z(mine, [(1, 0), (2, 1), (3, 2)])

    up = jnp.concatenate([jnp.where(z == 2, up_two[:share], mine), tail])
    up_one = along_z(up, [(0, 1), (1, 2), (2, 3)])
    near[1], down_one = lax.optimization_barrier((near[1], down_one, up))[:2]
    near.append(second_way(near[1]))
    down_two = along_z(down_one, [(1, 0), (2, 1)])
    up_one, down_two, near[3] = lax.optimization_barrier((up_one, down_two, near[3]))

    far = [
        jnp.where(z == 0, jnp.concatenate([down_one, tail]), jnp.where(z == 2, up, up_one))
    ]
    far += [first_way(far[0]), second_way(far[0])]
    ends = along_z(jnp.where(z == 1, down_two, up_one[:share]), [(1, 0), (2, 3)])
    near_other = [sibling(v) for v in near]
    bq, bv, table, rest_table, *ready = lax.optimization_barrier(
        (bq, bv, table, rest_table, *far, *near_other)
    )
    far, near_other = ready[:3], ready[3:]

    far.append(second_way(far[1]))
    far_other = [sibling(v) for v in far[:3]]
    last = jnp.stack(
        [
            jnp.where(z == 0, down_two, jnp.where(z == 3, up_two[:share], down_one)),
            jnp.where(z == 1, down_two, jnp.where(z == 2, up_one[:share], ends)),
        ]
    )
    far[3], last, *far_other = lax.optimization_barrier((far[3], last, *far_other))
    far_other.append(sibling(far[3]))
    projections = [*near, *near_other, *far, *far_other]
    last = [last, first_way(last), second_way(last)]
    return table, projections, rest_table, last, bq, bv


def other_planes(value, flip):
    return lax.ppermute(
        value, AXES, [(device(z, *p), device(z ^ flip, *p)) for z, *p in EVERY]
    )


def other_chips(value, flip_x, flip_y):
    return lax.ppermute(
        value, AXES,
        [(device(z, x, y, c), device(z, x ^ flip_x, y ^ flip_y, c)) for z, x, y, c in EVERY],
    )


def plane_total(value):
    value = value + sibling(value)
    along = value + other_chips(value, 1, 0)
    across = other_chips(value, 0, 1) + other_chips(value, 1, 1)
    return along + across


def planes_total(value):
    return (value + other_planes(value, 1)) + (other_planes(value, 2) + other_planes(value, 3))


def local(
    tokens,
    bucket_item_counts,
    slot_item_lengths,
    frozen,
    query_lowrank_matrix,
    value_lowrank_matrix,
    output_gradient,
    evaluation_tokens,
    evaluation_lengths,
    *,
    mesh,
):
    devices = mesh.shape["fsdp"] * mesh.shape["rep"]
    special = tuple(mesh.shape[axis] for axis in AXES) == (8, 4)
    if special:
        table, w, rest_table, last, bq, bv = collect(
            frozen, query_lowrank_matrix, value_lowrank_matrix
        )
    else:
        table, w, rest_table, rest = collect_generic(frozen, devices)
        bq, bv = query_lowrank_matrix.astype(bf16), value_lowrank_matrix.astype(bf16)
    counts, lengths = bucket_item_counts, slot_item_lengths
    blocks = evaluation_tokens.shape[0] // BUCKET

    x = evaluation_tokens
    most = blocks - blocks // 2
    ctx, q, k, v, tail, first_ctx, w_qkv, merged = first_attention(
        counts, lengths, evaluation_lengths, table, tokens, x, bq, bv, w, most
    )
    if special:
        last = list(lax.optimization_barrier((*last, first_ctx))[:3])
        x = after(x, *last)
        last.append(second_way(last[1]))
        other = [sibling(v) for v in last[:3]]
    last_ctx = eval_attention(
        evaluation_lengths, x, tail, w_qkv, merged, most, blocks - most
    )
    eval_ctx = [first_ctx, last_ctx]
    if special:
        last[3] = after(last[3], last_ctx)
        rest = w + last[:3] + other + [stays(last[3]), stays(sibling(last[3]))]
    grad = after(output_gradient, *eval_ctx)
    out, token_gradient, sums, w_rest = train_rest(
        counts, lengths, rest_table, tokens, q, k, v, ctx, grad, tail, bq, bv, w_qkv, rest
    )
    eval_in = [after(c, sums) for c in eval_ctx]
    eval_out = eval_tail(evaluation_tokens, eval_in[0], tail, w_rest, 0)
    second = eval_in[1]
    if special:
        sums = plane_total(sums)
        second = after(second, sums, eval_out)
    eval_out = eval_tail(evaluation_tokens, second, tail, w_rest, most, eval_out)
    sums = planes_total(sums) if special else lax.psum(sums, AXES)
    gq, gv = sums[:RANK], sums[RANK:]
    return out, token_gradient, gq, gv, eval_out


def solution(mesh):
    split = P(("fsdp", "rep"), None)
    flat = P(("fsdp", "rep"))
    return jax.shard_map(
        functools.partial(local, mesh=mesh),
        mesh=mesh,
        in_specs=(split, split, split, flat, P(), P(), split, split, flat),
        out_specs=(split, split, P(), P(), split),
        check_vma=False,
    )
```

```python
import functools

import jax
import jax.numpy as jnp
from jax import lax
from jax.experimental import pallas as pl
from jax.experimental.pallas import tpu as pltpu
from jax.sharding import PartitionSpec as P

WIDTH = 768
HEADS = 12
HEAD_DIM = 64
SLABS = 4
BUCKET = 512
CHUNK = 256
PAIR = 2 * HEAD_DIM
PAIRS = HEADS // 2
WEIGHT_ROWS = WIDTH * (4 + 2 * SLABS)
QKV_ROWS = 3 * WIDTH
VECTOR_ROWS = 12
RANK = 8
FORBIDDEN = -1e30
EPS = 1e-5
TRAIN_ATTENTION_MIB = 24
EVAL_ATTENTION_MIB = 24
TRAIN_REST_MIB = 40
EVAL_TAIL_MIB = 28
WINDOW_MIB = 16
REST_ROWS = WEIGHT_ROWS - QKV_ROWS
UP_AT = WIDTH
DOWN_AT = WIDTH * (1 + SLABS)
TAIL_ROWS = 32
PAD_ROWS = 16
A_AT = 16
LANES = 128

f32 = jnp.float32
bf16 = jnp.bfloat16

BQ, BV, BO, B1, B2, G1, C1, G2, C2 = 0, 1, 2, 3, 7, 8, 9, 10, 11


def dot(left, right):
    return jnp.dot(left, right, preferred_element_type=f32)


def dot_last(left, right):
    return lax.dot_general(left, right, (((1,), (1,)), ((), ())), preferred_element_type=f32)


def dot_first(left, right):
    return lax.dot_general(left, right, (((0,), (0,)), ((), ())), preferred_element_type=f32)


def row(tail_ref, at):
    return tail_ref[:A_AT].astype(f32)[at : at + 1]


def adapter(tail_ref, which):
    return tail_ref[A_AT:].astype(f32)[RANK * which : RANK * (which + 1)].astype(bf16)


def normalise(resid):
    centred = resid - jnp.mean(resid, axis=-1, keepdims=True)
    scale = lax.rsqrt(jnp.mean(centred * centred, axis=-1, keepdims=True) + EPS)
    return centred * scale, scale


def normalise_back(grad, normed, scale):
    return scale * (
        grad
        - jnp.mean(grad, axis=-1, keepdims=True)
        - normed * jnp.mean(grad * normed, axis=-1, keepdims=True)
    )


def half_error_function(value):
    return 0.5 + 0.5 * lax.erf(value * 0.7071067811865476)


def gelu(value):
    return value * half_error_function(value)


def gelu_slope(value):
    density = jnp.exp(value * value * -0.5) * 0.3989422804014327
    return half_error_function(value) + value * density


def low_lanes(rows):
    return lax.broadcasted_iota(jnp.int32, (rows, PAIR), 1) < HEAD_DIM


def head_stack(pair):
    low = low_lanes(pair.shape[0])
    zero = jnp.zeros_like(pair)
    return jnp.concatenate([jnp.where(low, pair, zero), jnp.where(low, zero, pair)], axis=0)


def item_masks(counts_ref, lengths_ref):
    position = lax.broadcasted_iota(jnp.int32, (BUCKET, 128), 0)
    column = lax.broadcasted_iota(jnp.int32, (BUCKET, 128), 1)
    start = jnp.zeros((BUCKET, 128), jnp.int32)
    finish = jnp.zeros((BUCKET, 128), jnp.int32)
    valid = jnp.zeros((BUCKET, 128), jnp.int32)
    base = jnp.int32(0)
    first = jnp.int32(0)
    for level in range(counts_ref.shape[1]):
        extent = BUCKET >> level
        count = counts_ref[0, level]
        inside = (column >= first) & (column < first + count)
        here = base + (column - first) * extent
        start = jnp.where(inside, here, start)
        finish = jnp.where(inside, here + extent, finish)
        base = base + count * extent
        first = first + count
    for slot in range(lengths_ref.shape[1]):
        valid = jnp.where(column == slot, lengths_ref[0, slot], valid)
    member = (position >= start) & (position < finish)
    allowed = member & (position < start + valid)
    return (
        jnp.where(member, 1.0, 0.0).astype(bf16),
        jnp.where(allowed, 0.0, FORBIDDEN).astype(bf16),
    )


def attend(q_s, k_s, v_s, query_mask, key_mask, put):
    rows = q_s.shape[0]
    ones = jnp.ones((rows, 128), bf16)
    masks = jnp.concatenate([query_mask, query_mask], axis=0)
    low = low_lanes(rows)

    def scores_of(pair):
        at = slice(PAIR * pair, PAIR * (pair + 1))
        left = jnp.concatenate([head_stack(q_s[:, at]), masks], axis=1)
        return dot_last(left, jnp.concatenate([k_s[:, at], key_mask], axis=1))

    scores = scores_of(0)
    for pair in range(PAIRS):
        later = scores_of(pair + 1) if pair + 1 < PAIRS else None
        at = slice(PAIR * pair, PAIR * (pair + 1))
        top = jnp.max(scores, axis=-1, keepdims=True)
        weights = jnp.exp(scores - top).astype(bf16)
        mixed = dot(weights, jnp.concatenate([v_s[:, at], ones], axis=1))
        mixed = mixed[:, :PAIR] / mixed[:, PAIR:]
        put(at, jnp.where(low, mixed[:rows], mixed[rows:]).astype(bf16))
        scores = later


def start_qkv(table_ref, refs, w, sem, tail=None, tail_sem=None):
    if len(refs) == 2:
        pltpu.make_async_copy(refs[0], w, sem).start()
        if tail is not None:
            pltpu.make_async_copy(refs[1], tail, tail_sem).start()
        return
    units = len(refs) // 2
    size = refs[0].shape[0]

    def start(chosen):
        for i, ref in enumerate(chosen):
            to = pl.multiple_of(table_ref[i] * size, 16)
            pltpu.make_async_copy(ref.at[pl.ds(0, size)], w.at[pl.ds(to, size)], sem).start()

    if tail is not None:
        for i, ref in enumerate(refs[units:]):

            @pl.when(table_ref[i] == 0)
            def _():
                rows = ref.at[pl.ds(size, TAIL_ROWS)]
                pltpu.make_async_copy(rows, tail, tail_sem).start()

    @pl.when(table_ref[units] == 0)
    def _():
        start(refs[:units])

    @pl.when(table_ref[units] != 0)
    def _():
        start(refs[units:])


def wait_all(ref, sem):
    pltpu.make_async_copy(ref, ref, sem).wait()


def start_rest(table_ref, refs, w, sems):
    units = len(refs) // 3
    size = refs[-1].shape[1] if units else w.shape[0]

    def start(ref, at):
        to = pl.multiple_of(at * size, 16)
        pltpu.make_async_copy(ref, w.at[pl.ds(to, size)], sems.at[at]).start()

    if units:

        @pl.when(table_ref[3 * units] == 0)
        def _():
            for i in range(units):
                start(refs[units + i].at[pl.ds(0, size)], table_ref[i])

        @pl.when(table_ref[3 * units] != 0)
        def _():
            for i in range(units):
                start(refs[i].at[pl.ds(0, size)], table_ref[i])

        for i in range(units):
            for slot in range(2):
                start(refs[2 * units + i].at[slot], table_ref[units + 2 * i + slot])
    else:
        start(refs[0], 0)

    waiting = set(range(w.shape[0] // size))

    def ready(first, last):
        for at in range(first // size, (last - 1) // size + 1):
            if at in waiting:
                waiting.remove(at)
                wait_all(w.at[pl.ds(at * size, size)], sems.at[at])

    return ready


def slabs_of_columns(w, lanes):
    rows = slice(UP_AT, DOWN_AT)
    for at in range(0, WIDTH, LANES):
        lanes[...] = w[rows, at : at + LANES].astype(f32)
        for slab in range(SLABS):
            to = UP_AT + WIDTH * slab
            part = lanes[pl.ds(slab, WIDTH, stride=SLABS), :]
            w[to : to + WIDTH, at : at + LANES] = part.astype(bf16)


def project(x, weights, biases, low, q_s, k_s, v_s):
    q = dot(x, weights[0]) + biases[0] + low[0]
    q_s[...] = (q.astype(bf16).astype(f32) * HEAD_DIM**-0.5).astype(bf16)
    k_s[...] = dot(x, weights[1]).astype(bf16)
    v_s[...] = (dot(x, weights[2]) + biases[1] + low[1]).astype(bf16)


def eval_block(lengths_ref, at, x_ref, tail_ref, w, merged, ctx_ref, q_s, k_s, v_s):
    position = lax.broadcasted_iota(jnp.int32, (BUCKET, LANES), 0)
    column = lax.broadcasted_iota(jnp.int32, (BUCKET, LANES), 1)
    key_mask = jnp.where((column > 0) | (position < lengths_ref[at]), 0.0, FORBIDDEN).astype(bf16)
    query_mask = jnp.where(column == 0, 1.0, 0.0).astype(bf16)
    project(
        x_ref[...],
        (merged[:WIDTH], w[WIDTH : 2 * WIDTH], merged[WIDTH:]),
        (row(tail_ref, BQ), row(tail_ref, BV)),
        (0.0, 0.0),
        q_s, k_s, v_s,
    )

    def put(at, value):
        ctx_ref[:, at] = value

    attend(q_s, k_s, v_s, query_mask, key_mask, put)


def train_attention_kernel(
    counts_ref, lengths_ref, table_ref, x_ref, bq_ref, bv_ref, *refs
):
    *refs, q_ref, k_ref, v_ref, sems = refs
    *refs, ctx_ref, tail_ref, w, merged_ref = refs
    w_refs, outs = refs[:-3], refs[-3:]
    start_qkv(table_ref, w_refs, w, sems.at[0], tail_ref, sems.at[1])
    masks = item_masks(counts_ref, lengths_ref)
    x = x_ref[...]
    wait_all(tail_ref, sems.at[1])
    aq = dot_last(x, adapter(tail_ref, 0)).astype(bf16)
    av = dot_last(x, adapter(tail_ref, 1)).astype(bf16)
    wait_all(w, sems.at[0])
    for which, b_ref in enumerate((bq_ref, bv_ref)):
        rows = slice(2 * WIDTH * which, 2 * WIDTH * which + WIDTH)
        merged = w[rows].astype(f32) + 2.0 * dot_first(adapter(tail_ref, which), b_ref[...])
        merged_ref[WIDTH * which : WIDTH * (which + 1)] = merged.astype(bf16)
    project(
        x,
        (w[:WIDTH], w[WIDTH : 2 * WIDTH], w[2 * WIDTH :]),
        (row(tail_ref, BQ), row(tail_ref, BV)),
        (2.0 * dot(aq, bq_ref[...]), 2.0 * dot(av, bv_ref[...])),
        q_ref, k_ref, v_ref,
    )
    keep = [
        pltpu.make_async_copy(ref, out, sems.at[2 + i])
        for i, (ref, out) in enumerate(zip((q_ref, k_ref, v_ref), outs))
    ]
    for copy in keep:
        copy.start()

    def put(at, value):
        ctx_ref[:, at] = value

    attend(q_ref, k_ref, v_ref, *masks, put)
    for copy in keep:
        copy.wait()


def eval_attention_kernel(
    lengths_ref, x_ref, tail_ref, w, merged, ctx_ref, q_s, k_s, v_s, *, first
):
    at = first + pl.program_id(0)
    eval_block(lengths_ref, at, x_ref, tail_ref, w, merged, ctx_ref, q_s, k_s, v_s)


def up_weight(w, slab, at):
    return w[UP_AT + WIDTH * slab : UP_AT + WIDTH * (slab + 1), at : at + CHUNK]


def down_weight(w, slab, at):
    rows = DOWN_AT + WIDTH * slab + at
    return w[rows : rows + CHUNK]


def feed_forward(h1, tail_ref, w, keep):
    chunks = [(slab, at) for slab in range(SLABS) for at in range(0, WIDTH, CHUNK)]

    def up(slab, at):
        u = dot(h1, up_weight(w, slab, at)) + row(tail_ref, B1 + slab)[:, at : at + CHUNK]
        keep(slab, at, u)
        return u

    total = None
    u = up(*chunks[0])
    for i, (slab, at) in enumerate(chunks):
        later = up(*chunks[i + 1]) if i + 1 < len(chunks) else None
        part = dot(gelu(u).astype(bf16), down_weight(w, slab, at))
        total = part if total is None else total + part
        u = later
    return total


def eval_tail_kernel(x_ref, ctx_ref, tail_ref, w, *refs):
    out_ref = refs[-1]
    resid = x_ref[...].astype(f32) + (dot(ctx_ref[...], w[:WIDTH]) + row(tail_ref, BO))
    normed, _ = normalise(resid)
    h1 = (normed * row(tail_ref, G1) + row(tail_ref, C1)).astype(bf16)
    down = feed_forward(h1, tail_ref, w, lambda slab, at, u: None)
    normed, _ = normalise(h1.astype(f32) + (down + row(tail_ref, B2)))
    out_ref[...] = (normed * row(tail_ref, G2) + row(tail_ref, C2)).astype(bf16)


def attention_back(q_ref, k_ref, v_ref, dctx, masks, dq_s, dk_s, dv_s):
    query_mask, key_mask = masks
    rows = q_ref.shape[0]
    masks = jnp.concatenate([query_mask, query_mask], axis=0)

    def products(pair):
        at = slice(PAIR * pair, PAIR * (pair + 1))
        q2, k, d2 = head_stack(q_ref[:, at]), k_ref[:, at], head_stack(dctx[:, at])
        scores = dot_last(
            jnp.concatenate([k, key_mask], axis=1), jnp.concatenate([q2, masks], axis=1)
        )
        return scores, dot_last(v_ref[:, at], d2), q2, k, d2

    now = products(0)
    for pair in range(PAIRS):
        later = products(pair + 1) if pair + 1 < PAIRS else None
        scores, grad_probs, q2, k, d2 = now
        at = slice(PAIR * pair, PAIR * (pair + 1))
        rounded, grad_scores = [], []
        for head in (slice(0, rows), slice(rows, 2 * rows)):
            probs = jnp.exp(scores[:, head] - jnp.max(scores[:, head], axis=0, keepdims=True))
            probs = probs * (1.0 / jnp.sum(probs, axis=0, keepdims=True))
            rounded.append(probs.astype(bf16))
            weighted = probs * grad_probs[:, head]
            inner = jnp.sum(weighted, axis=0, keepdims=True)
            grad_scores.append((weighted - probs * inner).astype(bf16))
        rounded = jnp.concatenate(rounded, axis=1)
        grad_scores = jnp.concatenate(grad_scores, axis=1)
        dv_s[:, at] = dot(rounded, d2).astype(bf16)
        dk_s[:, at] = dot(grad_scores, q2).astype(bf16)
        crossed = dot_first(k, grad_scores)
        dq = jnp.concatenate([crossed[:HEAD_DIM, :rows], crossed[HEAD_DIM:, rows:]], axis=0)
        dq_s[:, at] = (dq.T * HEAD_DIM**-0.5).astype(bf16)
        now = later


def train_kernel(
    counts_ref, lengths_ref, rest_table_ref, x_ref, q_any, k_any, v_any, ctx_ref, grad_any,
    tail_ref, bq_ref, bv_ref, wqkv_any, *refs,
):
    *refs, q_ref, k_ref, v_ref, grad_ref, out_ref, dq_s, dk_s, dv_s, sems = refs
    *w_refs, out_any, token_ref, sums_ref, w, wqkv, lanes, u_s = refs
    if len(w_refs) > 1:
        end = w_refs[-8:]
        w_refs = [*w_refs[:-8], *end[:3], end[6], *end[3:6], end[7]]
    ready = start_rest(rest_table_ref, w_refs, w, sems.at[pl.ds(5, 24)])
    later_in = [
        pltpu.make_async_copy(any_ref, ref, sems.at[i])
        for i, (any_ref, ref) in enumerate(
            ((grad_any, grad_ref), (q_any, q_ref), (k_any, k_ref), (v_any, v_ref))
        )
    ]
    last_in = pltpu.make_async_copy(wqkv_any, wqkv, sems.at[29])
    x = x_ref[...]
    aq = dot_last(x, adapter(tail_ref, 0)).astype(bf16)
    av = dot_last(x, adapter(tail_ref, 1)).astype(bf16)

    ready(0, WIDTH)
    resid = x.astype(f32) + (dot(ctx_ref[...], w[:WIDTH]) + row(tail_ref, BO))
    normed_one, scale_one = normalise(resid)
    h1 = (normed_one * row(tail_ref, G1) + row(tail_ref, C1)).astype(bf16)

    def keep(slab, at, u):
        u_s[slab, :, at : at + CHUNK] = u

    ready(UP_AT, DOWN_AT)
    if len(w_refs) > 1:
        slabs_of_columns(w, lanes)
    ready(DOWN_AT, REST_ROWS)
    for copy in [*later_in, last_in]:
        copy.start()
    down = feed_forward(h1, tail_ref, w, keep)
    normed_two, scale_two = normalise(h1.astype(f32) + (down + row(tail_ref, B2)))
    out_ref[...] = (normed_two * row(tail_ref, G2) + row(tail_ref, C2)).astype(bf16)
    keep_out = pltpu.make_async_copy(out_ref, out_any, sems.at[4])
    keep_out.start()

    for copy in later_in:
        copy.wait()
    grad_two = normalise_back(grad_ref[...].astype(f32) * row(tail_ref, G2), normed_two, scale_two)
    df = grad_two.astype(bf16)
    chunks = [(slab, at) for slab in range(SLABS) for at in range(0, WIDTH, CHUNK)]
    total = None
    grad_gelu = dot_last(df, down_weight(w, *chunks[0]))
    for i, (slab, at) in enumerate(chunks):
        later = dot_last(df, down_weight(w, *chunks[i + 1])) if i + 1 < len(chunks) else None
        du = (grad_gelu * gelu_slope(u_s[slab, :, at : at + CHUNK])).astype(bf16)
        part = dot_last(du, up_weight(w, slab, at))
        total = part if total is None else total + part
        grad_gelu = later
    dh1 = (grad_two + total).astype(bf16)
    grad_one = normalise_back(dh1.astype(f32) * row(tail_ref, G1), normed_one, scale_one)
    token_ref[...] = grad_one
    dctx = dot_last(grad_one.astype(bf16), w[:WIDTH]).astype(bf16)
    attention_back(q_ref, k_ref, v_ref, dctx, item_masks(counts_ref, lengths_ref), dq_s, dk_s, dv_s)

    last_in.wait()
    dq, dk, dv = dq_s[...], dk_s[...], dv_s[...]
    daq = (2.0 * dot_last(dq, bq_ref[...])).astype(bf16)
    dav = (2.0 * dot_last(dv, bv_ref[...])).astype(bf16)
    sums_ref[:RANK] = 2.0 * dot_first(aq, dq)
    sums_ref[RANK:] = 2.0 * dot_first(av, dv)
    token_ref[...] += (
        dot_last(dq, wqkv[:WIDTH])
        + dot_last(dk, wqkv[WIDTH : 2 * WIDTH])
        + dot_last(dv, wqkv[2 * WIDTH :])
        + dot(daq, adapter(tail_ref, 0))
        + dot(dav, adapter(tail_ref, 1))
    )
    keep_out.wait()


def window_kernel(place_ref, before_ref, own_ref, out_ref, padded_ref, flat, moved):
    ahead = before_ref.shape[0]
    flat[:ahead] = before_ref[...].astype(f32)
    flat[ahead : ahead + own_ref.shape[0]] = own_ref[...].astype(f32)
    flat[ahead + own_ref.shape[0] :] = jnp.zeros((LANES, LANES), f32)
    rows = moved.shape[0]
    start, turn = place_ref[0], place_ref[1]
    back = lax.rem(LANES - turn, LANES)
    here = pltpu.roll(flat[pl.ds(start, rows), :], back, 1)
    after = pltpu.roll(flat[pl.ds(start + 1, rows), :], back, 1)
    lane = lax.broadcasted_iota(jnp.int32, (rows, LANES), 1)
    moved[...] = jnp.where(lane < LANES - turn, here, after)
    per_row = WIDTH // LANES
    for tile in range(per_row):
        part = moved[pl.ds(tile, rows // per_row, stride=per_row), :]
        at = slice(LANES * tile, LANES * (tile + 1))
        out_ref[:, at] = part.astype(bf16)
        padded_ref[: rows // per_row, at] = part.astype(bf16)
    padded_ref[rows // per_row :] = jnp.zeros((PAD_ROWS, WIDTH), bf16)


def whole(shape):
    return pl.BlockSpec(shape, lambda *_: (0,) * len(shape))


def cost(microseconds):
    return pl.CostEstimate(flops=int(microseconds * 1e9), bytes_accessed=0, transcendentals=0)


def stays(value):
    return pltpu.with_memory_space_constraint(value, pltpu.VMEM)


def after(value, *others):
    return lax.optimization_barrier((value, *others))[0]


ANY = pl.BlockSpec(memory_space=pl.ANY)
IN_VMEM = pl.BlockSpec(memory_space=pltpu.VMEM)
SCALARS = pl.BlockSpec(memory_space=pltpu.SMEM)


def params(mebibytes):
    return pltpu.CompilerParams(vmem_limit_bytes=mebibytes * 2**20)


def train_attention(counts, lengths, table, x, bq, bv, w):
    shape = (x.shape[0], WIDTH)
    return pl.pallas_call(
        train_attention_kernel,
        in_specs=[SCALARS] * 3
        + [whole(x.shape), whole(bq.shape), whole(bv.shape)]
        + [ANY] * len(w),
        out_specs=[ANY] * 3 + [whole(shape), whole((TAIL_ROWS, WIDTH)), IN_VMEM, IN_VMEM],
        out_shape=[pltpu.HBM(shape, bf16)] * 4
        + [jax.ShapeDtypeStruct((TAIL_ROWS, WIDTH), bf16)]
        + [pltpu.VMEM((n, WIDTH), bf16) for n in (QKV_ROWS, 2 * WIDTH)],
        grid=(1,),
        scratch_shapes=[pltpu.VMEM(shape, bf16)] * 3 + [pltpu.SemaphoreType.DMA((5,))],
        compiler_params=params(TRAIN_ATTENTION_MIB),
        cost_estimate=cost(11),
        name="train_attention",
    )(counts, lengths, table, x, bq, bv, *w)


def eval_attention(lengths, x, tail, w, merged, first, count):
    return pl.pallas_call(
        functools.partial(eval_attention_kernel, first=first),
        in_specs=[
            SCALARS,
            pl.BlockSpec((BUCKET, WIDTH), lambda i: (i + first, 0)),
            whole(tail.shape),
            IN_VMEM,
            IN_VMEM,
        ],
        out_specs=pl.BlockSpec((BUCKET, WIDTH), lambda i: (i, 0)),
        out_shape=(jax.ShapeDtypeStruct if first else pltpu.HBM)((count * BUCKET, WIDTH), bf16),
        grid=(count,),
        scratch_shapes=[pltpu.VMEM((BUCKET, WIDTH), bf16)] * 3,
        compiler_params=params(EVAL_ATTENTION_MIB),
        cost_estimate=cost(1 + 7 * count),
        name="eval_attention",
    )(lengths, x, tail, stays(w), stays(merged))


def eval_tail(x, ctx, tail, w, first, done=None):
    rows = ctx.shape[0]
    given = [] if done is None else [done]
    return pl.pallas_call(
        eval_tail_kernel,
        in_specs=[
            pl.BlockSpec((BUCKET, WIDTH), lambda i: (i + first, 0)),
            pl.BlockSpec((BUCKET, WIDTH), lambda i: (i, 0)),
            whole(tail.shape),
            IN_VMEM,
        ]
        + [ANY] * len(given),
        out_specs=pl.BlockSpec((BUCKET, WIDTH), lambda i: (i + first, 0)),
        out_shape=jax.ShapeDtypeStruct(x.shape, bf16),
        grid=(rows // BUCKET,),
        input_output_aliases={4: 0} if given else {},
        compiler_params=params(EVAL_TAIL_MIB),
        cost_estimate=cost(3 + 8 * (rows // BUCKET)),
        name="eval_tail",
    )(x, ctx, tail, stays(w), *given)


def train_rest(counts, lengths, rest_table, x, q, k, v, ctx, grad, tail, bq, bv, w, rest):
    rows = x.shape[0]
    shape = (rows, WIDTH)
    return pl.pallas_call(
        train_kernel,
        in_specs=[SCALARS] * 3
        + [whole(shape), ANY, ANY, ANY, whole(shape), ANY]
        + [whole(v.shape) for v in (tail, bq, bv)]
        + [ANY]
        + ([ANY] * (len(rest) - 2) + [IN_VMEM] * 2 if len(rest) > 1 else [ANY]),
        out_specs=[ANY, whole(shape), whole((2 * RANK, WIDTH)), IN_VMEM],
        out_shape=[
            jax.ShapeDtypeStruct(shape, bf16),
            jax.ShapeDtypeStruct(shape, f32),
            jax.ShapeDtypeStruct((2 * RANK, WIDTH), f32),
            pltpu.VMEM((REST_ROWS, WIDTH), bf16),
        ],
        grid=(1,),
        scratch_shapes=[
            pltpu.VMEM((QKV_ROWS, WIDTH), bf16),
            pltpu.VMEM((SLABS * WIDTH, LANES), f32),
            pltpu.VMEM((SLABS, rows, WIDTH), f32),
            *[pltpu.VMEM(shape, bf16)] * 8,
            pltpu.SemaphoreType.DMA((30,)),
        ],
        compiler_params=params(TRAIN_REST_MIB),
        cost_estimate=cost(36),
        name="train_rest",
    )(counts, lengths, rest_table, x, q, k, v, ctx, grad, tail, bq, bv, w, *rest)


def window(start, turn, before, own, rows):
    ahead = before.shape[0]
    place = jnp.stack([start, turn]).astype(jnp.int32)
    return pl.pallas_call(
        window_kernel,
        in_specs=[SCALARS, whole(before.shape), whole(own.shape)],
        out_specs=[whole((rows, WIDTH)), whole((rows + PAD_ROWS, WIDTH))],
        out_shape=[
            jax.ShapeDtypeStruct((rows, WIDTH), bf16),
            jax.ShapeDtypeStruct((rows + PAD_ROWS, WIDTH), bf16),
        ],
        grid=(1,),
        scratch_shapes=[
            pltpu.VMEM((ahead + own.shape[0] + LANES, LANES), f32),
            pltpu.VMEM((rows * (WIDTH // LANES), LANES), f32),
        ],
        compiler_params=params(WINDOW_MIB),
        cost_estimate=cost(2),
        name="window",
    )(place, before, own)


AXES = ("fsdp", "rep")


def tail_rows(flat):
    at = VECTOR_ROWS * WIDTH
    vectors = jnp.pad(flat[:at].reshape(VECTOR_ROWS, WIDTH), ((0, A_AT - VECTOR_ROWS), (0, 0)))
    a = flat[at:].reshape(2, WIDTH, RANK).transpose(0, 2, 1).reshape(2 * RANK, WIDTH)
    return jnp.concatenate([vectors, a])


def collect_generic(frozen, devices):
    me = lax.axis_index(AXES)
    share = WEIGHT_ROWS // devices
    extra = frozen.shape[0] - share * WIDTH
    spill = extra * devices
    before = lax.ppermute(frozen[-spill:], AXES, [(d, (d + 1) % devices) for d in range(devices)])
    flat = lax.dynamic_slice(
        jnp.concatenate([before, frozen]), (spill - extra * me,), (share * WIDTH,)
    )
    gathered = lax.all_gather(flat.reshape(share, WIDTH), AXES, axis=0, tiled=True)
    tail = lax.psum(jnp.where(me == devices - 1, frozen[-spill:].astype(f32), 0.0), AXES)
    w1 = gathered[QKV_ROWS + WIDTH : QKV_ROWS + WIDTH * (1 + SLABS)]
    w1 = w1.reshape(WIDTH, SLABS, WIDTH).transpose(1, 0, 2).reshape(WIDTH * SLABS, WIDTH)
    rest = jnp.concatenate(
        [gathered[QKV_ROWS : QKV_ROWS + WIDTH], w1, gathered[QKV_ROWS + WIDTH * (1 + SLABS) :]]
    )
    none = jnp.zeros((8,), jnp.int32)
    return none, [gathered[:QKV_ROWS], tail_rows(tail.astype(bf16))], none, [rest]


def device(z, x, y, core):
    return ((z * 2 + x) * 2 + y) * 2 + core


PLANE = [(x, y, core) for x in range(2) for y in range(2) for core in range(2)]
EVERY = [(z, *p) for z in range(4) for p in PLANE]


def along_z(value, pairs):
    return lax.ppermute(
        value, AXES, [(device(a, *p), device(b, *p)) for a, b in pairs for p in PLANE]
    )


def first_way(value):
    return lax.ppermute(
        value, AXES,
        [(device(z, x, y, c), device(z, x ^ (1 - c), y ^ c, c)) for z, x, y, c in EVERY],
    )


def second_way(value):
    return lax.ppermute(
        value, AXES,
        [(device(z, x, y, c), device(z, x ^ c, y ^ (1 - c), c)) for z, x, y, c in EVERY],
    )


def sibling(value):
    return lax.ppermute(
        value, AXES, [(device(z, x, y, c), device(z, x, y, 1 - c)) for z, x, y, c in EVERY]
    )


def collect(frozen, query_b, value_b):
    me = lax.axis_index(AXES)
    z, core = me // 8, me % 2
    chip = me // 2
    share = WEIGHT_ROWS // 32
    extra = frozen.shape[0] - share * WIDTH
    spill = extra * 32
    padded = -(-frozen.shape[0] // 1024) * 1024
    own = jnp.pad(frozen, (0, padded - frozen.shape[0])).reshape(padded // LANES, LANES)
    first = spill - extra * me
    start, turn = first // LANES, first % LANES

    plane = chip % 4
    one, two = jnp.where(core == 0, 2, 1), jnp.where(core == 0, 1, 2)
    mine_at = jnp.stack([plane, plane ^ one, plane ^ two, plane ^ 3]) * 2 + core
    other_at = jnp.stack([plane, plane ^ two, plane ^ one, plane ^ 3]) * 2 + 1 - core
    at = jnp.concatenate([mine_at, other_at]).astype(jnp.int32)
    flag = z[None].astype(jnp.int32)
    level = jnp.stack([jnp.maximum(z, 1), jnp.where(z == 2, 3, 2), jnp.where(z < 2, 3, 1)])
    level = level.astype(jnp.int32)

    last_rows = frozen[-spill:]
    before = lax.ppermute(last_rows, AXES, [(d, d + 1) for d in range(31)])
    mine, padded = window(start, turn, before.reshape(spill // LANES, LANES), own, share)

    last_rows, query_b, value_b, at, flag, level = lax.optimization_barrier(
        (last_rows, query_b, value_b, at, flag, level, mine)
    )[:-1]
    tail = tail_rows(
        lax.ppermute(last_rows, AXES, [(31, device(0, 0, 0, 0))])
        + lax.ppermute(last_rows, AXES, [(31, device(2, 0, 0, 0))])
    )
    bq, bv = query_b.astype(bf16), value_b.astype(bf16)
    table = jnp.concatenate([at, flag])
    codes = jnp.stack([at + 8 * (level[1] - 1), at + 8 * (level[2] - 1)], axis=1).reshape(-1)
    rest_table = jnp.concatenate([at + 8 * (level[0] - 1), codes, flag])

    up_two = along_z(padded, [(0, 2), (2, 3)])
    near = [mine, first_way(mine), second_way(mine)]
    down_one = along_z(mine, [(1, 0), (2, 1), (3, 2)])

    up = jnp.concatenate([jnp.where(z == 2, up_two[:share], mine), tail])
    up_one = along_z(up, [(0, 1), (1, 2), (2, 3)])
    near[1], down_one = lax.optimization_barrier((near[1], down_one, up))[:2]
    near.append(second_way(near[1]))
    down_two = along_z(down_one, [(1, 0), (2, 1)])
    up_one, down_two, near[3] = lax.optimization_barrier((up_one, down_two, near[3]))

    far = [
        jnp.where(z == 0, jnp.concatenate([down_one, tail]), jnp.where(z == 2, up, up_one))
    ]
    far += [first_way(far[0]), second_way(far[0])]
    ends = along_z(jnp.where(z == 1, down_two, up_one[:share]), [(1, 0), (2, 3)])
    near_other = [sibling(v) for v in near]
    bq, bv, table, rest_table, *ready = lax.optimization_barrier(
        (bq, bv, table, rest_table, *far, *near_other)
    )
    far, near_other = ready[:3], ready[3:]

    far.append(second_way(far[1]))
    far_other = [sibling(v) for v in far[:3]]
    last = jnp.stack(
        [
            jnp.where(z == 0, down_two, jnp.where(z == 3, up_two[:share], down_one)),
            jnp.where(z == 1, down_two, jnp.where(z == 2, up_one[:share], ends)),
        ]
    )
    far[3], last, *far_other = lax.optimization_barrier((far[3], last, *far_other))
    far_other.append(sibling(far[3]))
    projections = [*near, *near_other, *far, *far_other]
    last = [last, first_way(last), second_way(last)]
    return table, projections, rest_table, last, bq, bv


def other_planes(value, flip):
    return lax.ppermute(
        value, AXES, [(device(z, *p), device(z ^ flip, *p)) for z, *p in EVERY]
    )


def other_chips(value, flip_x, flip_y):
    return lax.ppermute(
        value, AXES,
        [(device(z, x, y, c), device(z, x ^ flip_x, y ^ flip_y, c)) for z, x, y, c in EVERY],
    )


def plane_total(value):
    value = value + sibling(value)
    along = value + other_chips(value, 1, 0)
    across = other_chips(value, 0, 1) + other_chips(value, 1, 1)
    return along + across


def planes_total(value):
    return (value + other_planes(value, 1)) + (other_planes(value, 2) + other_planes(value, 3))


def local(
    tokens,
    bucket_item_counts,
    slot_item_lengths,
    frozen,
    query_lowrank_matrix,
    value_lowrank_matrix,
    output_gradient,
    evaluation_tokens,
    evaluation_lengths,
    *,
    mesh,
):
    devices = mesh.shape["fsdp"] * mesh.shape["rep"]
    special = tuple(mesh.shape[axis] for axis in AXES) == (8, 4)
    if special:
        table, w, rest_table, last, bq, bv = collect(
            frozen, query_lowrank_matrix, value_lowrank_matrix
        )
    else:
        table, w, rest_table, rest = collect_generic(frozen, devices)
        bq, bv = query_lowrank_matrix.astype(bf16), value_lowrank_matrix.astype(bf16)
    counts, lengths = bucket_item_counts, slot_item_lengths
    blocks = evaluation_tokens.shape[0] // BUCKET

    q, k, v, ctx, tail, w_qkv, merged = train_attention(
        counts, lengths, table, tokens, bq, bv, w
    )
    x = after(evaluation_tokens, ctx) if special else evaluation_tokens
    most = blocks - blocks // 2
    first_ctx = eval_attention(evaluation_lengths, x, tail, w_qkv, merged, 0, most)
    if special:
        last = list(lax.optimization_barrier((*last, first_ctx))[:3])
        x = after(x, *last)
        last.append(second_way(last[1]))
        other = [sibling(v) for v in last[:3]]
    last_ctx = eval_attention(
        evaluation_lengths, x, tail, w_qkv, merged, most, blocks - most
    )
    eval_ctx = [first_ctx, last_ctx]
    if special:
        last[3] = after(last[3], last_ctx)
        rest = w + last[:3] + other + [stays(last[3]), stays(sibling(last[3]))]
    grad = after(output_gradient, *eval_ctx)
    out, token_gradient, sums, w_rest = train_rest(
        counts, lengths, rest_table, tokens, q, k, v, ctx, grad, tail, bq, bv, w_qkv, rest
    )
    eval_in = [after(c, sums) for c in eval_ctx]
    eval_out = eval_tail(evaluation_tokens, eval_in[0], tail, w_rest, 0)
    second = eval_in[1]
    if special:
        sums = plane_total(sums)
        second = after(second, sums, eval_out)
    eval_out = eval_tail(evaluation_tokens, second, tail, w_rest, most, eval_out)
    sums = planes_total(sums) if special else lax.psum(sums, AXES)
    gq, gv = sums[:RANK], sums[RANK:]
    return out, token_gradient, gq, gv, eval_out


def solution(mesh):
    split = P(("fsdp", "rep"), None)
    flat = P(("fsdp", "rep"))
    return jax.shard_map(
        functools.partial(local, mesh=mesh),
        mesh=mesh,
        in_specs=(split, split, split, flat, P(), P(), split, split, flat),
        out_specs=(split, split, P(), P(), split),
        check_vma=False,
    )
```
